512 devices in a mesh: amp: 32 (over z_lo, x, core), intg: 16 (over z_hi, y).
Axes of the slice: x: 4, y: 8, z: 8 (z_hi: 2, z_lo: 4; z = z_hi * 4 + z_lo), core: 2. Of those that a mesh axis runs over, the one named last changes fastest.
Arguments:
- amplitudes: float32 [1, 128, 53248], P(None, 'intg', 'amp'), may hold values from -6 to 6
- cycle_block: float32 [8192, 8192], P('intg', 'amp'), may hold values from -0.0625 to 0.0625
- ladder_block: float32 [64, 64, 53248], P('intg', None, 'amp'), may hold values from -0.09375 to 0.09375
- occupied_energy: float32 [128], replicated, may hold values from -2.5 to -0.5
- virtual_energy: float32 [832], replicated, may hold values from 0.5 to 4
- window_tiles: int32 [2], replicated, may hold values from 0 to 12
Outputs:
- updated: float32 [1, 128, 53248], P(None, 'intg', 'amp')
The draws below stay inside these ranges and needn't reach their ends.
Inputs may be any that keep to these rules, and one draw needn't show every extreme that they name: `window_tiles`: virtual tile indices.
All inputs are finite; a program needn't handle non-finite values.
Results may differ from the reference program's by a relative error of at most 0.00007.
Values sent between devices are 32-bit elements; how exact they have to be, the bound alone decides.
No kernel may reach another device: no remote copies, remote signals or barrier semaphores. Data moves between devices by JAX's collectives and lax.ppermute only.
A program may use at most 128 MiB of HBM per device.

```python
import jax
import jax.numpy as jnp
from jax import lax

NI = 1
O = 128
V = 832
TILE = 64
NVT = 13


def shard_levels(key, shape, split, least, top_value):
    def one(position, blocks):
        draws = jax.random.uniform(jax.random.fold_in(jax.random.fold_in(key, 6), position), (blocks,), jnp.float32, least / len(split), top_value / len(split))
        return jnp.repeat(jnp.exp(draws), shape[position] // blocks).reshape((-1,) + (1,) * (len(shape) - position - 1))

    factor_of = one(*split[0])
    for cut in split[1:]:
        factor_of = factor_of * one(*cut)
    return factor_of


def noise(rng, dims, deviation, limit, split=(), dtype=jnp.bfloat16):
    drawn = deviation * jax.random.normal(rng, dims, jnp.float32)
    if split:
        drawn = drawn * shard_levels(rng, dims, split, -0.22, 0.18)
    return jnp.clip(drawn, -limit, limit).astype(dtype)


def setup_inputs(seed: int = 0) -> dict:
    keys = jax.random.split(jax.random.key(seed), 7)
    return {
        "amplitudes": noise(keys[0], (NI, O, V * TILE), 1.0, 6.0, ((1, 16), (2, 32)), jnp.float32),
        "cycle_block": noise(keys[1], (O * TILE, O * TILE), (O * TILE) ** -0.5, 0.0625, ((0, 16), (1, 32)), jnp.float32),
        "ladder_block": noise(keys[2], (TILE, TILE, V * TILE), (TILE * TILE) ** -0.5, 0.09375, ((0, 16), (2, 32)), jnp.float32),
        "occupied_energy": jnp.clip(jax.random.uniform(keys[3], (O,), jnp.float32, -2.5, -0.5), -2.5, -0.5),
        "virtual_energy": jnp.clip(jax.random.uniform(keys[4], (V,), jnp.float32, 0.5, 4.0), 0.5, 4.0),
        "window_tiles": jax.random.randint(keys[5], (2,), 0, NVT).astype(jnp.int32),
    }


def reference(amplitudes, cycle_block, ladder_block, occupied_energy, virtual_energy, window_tiles):
    highest = lax.Precision.HIGHEST
    blocked = amplitudes.reshape(NI, O, V, TILE)
    cycle_tiles = cycle_block.reshape(O, TILE, O, TILE)
    cycle_term = jnp.einsum("ikac,kcjb->ijab", blocked, cycle_tiles, precision=highest)
    ladder_start = (window_tiles[1] * TILE).astype(jnp.int32)
    ladder_slab = lax.dynamic_slice_in_dim(blocked, ladder_start, TILE, 2)
    ladder_tiles = ladder_block.reshape(TILE, TILE, V, TILE)
    ladder_term = jnp.einsum("ijdc,cdab->ijab", ladder_slab, ladder_tiles, precision=highest)
    residual = cycle_term + ladder_term
    spectator_start = (window_tiles[0] * TILE).astype(jnp.int32)
    spectator = lax.dynamic_slice_in_dim(virtual_energy, spectator_start, TILE)
    slab_energy = occupied_energy[:NI]
    denominator = (virtual_energy[None, None, :, None] + spectator[None, None, None, :]
                   - slab_energy[:, None, None, None] - occupied_energy[None, :, None, None])
    result = residual / denominator
    return result.reshape(NI, O, V * TILE)
```

```python
import functools

import jax
import jax.numpy as jnp
from jax import lax
from jax.experimental import pallas as pl
from jax.experimental.pallas import tpu as pltpu
from jax.sharding import Mesh
from jax.sharding import PartitionSpec as P

ZL, X, CORE, ZH, Y = 4, 4, 2, 2, 8
CHIPS = ZL * X
ROWS = 8
TILE = 64
PAIRS = 13
LANES = 2 * TILE
BLOCK = PAIRS * ROWS
EVERY = ("zl", "x", "core", "zh", "y")
VMEM = pl.BlockSpec(memory_space=pltpu.VMEM)
SMEM = pl.BlockSpec(memory_space=pltpu.SMEM)
PARAMS = pltpu.CompilerParams(vmem_limit_bytes=32 * 1024 * 1024)


def split(value):
    high = value.astype(jnp.bfloat16)
    return high, (value - high.astype(jnp.float32)).astype(jnp.bfloat16)


def product(left, right):
    dot = functools.partial(jnp.dot, preferred_element_type=jnp.float32)
    return dot(left[0], right[1]) + dot(left[1], right[0]) + dot(left[0], right[0])


def low_half(shape):
    return lax.broadcasted_iota(jnp.int32, shape, 1) < TILE


def pair_up(first, second):
    low = low_half(first.shape)
    return (
        jnp.where(low, first, pltpu.roll(second, TILE, 1)),
        jnp.where(low, pltpu.roll(first, TILE, 1), second),
    )


def pack_kernel(amplitudes, out):
    for pair in range(PAIRS):
        tile = amplitudes[0, :, pair * LANES : (pair + 1) * LANES]
        for chip in range(CHIPS):
            out[chip, pair * ROWS : (pair + 1) * ROWS, :] = tile


def window_kernel(tiles, gathered, out, window, columns, turned):
    core = lax.axis_index("core")
    for pair in range(TILE // 2):
        place = tiles[1] * (TILE // 2) + pair
        owner = place // PAIRS
        row = ((owner // 2) * PAIRS + (place - owner * PAIRS)) * ROWS
        tile = gathered[pl.ds(pl.multiple_of(row, ROWS), ROWS), :]
        window[pair * ROWS : (pair + 1) * ROWS, :] = jnp.where(owner % 2 == core, tile, 0.0)
    for half in range(ROWS // 2):
        for inner in range(2):
            both = window[pl.ds(half * 2 + inner, TILE // 2, stride=ROWS), :]
            columns[pl.ds(inner * TILE, TILE // 2, stride=2), :] = both
            columns[pl.ds(inner * TILE + 1, TILE // 2, stride=2), :] = pltpu.roll(both, TILE, 1)
        turned[...] = jnp.transpose(columns[...])
        for part in range(2):
            even = turned[pl.ds(2 * part, CHIPS, stride=4), :]
            odd = turned[pl.ds(2 * part + 1, CHIPS, stride=4), :]
            for inner, value in enumerate(pair_up(even, odd)):
                row = part * ROWS + half * 2 + inner
                for target in range(CORE):
                    out[pl.ds(target * CHIPS * 2 * ROWS + row, CHIPS, stride=2 * ROWS), :] = value


def cycle_kernel(gathered, own, other, out):
    core = lax.axis_index("core")
    chunks = ([], [])
    for k in range(0, ROWS, 2):
        first = gathered[pl.ds(k, CHIPS * PAIRS, stride=ROWS), :]
        second = gathered[pl.ds(k + 1, CHIPS * PAIRS, stride=ROWS), :]
        for chunk, value in zip(chunks, pair_up(first, second)):
            chunk.append(value)
    left = split(jnp.concatenate([jnp.concatenate(chunk, 1) for chunk in chunks], 0))
    for side in range(2):
        right = split(jnp.where(core == side, own[...], other[...]))
        result = product(left, right)
        for quarter in range(2):
            both = result[:, quarter * LANES : (quarter + 1) * LANES]
            rows = pair_up(both[: CHIPS * PAIRS], both[CHIPS * PAIRS :])
            for inner, value in enumerate(rows):
                j = side * 4 + quarter * 2 + inner
                out[pl.ds(j, CHIPS * PAIRS, stride=ROWS), :] = value


def ladder_kernel(received, integrals, out):
    lefts = []
    for part in range(2):
        rows = pl.ds(part * ROWS, ROWS)
        both = received[:CHIPS, rows, :] + received[CHIPS:, rows, :]
        lefts.append(both.reshape(CHIPS * ROWS, LANES))
    left = split(jnp.concatenate(lefts, 1))
    width = PAIRS * LANES
    for start in range(0, width, 2 * LANES):
        stop = min(start + 2 * LANES, width)
        result = product(left, split(integrals[:, start:stop]))
        for column in range(start, stop, LANES):
            value = result[:, column - start : column - start + LANES]
            rows = pl.ds(column // LANES * ROWS, ROWS)
            out[:, rows, :] = value.reshape(CHIPS, ROWS, LANES)


def last_kernel(tiles, occupied, virtual, ladder, near, far, out):
    column = lax.axis_index("zl") * (X * CORE) + lax.axis_index("x") * CORE + lax.axis_index("core")
    row = lax.axis_index("zh") * Y + lax.axis_index("y")
    shape = (ROWS, LANES)
    lane = lax.broadcasted_iota(jnp.int32, shape, 1)
    line = lax.broadcasted_iota(jnp.int32, shape, 0)
    spectator = jnp.zeros(shape, jnp.float32)
    for b in range(TILE):
        spectator = jnp.where(lane % TILE == b, virtual[tiles[0] * TILE + b], spectator)
    rows = jnp.zeros(shape, jnp.float32)
    for j in range(ROWS):
        rows = jnp.where(line == j, occupied[row * ROWS + j], rows)
    for pair in range(PAIRS):
        piece = pl.ds(pair * ROWS, ROWS)
        total = near[piece, :] + far[piece, :]
        for chip in range(CHIPS):
            total = total + ladder[chip, piece, :]
        a = column * (2 * PAIRS) + 2 * pair
        energy = jnp.where(lane < TILE, virtual[a], virtual[a + 1]) + spectator
        out[0, :, pair * LANES : (pair + 1) * LANES] = total / (energy - occupied[0] - rows)


def call(kernel, shape, specs, scratch=()):
    return pl.pallas_call(
        kernel,
        out_shape=jax.ShapeDtypeStruct(shape, jnp.float32),
        in_specs=specs,
        out_specs=VMEM,
        scratch_shapes=[pltpu.VMEM(s, jnp.float32) for s in scratch],
        compiler_params=PARAMS,
    )


def places(rule):
    pairs = []
    for chip in range(CHIPS):
        for core in range(CORE):
            for place in range(ZH * Y):
                to = rule(chip, core, place)
                pairs.append(
                    (
                        (chip * CORE + core) * ZH * Y + place,
                        (to[0] * CORE + to[1]) * ZH * Y + to[2],
                    )
                )
    return pairs


def near_rule(chip, core, place):
    zh, y = divmod(place, Y)
    return 2 * y + zh, core, chip


def far_rule(chip, core, place):
    zh, y = divmod(place, Y)
    return 2 * y + 1 - zh, core, chip


def per_device(amplitudes, cycle_block, ladder_block, occupied, virtual, tiles):
    other = lax.ppermute(cycle_block, "core", [(0, 1), (1, 0)])
    copies = call(pack_kernel, (CHIPS, BLOCK, LANES), [VMEM])(amplitudes)
    gathered = lax.all_to_all(copies, ("zl", "x"), 0, 0, tiled=True)
    gathered = gathered.reshape(CHIPS * BLOCK, LANES)
    window = call(
        window_kernel,
        (CORE * CHIPS * 2 * ROWS, LANES),
        [SMEM, VMEM],
        [(TILE // 2 * ROWS, LANES), (LANES, LANES), (LANES, LANES)],
    )(tiles, gathered)
    window = window.reshape(CORE * CHIPS, 2 * ROWS, LANES)
    window = lax.all_to_all(window, ("core", "zh", "y"), 0, 0, tiled=True)
    cycle = call(cycle_kernel, (CHIPS * BLOCK, LANES), [VMEM] * 3)(gathered, cycle_block, other)
    cycle = cycle.reshape(Y, ZH * BLOCK, LANES)
    cycle = lax.psum_scatter(cycle, "y", scatter_dimension=0, tiled=False)
    first, second = cycle[:BLOCK], cycle[BLOCK:]
    low = lax.axis_index("zh") == 0
    near = lax.ppermute(jnp.where(low, first, second), EVERY, places(near_rule))
    far = lax.ppermute(jnp.where(low, second, first), EVERY, places(far_rule))
    integrals = ladder_block.reshape(-1, ladder_block.shape[2])
    ladder = call(ladder_kernel, (CHIPS, BLOCK, LANES), [VMEM] * 2)(window, integrals)
    ladder = lax.all_to_all(ladder, ("zh", "y"), 0, 0, tiled=True)
    return call(last_kernel, amplitudes.shape, [SMEM] * 3 + [VMEM] * 3)(
        tiles, occupied, virtual, ladder, near, far
    )


def solution(mesh):
    parts = Mesh(mesh.devices.reshape(ZL, X, CORE, ZH, Y), EVERY)
    amp, intg = ("zl", "x", "core"), ("zh", "y")
    return jax.shard_map(
        per_device,
        mesh=parts,
        in_specs=(P(None, intg, amp), P(intg, amp), P(intg, None, amp), P(), P(), P()),
        out_specs=P(None, intg, amp),
        check_vma=False,
    )
```

```python
import functools

import jax
import jax.numpy as jnp
from jax import lax
from jax.experimental import pallas as pl
from jax.experimental.pallas import tpu as pltpu
from jax.sharding import Mesh
from jax.sharding import PartitionSpec as P

ZL, X, CORE, ZH, Y = 4, 4, 2, 2, 8
CHIPS = ZL * X
ROWS = 8
TILE = 64
PAIRS = 13
LANES = 2 * TILE
BLOCK = PAIRS * ROWS
EVERY = ("zl", "x", "core", "zh", "y")
VMEM = pl.BlockSpec(memory_space=pltpu.VMEM)
SMEM = pl.BlockSpec(memory_space=pltpu.SMEM)
PARAMS = pltpu.CompilerParams(vmem_limit_bytes=32 * 1024 * 1024)


def split(value):
    high = value.astype(jnp.bfloat16)
    return high, (value - high.astype(jnp.float32)).astype(jnp.bfloat16)


def product(left, right):
    dot = functools.partial(jnp.dot, preferred_element_type=jnp.float32)
    return dot(left[0], right[1]) + dot(left[1], right[0]) + dot(left[0], right[0])


def low_half(shape):
    return lax.broadcasted_iota(jnp.int32, shape, 1) < TILE


def pair_up(first, second):
    low = low_half(first.shape)
    return (
        jnp.where(low, first, pltpu.roll(second, TILE, 1)),
        jnp.where(low, pltpu.roll(first, TILE, 1), second),
    )


def pack_kernel(amplitudes, out):
    for pair in range(PAIRS):
        tile = amplitudes[0, :, pair * LANES : (pair + 1) * LANES]
        for chip in range(ZL):
            out[chip, pair * ROWS : (pair + 1) * ROWS, :] = tile


def window_kernel(tiles, gathered, out, window, columns, turned):
    core = lax.axis_index("core")
    for pair in range(TILE // 2):
        place = tiles[1] * (TILE // 2) + pair
        owner = place // PAIRS
        chip = owner // CORE
        block = (chip % X) * ZL + chip // X
        row = (block * PAIRS + (place - owner * PAIRS)) * ROWS
        tile = gathered[pl.ds(pl.multiple_of(row, ROWS), ROWS), :]
        window[pair * ROWS : (pair + 1) * ROWS, :] = jnp.where(owner % 2 == core, tile, 0.0)
    for half in range(ROWS // 2):
        for inner in range(2):
            both = window[pl.ds(half * 2 + inner, TILE // 2, stride=ROWS), :]
            columns[pl.ds(inner * TILE, TILE // 2, stride=2), :] = both
            columns[pl.ds(inner * TILE + 1, TILE // 2, stride=2), :] = pltpu.roll(both, TILE, 1)
        turned[...] = jnp.transpose(columns[...])
        for part in range(2):
            even = turned[pl.ds(2 * part, CHIPS, stride=4), :]
            odd = turned[pl.ds(2 * part + 1, CHIPS, stride=4), :]
            for inner, value in enumerate(pair_up(even, odd)):
                row = part * ROWS + half * 2 + inner
                for target in range(CORE):
                    out[pl.ds(target * CHIPS * 2 * ROWS + row, CHIPS, stride=2 * ROWS), :] = value


def cycle_kernel(gathered, own, other, out):
    core = lax.axis_index("core")
    chunks = ([], [])
    for k in range(0, ROWS, 2):
        first = gathered[pl.ds(k, CHIPS * PAIRS, stride=ROWS), :]
        second = gathered[pl.ds(k + 1, CHIPS * PAIRS, stride=ROWS), :]
        for chunk, value in zip(chunks, pair_up(first, second)):
            chunk.append(value)
    left = split(jnp.concatenate([jnp.concatenate(chunk, 1) for chunk in chunks], 0))
    for side in range(2):
        right = split(jnp.where(core == side, own[...], other[...]))
        result = product(left, right)
        for quarter in range(2):
            both = result[:, quarter * LANES : (quarter + 1) * LANES]
            rows = pair_up(both[: CHIPS * PAIRS], both[CHIPS * PAIRS :])
            for inner, value in enumerate(rows):
                j = side * 4 + quarter * 2 + inner
                out[pl.ds(j, CHIPS * PAIRS, stride=ROWS), :] = value


def ladder_kernel(received, integrals, out):
    lefts = []
    for part in range(2):
        rows = pl.ds(part * ROWS, ROWS)
        both = received[:CHIPS, rows, :] + received[CHIPS:, rows, :]
        lefts.append(both.reshape(CHIPS * ROWS, LANES))
    left = split(jnp.concatenate(lefts, 1))
    width = PAIRS * LANES
    for start in range(0, width, 2 * LANES):
        stop = min(start + 2 * LANES, width)
        result = product(left, split(integrals[:, start:stop]))
        for column in range(start, stop, LANES):
            value = result[:, column - start : column - start + LANES]
            rows = pl.ds(column // LANES * ROWS, ROWS)
            out[:, rows, :] = value.reshape(CHIPS, ROWS, LANES)


def last_kernel(tiles, occupied, virtual, ladder, near, far, out):
    column = lax.axis_index("zl") * (X * CORE) + lax.axis_index("x") * CORE + lax.axis_index("core")
    row = lax.axis_index("zh") * Y + lax.axis_index("y")
    shape = (ROWS, LANES)
    lane = lax.broadcasted_iota(jnp.int32, shape, 1)
    line = lax.broadcasted_iota(jnp.int32, shape, 0)
    spectator = jnp.zeros(shape, jnp.float32)
    for b in range(TILE):
        spectator = jnp.where(lane % TILE == b, virtual[tiles[0] * TILE + b], spectator)
    rows = jnp.zeros(shape, jnp.float32)
    for j in range(ROWS):
        rows = jnp.where(line == j, occupied[row * ROWS + j], rows)
    for pair in range(PAIRS):
        piece = pl.ds(pair * ROWS, ROWS)
        total = near[piece, :] + far[piece, :]
        for chip in range(CHIPS):
            total = total + ladder[chip, piece, :]
        a = column * (2 * PAIRS) + 2 * pair
        energy = jnp.where(lane < TILE, virtual[a], virtual[a + 1]) + spectator
        out[0, :, pair * LANES : (pair + 1) * LANES] = total / (energy - occupied[0] - rows)


def call(kernel, shape, specs, scratch=()):
    return pl.pallas_call(
        kernel,
        out_shape=jax.ShapeDtypeStruct(shape, jnp.float32),
        in_specs=specs,
        out_specs=VMEM,
        scratch_shapes=[pltpu.VMEM(s, jnp.float32) for s in scratch],
        compiler_params=PARAMS,
    )


def places(rule):
    pairs = []
    for chip in range(CHIPS):
        for core in range(CORE):
            for place in range(ZH * Y):
                to = rule(chip, core, place)
                pairs.append(
                    (
                        (chip * CORE + core) * ZH * Y + place,
                        (to[0] * CORE + to[1]) * ZH * Y + to[2],
                    )
                )
    return pairs


def chip_of(block):
    return block % ZL * X + block // ZL


def near_rule(chip, core, place):
    zh, y = divmod(place, Y)
    return chip_of(2 * y + zh), core, chip


def far_rule(chip, core, place):
    zh, y = divmod(place, Y)
    return chip_of(2 * y + 1 - zh), core, chip


def per_device(amplitudes, cycle_block, ladder_block, occupied, virtual, tiles):
    other = lax.ppermute(cycle_block, "core", [(0, 1), (1, 0)])
    copies = call(pack_kernel, (ZL, BLOCK, LANES), [VMEM])(amplitudes)
    column = lax.all_to_all(copies, "zl", 0, 0, tiled=True)
    copies = jnp.broadcast_to(column.reshape(1, ZL * BLOCK, LANES), (X, ZL * BLOCK, LANES))
    gathered = lax.all_to_all(copies, "x", 0, 0, tiled=True)
    gathered = gathered.reshape(CHIPS * BLOCK, LANES)
    cycle = call(cycle_kernel, (CHIPS * BLOCK, LANES), [VMEM] * 3)(gathered, cycle_block, other)
    cycle, gathered = lax.optimization_barrier((cycle, gathered))
    window = call(
        window_kernel,
        (CORE * CHIPS * 2 * ROWS, LANES),
        [SMEM, VMEM],
        [(TILE // 2 * ROWS, LANES), (LANES, LANES), (LANES, LANES)],
    )(tiles, gathered)
    window = window.reshape(CORE * CHIPS, 2 * ROWS, LANES)
    window = lax.all_to_all(window, ("core", "zh", "y"), 0, 0, tiled=True)
    cycle = cycle.reshape(Y, ZH * BLOCK, LANES)
    cycle = lax.psum_scatter(cycle, "y", scatter_dimension=0, tiled=False)
    first, second = cycle[:BLOCK], cycle[BLOCK:]
    low = lax.axis_index("zh") == 0
    near = lax.ppermute(jnp.where(low, first, second), EVERY, places(near_rule))
    far = lax.ppermute(jnp.where(low, second, first), EVERY, places(far_rule))
    integrals = ladder_block.reshape(-1, ladder_block.shape[2])
    ladder = call(ladder_kernel, (CHIPS, BLOCK, LANES), [VMEM] * 2)(window, integrals)
    ladder = lax.all_to_all(ladder, ("zh", "y"), 0, 0, tiled=True)
    return call(last_kernel, amplitudes.shape, [SMEM] * 3 + [VMEM] * 3)(
        tiles, occupied, virtual, ladder, near, far
    )


def solution(mesh):
    parts = Mesh(mesh.devices.reshape(ZL, X, CORE, ZH, Y), EVERY)
    amp, intg = ("zl", "x", "core"), ("zh", "y")
    return jax.shard_map(
        per_device,
        mesh=parts,
        in_specs=(P(None, intg, amp), P(intg, amp), P(intg, None, amp), P(), P(), P()),
        out_specs=P(None, intg, amp),
        check_vma=False,
    )
```

```python
import functools

import jax
import jax.numpy as jnp
from jax import lax
from jax.experimental import pallas as pl
from jax.experimental.pallas import tpu as pltpu
from jax.sharding import Mesh
from jax.sharding import PartitionSpec as P

ZL, X, CORE, ZH, Y = 4, 4, 2, 2, 8
CHIPS = ZL * X
ROWS = 8
TILE = 64
PAIRS = 13
LANES = 2 * TILE
BLOCK = PAIRS * ROWS
EVERY = ("zl", "x", "core", "zh", "y")
VMEM = pl.BlockSpec(memory_space=pltpu.VMEM)
SMEM = pl.BlockSpec(memory_space=pltpu.SMEM)
PARAMS = pltpu.CompilerParams(vmem_limit_bytes=32 * 1024 * 1024)


def split(value):
    high = value.astype(jnp.bfloat16)
    return high, (value - high.astype(jnp.float32)).astype(jnp.bfloat16)


def product(left, right):
    dot = functools.partial(jnp.dot, preferred_element_type=jnp.float32)
    return dot(left[0], right[1]) + dot(left[1], right[0]) + dot(left[0], right[0])


def low_half(shape):
    return lax.broadcasted_iota(jnp.int32, shape, 1) < TILE


def pair_up(first, second):
    low = low_half(first.shape)
    return (
        jnp.where(low, first, pltpu.roll(second, TILE, 1)),
        jnp.where(low, pltpu.roll(first, TILE, 1), second),
    )


def pack_kernel(amplitudes, out):
    for pair in range(PAIRS):
        tile = amplitudes[0, :, pair * LANES : (pair + 1) * LANES]
        for chip in range(ZL):
            out[chip, pair * ROWS : (pair + 1) * ROWS, :] = tile


def window_kernel(tiles, gathered, out, window, columns, turned):
    core = lax.axis_index("core")
    for pair in range(TILE // 2):
        place = tiles[1] * (TILE // 2) + pair
        owner = place // PAIRS
        chip = owner // CORE
        block = (chip % X) * ZL + chip // X
        row = (block * PAIRS + (place - owner * PAIRS)) * ROWS
        tile = gathered[pl.ds(pl.multiple_of(row, ROWS), ROWS), :]
        window[pair * ROWS : (pair + 1) * ROWS, :] = jnp.where(owner % 2 == core, tile, 0.0)
    for half in range(ROWS // 2):
        for inner in range(2):
            both = window[pl.ds(half * 2 + inner, TILE // 2, stride=ROWS), :]
            columns[pl.ds(inner * TILE, TILE // 2, stride=2), :] = both
            columns[pl.ds(inner * TILE + 1, TILE // 2, stride=2), :] = pltpu.roll(both, TILE, 1)
        turned[...] = jnp.transpose(columns[...])
        for part in range(2):
            even = turned[pl.ds(2 * part, CHIPS, stride=4), :]
            odd = turned[pl.ds(2 * part + 1, CHIPS, stride=4), :]
            for inner, value in enumerate(pair_up(even, odd)):
                row = part * ROWS + half * 2 + inner
                out[pl.ds(row, CHIPS, stride=2 * ROWS), :] = value


def cycle_kernel(gathered, own, other, out):
    core = lax.axis_index("core")
    chunks = ([], [])
    for k in range(0, ROWS, 2):
        first = gathered[pl.ds(k, CHIPS * PAIRS, stride=ROWS), :]
        second = gathered[pl.ds(k + 1, CHIPS * PAIRS, stride=ROWS), :]
        for chunk, value in zip(chunks, pair_up(first, second)):
            chunk.append(value)
    left = split(jnp.concatenate([jnp.concatenate(chunk, 1) for chunk in chunks], 0))
    for side in range(2):
        right = split(jnp.where(core == side, own[...], other[...]))
        result = product(left, right)
        for quarter in range(2):
            both = result[:, quarter * LANES : (quarter + 1) * LANES]
            rows = pair_up(both[: CHIPS * PAIRS], both[CHIPS * PAIRS :])
            for inner, value in enumerate(rows):
                j = side * 4 + quarter * 2 + inner
                out[pl.ds(j, CHIPS * PAIRS, stride=ROWS), :] = value


def join_kernel(cycle, own, other, out):
    for place in range(CHIPS):
        out[place, :BLOCK, :] = cycle[place, :, :]
        out[place, BLOCK:, :] = own[place, :, :] + other[place, :, :]


def sum_kernel(received, out):
    total = received[0, :BLOCK, :]
    for place in range(1, CHIPS):
        total = total + received[place, :BLOCK, :]
    out[...] = total


def ladder_kernel(received, integrals, out):
    lefts = []
    for part in range(2):
        rows = received[:, BLOCK + part * ROWS : BLOCK + (part + 1) * ROWS, :]
        lefts.append(rows.reshape(CHIPS * ROWS, LANES))
    left = split(jnp.concatenate(lefts, 1))
    width = PAIRS * LANES
    for start in range(0, width, 2 * LANES):
        stop = min(start + 2 * LANES, width)
        result = product(left, split(integrals[:, start:stop]))
        for column in range(start, stop, LANES):
            value = result[:, column - start : column - start + LANES]
            rows = pl.ds(column // LANES * ROWS, ROWS)
            out[:, rows, :] = value.reshape(CHIPS, ROWS, LANES)


def last_kernel(tiles, occupied, virtual, ladder, cycle, out):
    column = lax.axis_index("zl") * (X * CORE) + lax.axis_index("x") * CORE + lax.axis_index("core")
    row = lax.axis_index("zh") * Y + lax.axis_index("y")
    shape = (ROWS, LANES)
    lane = lax.broadcasted_iota(jnp.int32, shape, 1)
    line = lax.broadcasted_iota(jnp.int32, shape, 0)
    spectator = jnp.zeros(shape, jnp.float32)
    for b in range(TILE):
        spectator = jnp.where(lane % TILE == b, virtual[tiles[0] * TILE + b], spectator)
    rows = jnp.zeros(shape, jnp.float32)
    for j in range(ROWS):
        rows = jnp.where(line == j, occupied[row * ROWS + j], rows)
    for pair in range(PAIRS):
        piece = pl.ds(pair * ROWS, ROWS)
        total = cycle[piece, :]
        for chip in range(CHIPS):
            total = total + ladder[chip, piece, :]
        a = column * (2 * PAIRS) + 2 * pair
        energy = jnp.where(lane < TILE, virtual[a], virtual[a + 1]) + spectator
        out[0, :, pair * LANES : (pair + 1) * LANES] = total / (energy - occupied[0] - rows)


def call(kernel, shape, specs, scratch=()):
    return pl.pallas_call(
        kernel,
        out_shape=jax.ShapeDtypeStruct(shape, jnp.float32),
        in_specs=specs,
        out_specs=VMEM,
        scratch_shapes=[pltpu.VMEM(s, jnp.float32) for s in scratch],
        compiler_params=PARAMS,
    )


def places(rule):
    pairs = []
    for chip in range(CHIPS):
        for core in range(CORE):
            for place in range(ZH * Y):
                to = rule(chip, core, place)
                pairs.append(
                    (
                        (chip * CORE + core) * ZH * Y + place,
                        (to[0] * CORE + to[1]) * ZH * Y + to[2],
                    )
                )
    return pairs


def chip_of(block):
    return block % ZL * X + block // ZL


def owner_rule(chip, core, place):
    return chip_of(place), core, chip


def per_device(amplitudes, cycle_block, ladder_block, occupied, virtual, tiles):
    other = lax.ppermute(cycle_block, "core", [(0, 1), (1, 0)])
    copies = call(pack_kernel, (ZL, BLOCK, LANES), [VMEM])(amplitudes)
    column = lax.all_to_all(copies, "zl", 0, 0, tiled=True)
    copies = jnp.broadcast_to(column.reshape(1, ZL * BLOCK, LANES), (X, ZL * BLOCK, LANES))
    gathered = lax.all_to_all(copies, "x", 0, 0, tiled=True)
    gathered = gathered.reshape(CHIPS * BLOCK, LANES)
    window = call(
        window_kernel,
        (CHIPS * 2 * ROWS, LANES),
        [SMEM, VMEM],
        [(TILE // 2 * ROWS, LANES), (LANES, LANES), (LANES, LANES)],
    )(tiles, gathered)
    window = window.reshape(CHIPS, 2 * ROWS, LANES)
    other_window = lax.ppermute(window, "core", [(0, 1), (1, 0)])
    cycle = call(cycle_kernel, (CHIPS * BLOCK, LANES), [VMEM] * 3)(gathered, cycle_block, other)
    cycle = cycle.reshape(CHIPS, BLOCK, LANES)
    joined = (CHIPS, BLOCK + 2 * ROWS, LANES)
    joined = call(join_kernel, joined, [VMEM] * 3)(cycle, window, other_window)
    received = lax.all_to_all(joined, ("zh", "y"), 0, 0, tiled=True)
    integrals = ladder_block.reshape(-1, ladder_block.shape[2])
    ladder = call(ladder_kernel, (CHIPS, BLOCK, LANES), [VMEM] * 2)(received, integrals)
    ladder, received = lax.optimization_barrier((ladder, received))
    cycle = call(sum_kernel, (BLOCK, LANES), [VMEM])(received)
    cycle = lax.ppermute(cycle, EVERY, places(owner_rule))
    ladder = lax.all_to_all(ladder, ("zh", "y"), 0, 0, tiled=True)
    return call(last_kernel, amplitudes.shape, [SMEM] * 3 + [VMEM] * 2)(
        tiles, occupied, virtual, ladder, cycle
    )


def solution(mesh):
    parts = Mesh(mesh.devices.reshape(ZL, X, CORE, ZH, Y), EVERY)
    amp, intg = ("zl", "x", "core"), ("zh", "y")
    return jax.shard_map(
        per_device,
        mesh=parts,
        in_specs=(P(None, intg, amp), P(intg, amp), P(intg, None, amp), P(), P(), P()),
        out_specs=P(None, intg, amp),
        check_vma=False,
    )
```

```python
import functools

import jax
import jax.numpy as jnp
from jax import lax
from jax.experimental import pallas as pl
from jax.experimental.pallas import tpu as pltpu
from jax.sharding import Mesh
from jax.sharding import PartitionSpec as P

ZL, X, CORE, ZH, Y = 4, 4, 2, 2, 8
CHIPS = ZL * X
ROWS = 8
TILE = 64
PAIRS = 13
LANES = 2 * TILE
BLOCK = PAIRS * ROWS
EVERY = ("zl", "x", "core", "zh", "y")
VMEM = pl.BlockSpec(memory_space=pltpu.VMEM)
SMEM = pl.BlockSpec(memory_space=pltpu.SMEM)
PARAMS = pltpu.CompilerParams(vmem_limit_bytes=32 * 1024 * 1024)


def split(value):
    high = value.astype(jnp.bfloat16)
    return high, (value - high.astype(jnp.float32)).astype(jnp.bfloat16)


def product(left, right):
    dot = functools.partial(jnp.dot, preferred_element_type=jnp.float32)
    return dot(left[0], right[1]) + dot(left[1], right[0]) + dot(left[0], right[0])


def low_half(shape):
    return lax.broadcasted_iota(jnp.int32, shape, 1) < TILE


def pair_up(first, second):
    low = low_half(first.shape)
    return (
        jnp.where(low, first, pltpu.roll(second, TILE, 1)),
        jnp.where(low, pltpu.roll(first, TILE, 1), second),
    )


def pack_kernel(amplitudes, out):
    for pair in range(PAIRS):
        tile = amplitudes[0, :, pair * LANES : (pair + 1) * LANES]
        for chip in range(ZL):
            out[chip, pair * ROWS : (pair + 1) * ROWS, :] = tile


def window_kernel(tiles, gathered, out, window, columns, turned):
    core = lax.axis_index("core")
    for pair in range(TILE // 2):
        place = tiles[1] * (TILE // 2) + pair
        owner = place // PAIRS
        chip = owner // CORE
        block = (chip % X) * ZL + chip // X
        row = (block * PAIRS + (place - owner * PAIRS)) * ROWS
        tile = gathered[pl.ds(pl.multiple_of(row, ROWS), ROWS), :]
        window[pair * ROWS : (pair + 1) * ROWS, :] = jnp.where(owner % 2 == core, tile, 0.0)
    for half in range(ROWS // 2):
        for inner in range(2):
            both = window[pl.ds(half * 2 + inner, TILE // 2, stride=ROWS), :]
            columns[pl.ds(inner * TILE, TILE // 2, stride=2), :] = both
            columns[pl.ds(inner * TILE + 1, TILE // 2, stride=2), :] = pltpu.roll(both, TILE, 1)
        turned[...] = jnp.transpose(columns[...])
        for part in range(2):
            even = turned[pl.ds(2 * part, CHIPS, stride=4), :]
            odd = turned[pl.ds(2 * part + 1, CHIPS, stride=4), :]
            for inner, value in enumerate(pair_up(even, odd)):
                row = part * ROWS + half * 2 + inner
                for target in range(CORE):
                    start = target * CHIPS * 2 * ROWS + row
                    out[pl.ds(start, CHIPS, stride=2 * ROWS), :] = value


def cycle_kernel(gathered, own, other, out):
    core = lax.axis_index("core")
    chunks = ([], [])
    for k in range(0, ROWS, 2):
        first = gathered[pl.ds(k, CHIPS * PAIRS, stride=ROWS), :]
        second = gathered[pl.ds(k + 1, CHIPS * PAIRS, stride=ROWS), :]
        for chunk, value in zip(chunks, pair_up(first, second)):
            chunk.append(value)
    left = split(jnp.concatenate([jnp.concatenate(chunk, 1) for chunk in chunks], 0))
    for side in range(2):
        right = split(jnp.where(core == side, own[...], other[...]))
        result = product(left, right)
        for quarter in range(2):
            both = result[:, quarter * LANES : (quarter + 1) * LANES]
            rows = pair_up(both[: CHIPS * PAIRS], both[CHIPS * PAIRS :])
            for inner, value in enumerate(rows):
                j = side * 4 + quarter * 2 + inner
                out[pl.ds(j, CHIPS * PAIRS, stride=ROWS), :] = value


def join_kernel(cycle, window, out):
    for y in range(Y):
        out[y, : ZH * BLOCK, :] = cycle[y, :, :]
        rows = slice(y * 2 * ROWS, (y + 1) * 2 * ROWS)
        for zh in range(ZH):
            start = ZH * BLOCK + zh * 2 * ROWS
            out[y, start : start + 2 * ROWS, :] = window[zh, rows, :] + window[ZH + zh, rows, :]


def cycle_sum_kernel(received, near, far):
    first = lax.axis_index("zh") == 0
    for row in range(0, BLOCK, ROWS):
        halves = []
        for start in (row, BLOCK + row):
            total = received[0, start : start + ROWS, :]
            for place in range(1, Y):
                total = total + received[place, start : start + ROWS, :]
            halves.append(total)
        near[row : row + ROWS, :] = jnp.where(first, halves[0], halves[1])
        far[row : row + ROWS, :] = jnp.where(first, halves[1], halves[0])


def ladder_kernel(received, integrals, out):
    lefts = []
    for part in range(2):
        halves = []
        for zh in range(ZH):
            start = ZH * BLOCK + (zh * 2 + part) * ROWS
            halves.append(received[:, start : start + ROWS, :].reshape(Y * ROWS, LANES))
        lefts.append(jnp.concatenate(halves, 0))
    left = split(jnp.concatenate(lefts, 1))
    width = PAIRS * LANES
    for start in range(0, width, 2 * LANES):
        stop = min(start + 2 * LANES, width)
        result = product(left, split(integrals[:, start:stop]))
        for column in range(start, stop, LANES):
            value = result[:, column - start : column - start + LANES]
            rows = pl.ds(column // LANES * ROWS, ROWS)
            out[:, rows, :] = value.reshape(CHIPS, ROWS, LANES)


def last_kernel(tiles, occupied, virtual, ladder, near, far, out):
    column = lax.axis_index("zl") * (X * CORE) + lax.axis_index("x") * CORE + lax.axis_index("core")
    row = lax.axis_index("zh") * Y + lax.axis_index("y")
    shape = (ROWS, LANES)
    lane = lax.broadcasted_iota(jnp.int32, shape, 1)
    line = lax.broadcasted_iota(jnp.int32, shape, 0)
    spectator = jnp.zeros(shape, jnp.float32)
    for b in range(TILE):
        spectator = jnp.where(lane % TILE == b, virtual[tiles[0] * TILE + b], spectator)
    rows = jnp.zeros(shape, jnp.float32)
    for j in range(ROWS):
        rows = jnp.where(line == j, occupied[row * ROWS + j], rows)
    for pair in range(PAIRS):
        piece = pl.ds(pair * ROWS, ROWS)
        total = ladder[0, piece, :]
        for place in range(1, ZH * Y):
            total = total + ladder[place, piece, :]
        total = total + (near[piece, :] + far[piece, :])
        a = column * (2 * PAIRS) + 2 * pair
        energy = jnp.where(lane < TILE, virtual[a], virtual[a + 1]) + spectator
        out[0, :, pair * LANES : (pair + 1) * LANES] = total / (energy - occupied[0] - rows)


def call(kernel, shapes, specs, scratch=()):
    return pl.pallas_call(
        kernel,
        out_shape=[jax.ShapeDtypeStruct(shape, jnp.float32) for shape in shapes],
        in_specs=specs,
        out_specs=[VMEM] * len(shapes),
        scratch_shapes=[pltpu.VMEM(shape, jnp.float32) for shape in scratch],
        compiler_params=PARAMS,
    )


def places(rule):
    pairs = []
    for chip in range(CHIPS):
        for core in range(CORE):
            for place in range(ZH * Y):
                to = rule(chip, core, place)
                pairs.append(
                    (
                        (chip * CORE + core) * ZH * Y + place,
                        (to[0] * CORE + to[1]) * ZH * Y + to[2],
                    )
                )
    return pairs


def chip_of(block):
    return block % ZL * X + block // ZL


def near_rule(chip, core, place):
    zh, y = divmod(place, Y)
    return chip_of(2 * y + zh), core, chip


def far_rule(chip, core, place):
    zh, y = divmod(place, Y)
    return chip_of(2 * y + 1 - zh), core, chip


def per_device(amplitudes, cycle_block, ladder_block, occupied, virtual, tiles):
    swap = [(0, 1), (1, 0)]
    other = lax.ppermute(cycle_block, "core", swap)
    (copies,) = call(pack_kernel, [(ZL, BLOCK, LANES)], [VMEM])(amplitudes)
    column = lax.all_to_all(copies, "zl", 0, 0, tiled=True)
    copies = jnp.broadcast_to(column.reshape(1, ZL * BLOCK, LANES), (X, ZL * BLOCK, LANES))
    gathered = lax.all_to_all(copies, "x", 0, 0, tiled=True)
    gathered = gathered.reshape(CHIPS * BLOCK, LANES)

    (window,) = call(
        window_kernel,
        [(CORE * CHIPS * 2 * ROWS, LANES)],
        [SMEM, VMEM],
        [(TILE // 2 * ROWS, LANES), (LANES, LANES), (LANES, LANES)],
    )(tiles, gathered)
    window = window.reshape(CORE * ZH, Y * 2 * ROWS, LANES)
    window = lax.all_to_all(window, ("core", "zh"), 0, 0, tiled=True)
    (cycle,) = call(cycle_kernel, [(CHIPS * BLOCK, LANES)], [VMEM] * 3)(gathered, cycle_block, other)
    cycle = cycle.reshape(Y, ZH * BLOCK, LANES)
    joined = (Y, ZH * (BLOCK + 2 * ROWS), LANES)
    (joined,) = call(join_kernel, [joined], [VMEM] * 2)(cycle, window)
    received = lax.all_to_all(joined, "y", 0, 0, tiled=True)

    integrals = ladder_block.reshape(-1, ladder_block.shape[2])
    (ladder,) = call(ladder_kernel, [(CHIPS, BLOCK, LANES)], [VMEM] * 2)(received, integrals)
    ladder, received = lax.optimization_barrier((ladder, received))
    near, far = call(cycle_sum_kernel, [(BLOCK, LANES)] * 2, [VMEM])(received)
    near = lax.ppermute(near, EVERY, places(near_rule))
    far = lax.ppermute(far, EVERY, places(far_rule))
    ladder = lax.all_to_all(ladder, ("zh", "y"), 0, 0, tiled=True)
    (result,) = call(last_kernel, [amplitudes.shape], [SMEM] * 3 + [VMEM] * 3)(
        tiles, occupied, virtual, ladder, near, far
    )
    return result


def solution(mesh):
    parts = Mesh(mesh.devices.reshape(ZL, X, CORE, ZH, Y), EVERY)
    amp, intg = ("zl", "x", "core"), ("zh", "y")
    return jax.shard_map(
        per_device,
        mesh=parts,
        in_specs=(P(None, intg, amp), P(intg, amp), P(intg, None, amp), P(), P(), P()),
        out_specs=P(None, intg, amp),
        check_vma=False,
    )
```

```python
import functools

import jax
import jax.numpy as jnp
from jax import lax
from jax.experimental import pallas as pl
from jax.experimental.pallas import tpu as pltpu
from jax.sharding import Mesh
from jax.sharding import PartitionSpec as P

ZL, X, CORE, ZH, Y = 4, 4, 2, 2, 8
CHIPS = ZL * X
ROWS = 8
TILE = 64
PAIRS = 13
LANES = 2 * TILE
BLOCK = PAIRS * ROWS
SIDE = (PAIRS + 1) // 2
SKIP = PAIRS - SIDE
EVERY = ("zl", "x", "core", "zh", "y")
VMEM = pl.BlockSpec(memory_space=pltpu.VMEM)
SMEM = pl.BlockSpec(memory_space=pltpu.SMEM)
PARAMS = pltpu.CompilerParams(vmem_limit_bytes=32 * 1024 * 1024)


def split(value):
    high = value.astype(jnp.bfloat16)
    return high, (value - high.astype(jnp.float32)).astype(jnp.bfloat16)


def product(left, right):
    dot = functools.partial(jnp.dot, preferred_element_type=jnp.float32)
    return dot(left[0], right[1]) + dot(left[1], right[0]) + dot(left[0], right[0])


def low_half(shape):
    return lax.broadcasted_iota(jnp.int32, shape, 1) < TILE


def pair_up(first, second):
    low = low_half(first.shape)
    return (
        jnp.where(low, first, pltpu.roll(second, TILE, 1)),
        jnp.where(low, pltpu.roll(first, TILE, 1), second),
    )


def pack_kernel(amplitudes, out):
    for pair in range(PAIRS):
        tile = amplitudes[0, :, pair * LANES : (pair + 1) * LANES]
        for chip in range(ZL):
            out[chip, pair * ROWS : (pair + 1) * ROWS, :] = tile


def window_kernel(tiles, gathered, out, window, columns, turned):
    core = lax.axis_index("core")
    for pair in range(TILE // 2):
        place = tiles[1] * (TILE // 2) + pair
        owner = place // PAIRS
        chip = owner // CORE
        block = (chip % X) * ZL + chip // X
        row = (block * PAIRS + (place - owner * PAIRS)) * ROWS
        tile = gathered[pl.ds(pl.multiple_of(row, ROWS), ROWS), :]
        window[pair * ROWS : (pair + 1) * ROWS, :] = jnp.where(owner % 2 == core, tile, 0.0)
    for half in range(ROWS // 2):
        for inner in range(2):
            both = window[pl.ds(half * 2 + inner, TILE // 2, stride=ROWS), :]
            columns[pl.ds(inner * TILE, TILE // 2, stride=2), :] = both
            columns[pl.ds(inner * TILE + 1, TILE // 2, stride=2), :] = pltpu.roll(both, TILE, 1)
        turned[...] = jnp.transpose(columns[...])
        for part in range(2):
            even = turned[pl.ds(2 * part, CHIPS, stride=4), :]
            odd = turned[pl.ds(2 * part + 1, CHIPS, stride=4), :]
            for inner, value in enumerate(pair_up(even, odd)):
                row = part * ROWS + half * 2 + inner
                out[pl.ds(row, CHIPS, stride=2 * ROWS), :] = value


def cycle_kernel(gathered, own, other, out):
    core = lax.axis_index("core")
    chunks = ([], [])
    for k in range(0, ROWS, 2):
        first = gathered[pl.ds(k, CHIPS * PAIRS, stride=ROWS), :]
        second = gathered[pl.ds(k + 1, CHIPS * PAIRS, stride=ROWS), :]
        for chunk, value in zip(chunks, pair_up(first, second)):
            chunk.append(value)
    left = split(jnp.concatenate([jnp.concatenate(chunk, 1) for chunk in chunks], 0))
    for side in range(2):
        right = split(jnp.where(core == side, own[...], other[...]))
        result = product(left, right)
        for quarter in range(2):
            both = result[:, quarter * LANES : (quarter + 1) * LANES]
            rows = pair_up(both[: CHIPS * PAIRS], both[CHIPS * PAIRS :])
            for inner, value in enumerate(rows):
                j = side * 4 + quarter * 2 + inner
                out[pl.ds(j, CHIPS * PAIRS, stride=ROWS), :] = value


def join_kernel(cycle, own, other, out):
    for place in range(CHIPS):
        out[place, :BLOCK, :] = cycle[place, :, :]
        for start, source in ((BLOCK, place), (BLOCK + 2 * ROWS, place ^ 1)):
            out[place, start : start + 2 * ROWS, :] = own[source, :, :] + other[source, :, :]


def sum_kernel(received, out):
    total = received[0, :BLOCK, :]
    for place in range(1, CHIPS):
        total = total + received[place, :BLOCK, :]
    out[...] = total


def ladder_kernel(received, own, other, out):
    lefts = []
    for part in range(4):
        rows = received[:, BLOCK + part * ROWS : BLOCK + (part + 1) * ROWS, :]
        lefts.append(rows.reshape(CHIPS * ROWS, LANES))
    left = split(jnp.concatenate(lefts, 1))
    first = lax.axis_index("y") % 2 * (SKIP * LANES)
    width = SIDE * LANES
    for start in range(0, width, 2 * LANES):
        stop = min(start + 2 * LANES, width)
        columns = pl.ds(pl.multiple_of(first + start, LANES), stop - start)
        right = jnp.concatenate([own[:, columns], other[:, start:stop]], 0)
        result = product(left, split(right))
        for column in range(start, stop, LANES):
            value = result[:, column - start : column - start + LANES]
            rows = pl.ds(column // LANES * ROWS, ROWS)
            out[:, rows, :] = value.reshape(CHIPS, ROWS, LANES)


def last_kernel(tiles, occupied, virtual, ladder, cycle, out):
    column = lax.axis_index("zl") * (X * CORE) + lax.axis_index("x") * CORE + lax.axis_index("core")
    row = lax.axis_index("zh") * Y + lax.axis_index("y")
    shape = (ROWS, LANES)
    lane = lax.broadcasted_iota(jnp.int32, shape, 1)
    line = lax.broadcasted_iota(jnp.int32, shape, 0)
    spectator = jnp.zeros(shape, jnp.float32)
    for b in range(TILE):
        spectator = jnp.where(lane % TILE == b, virtual[tiles[0] * TILE + b], spectator)
    rows = jnp.zeros(shape, jnp.float32)
    for j in range(ROWS):
        rows = jnp.where(line == j, occupied[row * ROWS + j], rows)
    for pair in range(PAIRS):
        piece = pl.ds(pair * ROWS, ROWS)
        total = cycle[piece, :]
        side = int(pair >= SIDE)
        rows_of_side = pl.ds((pair - side * SKIP) * ROWS, ROWS)
        for place in range(side, ZH * Y, 2):
            total = total + ladder[place, rows_of_side, :]
        a = column * (2 * PAIRS) + 2 * pair
        energy = jnp.where(lane < TILE, virtual[a], virtual[a + 1]) + spectator
        out[0, :, pair * LANES : (pair + 1) * LANES] = total / (energy - occupied[0] - rows)


def call(kernel, shape, specs, scratch=()):
    return pl.pallas_call(
        kernel,
        out_shape=jax.ShapeDtypeStruct(shape, jnp.float32),
        in_specs=specs,
        out_specs=VMEM,
        scratch_shapes=[pltpu.VMEM(s, jnp.float32) for s in scratch],
        compiler_params=PARAMS,
    )


def places(rule):
    pairs = []
    for chip in range(CHIPS):
        for core in range(CORE):
            for place in range(ZH * Y):
                to = rule(chip, core, place)
                pairs.append(
                    (
                        (chip * CORE + core) * ZH * Y + place,
                        (to[0] * CORE + to[1]) * ZH * Y + to[2],
                    )
                )
    return pairs


def chip_of(block):
    return block % ZL * X + block // ZL


def owner_rule(chip, core, place):
    return chip_of(place), core, chip


def per_device(amplitudes, cycle_block, ladder_block, occupied, virtual, tiles):
    other = lax.ppermute(cycle_block, "core", [(0, 1), (1, 0)])
    integrals = ladder_block.reshape(-1, ladder_block.shape[2])
    start = (1 - lax.axis_index("y") % 2) * (SKIP * LANES)
    side = lax.dynamic_slice_in_dim(integrals, start, SIDE * LANES, 1)
    side = lax.ppermute(side, "y", [(y, y ^ 1) for y in range(Y)])
    copies = call(pack_kernel, (ZL, BLOCK, LANES), [VMEM])(amplitudes)
    column = lax.all_to_all(copies, "zl", 0, 0, tiled=True)
    copies = jnp.broadcast_to(column.reshape(1, ZL * BLOCK, LANES), (X, ZL * BLOCK, LANES))
    gathered = lax.all_to_all(copies, "x", 0, 0, tiled=True)
    gathered = gathered.reshape(CHIPS * BLOCK, LANES)
    window = call(
        window_kernel,
        (CHIPS * 2 * ROWS, LANES),
        [SMEM, VMEM],
        [(TILE // 2 * ROWS, LANES), (LANES, LANES), (LANES, LANES)],
    )(tiles, gathered)
    window = window.reshape(CHIPS, 2 * ROWS, LANES)
    other_window = lax.ppermute(window, "core", [(0, 1), (1, 0)])
    cycle = call(cycle_kernel, (CHIPS * BLOCK, LANES), [VMEM] * 3)(gathered, cycle_block, other)
    cycle = cycle.reshape(CHIPS, BLOCK, LANES)
    joined = (CHIPS, BLOCK + 4 * ROWS, LANES)
    joined = call(join_kernel, joined, [VMEM] * 3)(cycle, window, other_window)
    received = lax.all_to_all(joined, ("zh", "y"), 0, 0, tiled=True)
    cycle = call(sum_kernel, (BLOCK, LANES), [VMEM])(received)
    cycle, received = lax.optimization_barrier((cycle, received))
    cycle = lax.ppermute(cycle, EVERY, places(owner_rule))
    ladder = call(ladder_kernel, (CHIPS, SIDE * ROWS, LANES), [VMEM] * 3)(received, integrals, side)
    ladder = lax.all_to_all(ladder, ("zh", "y"), 0, 0, tiled=True)
    return call(last_kernel, amplitudes.shape, [SMEM] * 3 + [VMEM] * 2)(
        tiles, occupied, virtual, ladder, cycle
    )


def solution(mesh):
    parts = Mesh(mesh.devices.reshape(ZL, X, CORE, ZH, Y), EVERY)
    amp, intg = ("zl", "x", "core"), ("zh", "y")
    return jax.shard_map(
        per_device,
        mesh=parts,
        in_specs=(P(None, intg, amp), P(intg, amp), P(intg, None, amp), P(), P(), P()),
        out_specs=P(None, intg, amp),
        check_vma=False,
    )
```

```python
import functools

import jax
import jax.numpy as jnp
from jax import lax
from jax.experimental import pallas as pl
from jax.experimental.pallas import tpu as pltpu
from jax.sharding import Mesh
from jax.sharding import PartitionSpec as P

ZL, X, CORE, ZH, Y = 4, 4, 2, 2, 8
CHIPS = ZL * X
ROWS = 8
TILE = 64
PAIRS = 13
LANES = 2 * TILE
BLOCK = PAIRS * ROWS
EVERY = ("zl", "x", "core", "zh", "y")
VMEM = pl.BlockSpec(memory_space=pltpu.VMEM)
SMEM = pl.BlockSpec(memory_space=pltpu.SMEM)
PARAMS = pltpu.CompilerParams(vmem_limit_bytes=32 * 1024 * 1024)


def split(value):
    high = value.astype(jnp.bfloat16)
    return high, (value - high.astype(jnp.float32)).astype(jnp.bfloat16)


def product(left, right):
    dot = functools.partial(jnp.dot, preferred_element_type=jnp.float32)
    return dot(left[0], right[1]) + dot(left[1], right[0]) + dot(left[0], right[0])


def low_half(shape):
    return lax.broadcasted_iota(jnp.int32, shape, 1) < TILE


def pair_up(first, second):
    low = low_half(first.shape)
    return (
        jnp.where(low, first, pltpu.roll(second, TILE, 1)),
        jnp.where(low, pltpu.roll(first, TILE, 1), second),
    )


def pack_kernel(amplitudes, out):
    for pair in range(PAIRS):
        tile = amplitudes[0, :, pair * LANES : (pair + 1) * LANES]
        for chip in range(ZL):
            out[chip, pair * ROWS : (pair + 1) * ROWS, :] = tile


def window_kernel(tiles, gathered, out, window, columns, turned):
    core = lax.axis_index("core")
    for pair in range(TILE // 2):
        place = tiles[1] * (TILE // 2) + pair
        owner = place // PAIRS
        chip = owner // CORE
        block = (chip % X) * ZL + chip // X
        row = (block * PAIRS + (place - owner * PAIRS)) * ROWS
        tile = gathered[pl.ds(pl.multiple_of(row, ROWS), ROWS), :]
        window[pair * ROWS : (pair + 1) * ROWS, :] = jnp.where(owner % 2 == core, tile, 0.0)
    for half in range(ROWS // 2):
        for inner in range(2):
            both = window[pl.ds(half * 2 + inner, TILE // 2, stride=ROWS), :]
            columns[pl.ds(inner * TILE, TILE // 2, stride=2), :] = both
            columns[pl.ds(inner * TILE + 1, TILE // 2, stride=2), :] = pltpu.roll(both, TILE, 1)
        turned[...] = jnp.transpose(columns[...])
        for part in range(2):
            even = turned[pl.ds(2 * part, CHIPS, stride=4), :]
            odd = turned[pl.ds(2 * part + 1, CHIPS, stride=4), :]
            for inner, value in enumerate(pair_up(even, odd)):
                row = part * ROWS + half * 2 + inner
                out[pl.ds(row, CHIPS, stride=2 * ROWS), :] = value


def cycle_kernel(gathered, own, other, out):
    core = lax.axis_index("core")
    chunks = ([], [])
    for k in range(0, ROWS, 2):
        first = gathered[pl.ds(k, CHIPS * PAIRS, stride=ROWS), :]
        second = gathered[pl.ds(k + 1, CHIPS * PAIRS, stride=ROWS), :]
        for chunk, value in zip(chunks, pair_up(first, second)):
            chunk.append(value)
    left = split(jnp.concatenate([jnp.concatenate(chunk, 1) for chunk in chunks], 0))
    for side in range(2):
        right = split(jnp.where(core == side, own[...], other[...]))
        result = product(left, right)
        for quarter in range(2):
            both = result[:, quarter * LANES : (quarter + 1) * LANES]
            rows = pair_up(both[: CHIPS * PAIRS], both[CHIPS * PAIRS :])
            for inner, value in enumerate(rows):
                j = side * 4 + quarter * 2 + inner
                out[pl.ds(j, CHIPS * PAIRS, stride=ROWS), :] = value


def sum_kernel(received, near_cycle, far_cycle, near, far):
    first = lax.axis_index("zh") == 0
    for row in range(0, BLOCK, ROWS):
        sums = []
        for start in range(row, 4 * BLOCK, BLOCK):
            total = received[0, start : start + ROWS, :]
            for place in range(1, Y):
                total = total + received[place, start : start + ROWS, :]
            sums.append(total)
        rows = slice(row, row + ROWS)
        near_cycle[rows, :] = jnp.where(first, sums[0], sums[1])
        far_cycle[rows, :] = jnp.where(first, sums[1], sums[0])
        near[rows, :] = jnp.where(first, sums[2], sums[3])
        far[rows, :] = jnp.where(first, sums[3], sums[2])


def ladder_kernel(window, integrals, cycle, out):
    out[:, : ZH * BLOCK, :] = cycle[...]
    lefts = []
    for part in range(2):
        rows = window[:, part * ROWS : (part + 1) * ROWS, :]
        lefts.append(rows.reshape(CHIPS * ROWS, LANES))
    left = split(jnp.concatenate(lefts, 1))
    width = PAIRS * LANES
    for start in range(0, width, 2 * LANES):
        stop = min(start + 2 * LANES, width)
        result = product(left, split(integrals[:, start:stop]))
        for column in range(start, stop, LANES):
            value = result[:, column - start : column - start + LANES]
            for zh in range(ZH):
                rows = pl.ds((ZH + zh) * BLOCK + column // LANES * ROWS, ROWS)
                part = value[zh * Y * ROWS : (zh + 1) * Y * ROWS]
                out[:, rows, :] = part.reshape(Y, ROWS, LANES)


def last_kernel(tiles, occupied, virtual, near, far, near_cycle, far_cycle, out):
    column = lax.axis_index("zl") * (X * CORE) + lax.axis_index("x") * CORE + lax.axis_index("core")
    row = lax.axis_index("zh") * Y + lax.axis_index("y")
    shape = (ROWS, LANES)
    lane = lax.broadcasted_iota(jnp.int32, shape, 1)
    line = lax.broadcasted_iota(jnp.int32, shape, 0)
    spectator = jnp.zeros(shape, jnp.float32)
    for b in range(TILE):
        spectator = jnp.where(lane % TILE == b, virtual[tiles[0] * TILE + b], spectator)
    rows = jnp.zeros(shape, jnp.float32)
    for j in range(ROWS):
        rows = jnp.where(line == j, occupied[row * ROWS + j], rows)
    for pair in range(PAIRS):
        piece = pl.ds(pair * ROWS, ROWS)
        total = (near[piece, :] + far[piece, :]) + (near_cycle[piece, :] + far_cycle[piece, :])
        a = column * (2 * PAIRS) + 2 * pair
        energy = jnp.where(lane < TILE, virtual[a], virtual[a + 1]) + spectator
        out[0, :, pair * LANES : (pair + 1) * LANES] = total / (energy - occupied[0] - rows)


def call(kernel, shapes, specs, scratch=()):
    return pl.pallas_call(
        kernel,
        out_shape=[jax.ShapeDtypeStruct(shape, jnp.float32) for shape in shapes],
        in_specs=specs,
        out_specs=[VMEM] * len(shapes),
        scratch_shapes=[pltpu.VMEM(shape, jnp.float32) for shape in scratch],
        compiler_params=PARAMS,
    )


def places(rule):
    pairs = []
    for chip in range(CHIPS):
        for core in range(CORE):
            for place in range(ZH * Y):
                to = rule(chip, core, place)
                pairs.append(
                    (
                        (chip * CORE + core) * ZH * Y + place,
                        (to[0] * CORE + to[1]) * ZH * Y + to[2],
                    )
                )
    return pairs


def chip_of(block):
    return block % ZL * X + block // ZL


def near_rule(chip, core, place):
    zh, y = divmod(place, Y)
    return chip_of(2 * y + zh), core, chip


def far_rule(chip, core, place):
    zh, y = divmod(place, Y)
    return chip_of(2 * y + 1 - zh), core, chip


def per_device(amplitudes, cycle_block, ladder_block, occupied, virtual, tiles):
    swap = [(0, 1), (1, 0)]
    other = lax.ppermute(cycle_block, "core", swap)
    (copies,) = call(pack_kernel, [(ZL, BLOCK, LANES)], [VMEM])(amplitudes)
    column = lax.all_to_all(copies, "zl", 0, 0, tiled=True)
    copies = jnp.broadcast_to(column.reshape(1, ZL * BLOCK, LANES), (X, ZL * BLOCK, LANES))
    gathered = lax.all_to_all(copies, "x", 0, 0, tiled=True)
    gathered = gathered.reshape(CHIPS * BLOCK, LANES)

    (window,) = call(
        window_kernel,
        [(CHIPS * 2 * ROWS, LANES)],
        [SMEM, VMEM],
        [(TILE // 2 * ROWS, LANES), (LANES, LANES), (LANES, LANES)],
    )(tiles, gathered)
    window = window + lax.ppermute(window, "core", swap)
    window = lax.all_to_all(window.reshape(CHIPS, 2 * ROWS, LANES), ("zh", "y"), 0, 0, tiled=True)

    (cycle,) = call(cycle_kernel, [(CHIPS * BLOCK, LANES)], [VMEM] * 3)(gathered, cycle_block, other)
    integrals = ladder_block.reshape(-1, ladder_block.shape[2])
    (parts,) = call(ladder_kernel, [(Y, 4 * BLOCK, LANES)], [VMEM] * 3)(
        window, integrals, cycle.reshape(Y, ZH * BLOCK, LANES)
    )
    parts = lax.all_to_all(parts, "y", 0, 0, tiled=True)
    near_cycle, far_cycle, near, far = call(sum_kernel, [(BLOCK, LANES)] * 4, [VMEM])(parts)
    near_cycle = lax.ppermute(near_cycle, EVERY, places(near_rule))
    far_cycle = lax.ppermute(far_cycle, EVERY, places(far_rule))
    far = lax.ppermute(far, "zh", swap)
    (result,) = call(last_kernel, [amplitudes.shape], [SMEM] * 3 + [VMEM] * 4)(
        tiles, occupied, virtual, near, far, near_cycle, far_cycle
    )
    return result


def solution(mesh):
    parts = Mesh(mesh.devices.reshape(ZL, X, CORE, ZH, Y), EVERY)
    amp, intg = ("zl", "x", "core"), ("zh", "y")
    return jax.shard_map(
        per_device,
        mesh=parts,
        in_specs=(P(None, intg, amp), P(intg, amp), P(intg, None, amp), P(), P(), P()),
        out_specs=P(None, intg, amp),
        check_vma=False,
    )
```

```python
import functools

import jax
import jax.numpy as jnp
from jax import lax
from jax.experimental import pallas as pl
from jax.experimental.pallas import tpu as pltpu
from jax.sharding import Mesh
from jax.sharding import PartitionSpec as P

ZL, X, CORE, ZH, Y = 4, 4, 2, 2, 8
CHIPS = ZL * X
ROWS = 8
TILE = 64
PAIRS = 13
LANES = 2 * TILE
BLOCK = PAIRS * ROWS
SIDE = (PAIRS + 1) // 2
SKIP = PAIRS - SIDE
HALF = ROWS // ZH
PIECE = PAIRS * HALF
EVERY = ("zl", "x", "core", "zh", "y")
VMEM = pl.BlockSpec(memory_space=pltpu.VMEM)
SMEM = pl.BlockSpec(memory_space=pltpu.SMEM)
PARAMS = pltpu.CompilerParams(vmem_limit_bytes=32 * 1024 * 1024)


def split(value):
    high = value.astype(jnp.bfloat16)
    return high, (value - high.astype(jnp.float32)).astype(jnp.bfloat16)


def product(left, right):
    dot = functools.partial(jnp.dot, preferred_element_type=jnp.float32)
    return dot(left[0], right[1]) + dot(left[1], right[0]) + dot(left[0], right[0])


def low_half(shape):
    return lax.broadcasted_iota(jnp.int32, shape, 1) < TILE


def pair_up(first, second):
    low = low_half(first.shape)
    return (
        jnp.where(low, first, pltpu.roll(second, TILE, 1)),
        jnp.where(low, pltpu.roll(first, TILE, 1), second),
    )


def pack_kernel(amplitudes, out):
    for pair in range(PAIRS):
        tile = amplitudes[0, :, pair * LANES : (pair + 1) * LANES]
        for chip in range(ZH * ZL):
            out[chip, pair * ROWS : (pair + 1) * ROWS, :] = tile


def window_kernel(tiles, gathered, out, window, columns, turned):
    core, first = lax.axis_index("core"), lax.axis_index("zh") == 0
    for pair in range(TILE // 2):
        place = tiles[1] * (TILE // 2) + pair
        owner = place // PAIRS
        chip = owner // CORE
        for zh in range(ZH):
            block = (chip % X * ZH + zh) * ZL + chip // X
            row = (block * PAIRS + (place - owner * PAIRS)) * ROWS
            tile = gathered[pl.ds(pl.multiple_of(row, ROWS), ROWS), :]
            start = (zh * (TILE // 2) + pair) * ROWS
            window[start : start + ROWS, :] = jnp.where(owner % CORE == core, tile, 0.0)
    for zh in range(ZH):
        for half in range(ROWS // 2):
            for inner in range(2):
                start = zh * (TILE // 2) * ROWS + half * 2 + inner
                both = window[pl.ds(start, TILE // 2, stride=ROWS), :]
                columns[pl.ds(inner * TILE, TILE // 2, stride=2), :] = both
                columns[pl.ds(inner * TILE + 1, TILE // 2, stride=2), :] = pltpu.roll(both, TILE, 1)
            turned[...] = jnp.transpose(columns[...])
            for part in range(2):
                even = turned[pl.ds(2 * part, CHIPS, stride=4), :]
                odd = turned[pl.ds(2 * part + 1, CHIPS, stride=4), :]
                for inner, value in enumerate(pair_up(even, odd)):
                    row = (zh * 2 + part) * ROWS + half * 2 + inner
                    mine = jnp.where(first, value[:Y], value[Y:])
                    out[pl.ds(row, Y, stride=4 * ROWS), :] = mine


def cycle_kernel(gathered, own, first, second, out, ordered):
    core, zh = lax.axis_index("core"), lax.axis_index("zh")
    span = ZL * BLOCK
    for x in range(X):
        for half in range(ZH):
            ordered[half, x * span : (x + 1) * span, :] = gathered[pl.ds((x * ZH + half) * span, span), :]
    chunks = ([], [])
    for half in range(ZH):
        for k in range(0, ROWS, 2):
            even = ordered[half, pl.ds(k, CHIPS * PAIRS, stride=ROWS), :]
            odd = ordered[half, pl.ds(k + 1, CHIPS * PAIRS, stride=ROWS), :]
            for chunk, value in zip(chunks, pair_up(even, odd)):
                chunk.append(value)
    left = split(jnp.concatenate([jnp.concatenate(chunk, 1) for chunk in chunks], 0))
    same = core == zh
    near = jnp.where(same, own[...], first[...])
    far = jnp.where(same, first[...], second[...])
    right = jnp.concatenate([jnp.where(zh == 0, near, far), jnp.where(zh == 0, far, near)], 0)
    result = product(left, split(right))
    for quarter in range(2):
        both = result[:, quarter * LANES : (quarter + 1) * LANES]
        rows = pair_up(both[: CHIPS * PAIRS], both[CHIPS * PAIRS :])
        for inner, value in enumerate(rows):
            out[pl.ds(quarter * 2 + inner, CHIPS * PAIRS, stride=HALF), :] = value


def join_kernel(cycle, own, other, out):
    for y in range(Y):
        out[y, :BLOCK, :] = cycle[y, :, :]
        for slot in range(2):
            start = BLOCK + slot * 4 * ROWS
            out[y, start : start + 4 * ROWS, :] = own[y ^ slot, :, :] + other[y ^ slot, :, :]


def sum_kernel(received, near, far):
    total = received[0, :BLOCK, :]
    for place in range(1, Y):
        total = total + received[place, :BLOCK, :]
    first = lax.axis_index("zh") == 0
    near[...] = jnp.where(first, total[:PIECE], total[PIECE:])
    far[...] = jnp.where(first, total[PIECE:], total[:PIECE])


def ladder_kernel(received, own, other, out):
    lefts = []
    for slot in range(2):
        for part in range(2):
            halves = []
            for zh in range(ZH):
                start = BLOCK + ((slot * ZH + zh) * 2 + part) * ROWS
                halves.append(received[:, start : start + ROWS, :].reshape(Y * ROWS, LANES))
            lefts.append(jnp.concatenate(halves, 0))
    left = split(jnp.concatenate(lefts, 1))
    first = lax.axis_index("y") % 2 * (SKIP * LANES)
    width = SIDE * LANES
    for start in range(0, width, 2 * LANES):
        stop = min(start + 2 * LANES, width)
        columns = pl.ds(pl.multiple_of(first + start, LANES), stop - start)
        right = jnp.concatenate([own[:, columns], other[:, start:stop]], 0)
        result = product(left, split(right))
        for column in range(start, stop, LANES):
            value = result[:, column - start : column - start + LANES]
            rows = pl.ds(column // LANES * ROWS, ROWS)
            out[:, rows, :] = value.reshape(CHIPS, ROWS, LANES)


def last_kernel(tiles, occupied, virtual, ladder, near, far, out):
    column = lax.axis_index("zl") * (X * CORE) + lax.axis_index("x") * CORE + lax.axis_index("core")
    row = lax.axis_index("zh") * Y + lax.axis_index("y")
    shape = (ROWS, LANES)
    lane = lax.broadcasted_iota(jnp.int32, shape, 1)
    line = lax.broadcasted_iota(jnp.int32, shape, 0)
    spectator = jnp.zeros(shape, jnp.float32)
    for b in range(TILE):
        spectator = jnp.where(lane % TILE == b, virtual[tiles[0] * TILE + b], spectator)
    rows = jnp.zeros(shape, jnp.float32)
    for j in range(ROWS):
        rows = jnp.where(line == j, occupied[row * ROWS + j], rows)
    straight = lax.axis_index("zl") % 2 == 0
    for pair in range(PAIRS):
        piece = pl.ds(pair * HALF, HALF)
        one, two = near[piece, :], far[piece, :]
        low, high = jnp.where(straight, one, two), jnp.where(straight, two, one)
        total = jnp.concatenate([low, high], 0)
        side = int(pair >= SIDE)
        rows_of_side = pl.ds((pair - side * SKIP) * ROWS, ROWS)
        for place in range(side, ZH * Y, 2):
            total = total + ladder[place, rows_of_side, :]
        a = column * (2 * PAIRS) + 2 * pair
        energy = jnp.where(lane < TILE, virtual[a], virtual[a + 1]) + spectator
        out[0, :, pair * LANES : (pair + 1) * LANES] = total / (energy - occupied[0] - rows)


def call(kernel, shapes, specs, scratch=()):
    return pl.pallas_call(
        kernel,
        out_shape=[jax.ShapeDtypeStruct(shape, jnp.float32) for shape in shapes],
        in_specs=specs,
        out_specs=[VMEM] * len(shapes),
        scratch_shapes=[pltpu.VMEM(shape, jnp.float32) for shape in scratch],
        compiler_params=PARAMS,
    )


def places(rule):
    pairs = []
    for chip in range(CHIPS):
        for core in range(CORE):
            for place in range(ZH * Y):
                to = rule(chip, core, place)
                pairs.append(
                    (
                        (chip * CORE + core) * ZH * Y + place,
                        (to[0] * CORE + to[1]) * ZH * Y + to[2],
                    )
                )
    return pairs


def chip_of(block):
    return block % ZL * X + block // ZL


def near_rule(chip, core, place):
    zh, y = divmod(place, Y)
    return chip_of(2 * y + zh), core, chip


def far_rule(chip, core, place):
    zh, y = divmod(place, Y)
    return chip_of(2 * y + 1 - zh), core, chip


def per_device(amplitudes, cycle_block, ladder_block, occupied, virtual, tiles):
    first = lax.ppermute(cycle_block, ("core", "zh"), [(0, 2), (3, 1), (2, 3), (1, 0)])
    second = lax.ppermute(first, ("core", "zh"), [(0, 2), (3, 1)])
    integrals = ladder_block.reshape(-1, ladder_block.shape[2])
    start = (1 - lax.axis_index("y") % 2) * (SKIP * LANES)
    side = lax.dynamic_slice_in_dim(integrals, start, SIDE * LANES, 1)
    side = lax.ppermute(side, "y", [(y, y ^ 1) for y in range(Y)])

    (copies,) = call(pack_kernel, [(ZH * ZL, BLOCK, LANES)], [VMEM])(amplitudes)
    column = lax.all_to_all(copies, ("zh", "zl"), 0, 0, tiled=True)
    span = ZH * ZL * BLOCK
    copies = jnp.broadcast_to(column.reshape(1, span, LANES), (X, span, LANES))
    gathered = lax.all_to_all(copies, "x", 0, 0, tiled=True)
    gathered = gathered.reshape(X * span, LANES)
    gathered, side = lax.optimization_barrier((gathered, side))

    (window,) = call(
        window_kernel,
        [(Y * 4 * ROWS, LANES)],
        [SMEM, VMEM],
        [(ZH * TILE // 2 * ROWS, LANES), (LANES, LANES), (LANES, LANES)],
    )(tiles, gathered)
    window = window.reshape(Y, 4 * ROWS, LANES)
    other_window = lax.ppermute(window, "core", [(0, 1), (1, 0)])
    (cycle,) = call(
        cycle_kernel, [(CHIPS * PIECE, LANES)], [VMEM] * 4, [(ZH, CHIPS * BLOCK, LANES)]
    )(gathered, cycle_block, first, second)
    (joined,) = call(join_kernel, [(Y, BLOCK + 8 * ROWS, LANES)], [VMEM] * 3)(
        cycle.reshape(Y, BLOCK, LANES), window, other_window
    )
    received = lax.all_to_all(joined, "y", 0, 0, tiled=True)
    (ladder,) = call(ladder_kernel, [(CHIPS, SIDE * ROWS, LANES)], [VMEM] * 3)(
        received, integrals, side
    )
    ladder, received = lax.optimization_barrier((ladder, received))
    near, far = call(sum_kernel, [(PIECE, LANES)] * 2, [VMEM])(received)
    near = lax.ppermute(near, EVERY, places(near_rule))
    far = lax.ppermute(far, EVERY, places(far_rule))
    ladder = lax.all_to_all(ladder, ("zh", "y"), 0, 0, tiled=True)
    (result,) = call(last_kernel, [amplitudes.shape], [SMEM] * 3 + [VMEM] * 3)(
        tiles, occupied, virtual, ladder, near, far
    )
    return result


def solution(mesh):
    parts = Mesh(mesh.devices.reshape(ZL, X, CORE, ZH, Y), EVERY)
    amp, intg = ("zl", "x", "core"), ("zh", "y")
    return jax.shard_map(
        per_device,
        mesh=parts,
        in_specs=(P(None, intg, amp), P(intg, amp), P(intg, None, amp), P(), P(), P()),
        out_specs=P(None, intg, amp),
        check_vma=False,
    )
```

```python
import functools

import jax
import jax.numpy as jnp
from jax import lax
from jax.experimental import pallas as pl
from jax.experimental.pallas import tpu as pltpu
from jax.sharding import Mesh
from jax.sharding import PartitionSpec as P

ZL, X, CORE, ZH, Y = 4, 4, 2, 2, 8
CHIPS = ZL * X
ROWS = 8
TILE = 64
PAIRS = 13
LANES = 2 * TILE
BLOCK = PAIRS * ROWS
SIDE = (PAIRS + 1) // 2
SKIP = PAIRS - SIDE
EVERY = ("zl", "x", "core", "zh", "y")
VMEM = pl.BlockSpec(memory_space=pltpu.VMEM)
SMEM = pl.BlockSpec(memory_space=pltpu.SMEM)
PARAMS = pltpu.CompilerParams(vmem_limit_bytes=32 * 1024 * 1024)


def split(value):
    high = value.astype(jnp.bfloat16)
    return high, (value - high.astype(jnp.float32)).astype(jnp.bfloat16)


def product(left, right):
    dot = functools.partial(jnp.dot, preferred_element_type=jnp.float32)
    return dot(left[0], right[1]) + dot(left[1], right[0]) + dot(left[0], right[0])


def low_half(shape):
    return lax.broadcasted_iota(jnp.int32, shape, 1) < TILE


def pair_up(first, second):
    low = low_half(first.shape)
    return (
        jnp.where(low, first, pltpu.roll(second, TILE, 1)),
        jnp.where(low, pltpu.roll(first, TILE, 1), second),
    )


def pack_kernel(amplitudes, out):
    for pair in range(PAIRS):
        tile = amplitudes[0, :, pair * LANES : (pair + 1) * LANES]
        for chip in range(ZL):
            out[chip, pair * ROWS : (pair + 1) * ROWS, :] = tile


def window_kernel(tiles, gathered, out, window, columns, turned):
    core = lax.axis_index("core")
    for pair in range(TILE // 2):
        place = tiles[1] * (TILE // 2) + pair
        owner = place // PAIRS
        chip = owner // CORE
        block = (chip % X) * ZL + chip // X
        row = (block * PAIRS + (place - owner * PAIRS)) * ROWS
        tile = gathered[pl.ds(pl.multiple_of(row, ROWS), ROWS), :]
        window[pair * ROWS : (pair + 1) * ROWS, :] = jnp.where(owner % 2 == core, tile, 0.0)
    for half in range(ROWS // 2):
        for inner in range(2):
            both = window[pl.ds(half * 2 + inner, TILE // 2, stride=ROWS), :]
            columns[pl.ds(inner * TILE, TILE // 2, stride=2), :] = both
            columns[pl.ds(inner * TILE + 1, TILE // 2, stride=2), :] = pltpu.roll(both, TILE, 1)
        turned[...] = jnp.transpose(columns[...])
        for part in range(2):
            even = turned[pl.ds(2 * part, CHIPS, stride=4), :]
            odd = turned[pl.ds(2 * part + 1, CHIPS, stride=4), :]
            for inner, value in enumerate(pair_up(even, odd)):
                row = part * ROWS + half * 2 + inner
                out[pl.ds(row, CHIPS, stride=2 * ROWS), :] = value


def cycle_kernel(gathered, own, other, out):
    core = lax.axis_index("core")
    chunks = ([], [])
    for k in range(0, ROWS, 2):
        first = gathered[pl.ds(k, CHIPS * PAIRS, stride=ROWS), :]
        second = gathered[pl.ds(k + 1, CHIPS * PAIRS, stride=ROWS), :]
        for chunk, value in zip(chunks, pair_up(first, second)):
            chunk.append(value)
    left = split(jnp.concatenate([jnp.concatenate(chunk, 1) for chunk in chunks], 0))
    for side in range(2):
        right = split(jnp.where(core == side, own[...], other[...]))
        result = product(left, right)
        for quarter in range(2):
            both = result[:, quarter * LANES : (quarter + 1) * LANES]
            rows = pair_up(both[: CHIPS * PAIRS], both[CHIPS * PAIRS :])
            for inner, value in enumerate(rows):
                j = side * 4 + quarter * 2 + inner
                out[pl.ds(j, CHIPS * PAIRS, stride=ROWS), :] = value


def join_kernel(cycle, own, other, out):
    for place in range(CHIPS):
        out[place, :BLOCK, :] = cycle[place, :, :]
        for start, source in ((BLOCK, place), (BLOCK + 2 * ROWS, place ^ 1)):
            out[place, start : start + 2 * ROWS, :] = own[source, :, :] + other[source, :, :]


def sum_kernel(received, out):
    total = received[0, :BLOCK, :]
    for place in range(1, CHIPS):
        total = total + received[place, :BLOCK, :]
    out[...] = total


def ladder_kernel(received, own, other, out):
    lefts = []
    for part in range(4):
        rows = received[:, BLOCK + part * ROWS : BLOCK + (part + 1) * ROWS, :]
        lefts.append(rows.reshape(CHIPS * ROWS, LANES))
    left = split(jnp.concatenate(lefts, 1))
    first = lax.axis_index("y") % 2 * (SKIP * LANES)
    width = SIDE * LANES
    for start in range(0, width, 2 * LANES):
        stop = min(start + 2 * LANES, width)
        columns = pl.ds(pl.multiple_of(first + start, LANES), stop - start)
        right = jnp.concatenate([own[:, columns], other[:, start:stop]], 0)
        result = product(left, split(right))
        for column in range(start, stop, LANES):
            value = result[:, column - start : column - start + LANES]
            rows = pl.ds(column // LANES * ROWS, ROWS)
            out[:, rows, :] = value.reshape(CHIPS, ROWS, LANES)


def last_kernel(tiles, occupied, virtual, ladder, cycle, out):
    column = lax.axis_index("zl") * (X * CORE) + lax.axis_index("x") * CORE + lax.axis_index("core")
    row = lax.axis_index("zh") * Y + lax.axis_index("y")
    shape = (ROWS, LANES)
    lane = lax.broadcasted_iota(jnp.int32, shape, 1)
    line = lax.broadcasted_iota(jnp.int32, shape, 0)
    spectator = jnp.zeros(shape, jnp.float32)
    for b in range(TILE):
        spectator = jnp.where(lane % TILE == b, virtual[tiles[0] * TILE + b], spectator)
    rows = jnp.zeros(shape, jnp.float32)
    for j in range(ROWS):
        rows = jnp.where(line == j, occupied[row * ROWS + j], rows)
    for pair in range(PAIRS):
        piece = pl.ds(pair * ROWS, ROWS)
        total = cycle[piece, :]
        side = int(pair >= SIDE)
        rows_of_side = pl.ds((pair - side * SKIP) * ROWS, ROWS)
        for place in range(side, ZH * Y, 2):
            total = total + ladder[place, rows_of_side, :]
        a = column * (2 * PAIRS) + 2 * pair
        energy = jnp.where(lane < TILE, virtual[a], virtual[a + 1]) + spectator
        out[0, :, pair * LANES : (pair + 1) * LANES] = total / (energy - occupied[0] - rows)


def call(kernel, shape, specs, scratch=()):
    return pl.pallas_call(
        kernel,
        out_shape=jax.ShapeDtypeStruct(shape, jnp.float32),
        in_specs=specs,
        out_specs=VMEM,
        scratch_shapes=[pltpu.VMEM(s, jnp.float32) for s in scratch],
        compiler_params=PARAMS,
    )


def places(rule):
    pairs = []
    for chip in range(CHIPS):
        for core in range(CORE):
            for place in range(ZH * Y):
                to = rule(chip, core, place)
                pairs.append(
                    (
                        (chip * CORE + core) * ZH * Y + place,
                        (to[0] * CORE + to[1]) * ZH * Y + to[2],
                    )
                )
    return pairs


def chip_of(block):
    return block % ZL * X + block // ZL


def owner_rule(chip, core, place):
    return chip_of(place), core, chip


def per_device(amplitudes, cycle_block, ladder_block, occupied, virtual, tiles):
    other = lax.ppermute(cycle_block, "core", [(0, 1), (1, 0)])
    integrals = ladder_block.reshape(-1, ladder_block.shape[2])
    start = (1 - lax.axis_index("y") % 2) * (SKIP * LANES)
    side = lax.dynamic_slice_in_dim(integrals, start, SIDE * LANES, 1)
    side = lax.ppermute(side, "y", [(y, y ^ 1) for y in range(Y)])
    copies = call(pack_kernel, (ZL, BLOCK, LANES), [VMEM])(amplitudes)
    column = lax.all_to_all(copies, "zl", 0, 0, tiled=True)
    copies = jnp.broadcast_to(column.reshape(1, ZL * BLOCK, LANES), (X, ZL * BLOCK, LANES))
    gathered = lax.all_to_all(copies, "x", 0, 0, tiled=True)
    gathered = gathered.reshape(CHIPS * BLOCK, LANES)
    gathered, side = lax.optimization_barrier((gathered, side))
    window = call(
        window_kernel,
        (CHIPS * 2 * ROWS, LANES),
        [SMEM, VMEM],
        [(TILE // 2 * ROWS, LANES), (LANES, LANES), (LANES, LANES)],
    )(tiles, gathered)
    window = window.reshape(CHIPS, 2 * ROWS, LANES)
    other_window = lax.ppermute(window, "core", [(0, 1), (1, 0)])
    cycle = call(cycle_kernel, (CHIPS * BLOCK, LANES), [VMEM] * 3)(gathered, cycle_block, other)
    cycle = cycle.reshape(CHIPS, BLOCK, LANES)
    joined = (CHIPS, BLOCK + 4 * ROWS, LANES)
    joined = call(join_kernel, joined, [VMEM] * 3)(cycle, window, other_window)
    received = lax.all_to_all(joined, ("zh", "y"), 0, 0, tiled=True)
    ladder = call(ladder_kernel, (CHIPS, SIDE * ROWS, LANES), [VMEM] * 3)(received, integrals, side)
    ladder, received = lax.optimization_barrier((ladder, received))
    cycle = call(sum_kernel, (BLOCK, LANES), [VMEM])(received)
    cycle = lax.ppermute(cycle, EVERY, places(owner_rule))
    ladder = lax.all_to_all(ladder, ("zh", "y"), 0, 0, tiled=True)
    return call(last_kernel, amplitudes.shape, [SMEM] * 3 + [VMEM] * 2)(
        tiles, occupied, virtual, ladder, cycle
    )


def solution(mesh):
    parts = Mesh(mesh.devices.reshape(ZL, X, CORE, ZH, Y), EVERY)
    amp, intg = ("zl", "x", "core"), ("zh", "y")
    return jax.shard_map(
        per_device,
        mesh=parts,
        in_specs=(P(None, intg, amp), P(intg, amp), P(intg, None, amp), P(), P(), P()),
        out_specs=P(None, intg, amp),
        check_vma=False,
    )
```

```python
import functools

import jax
import jax.numpy as jnp
from jax import lax
from jax.experimental import pallas as pl
from jax.experimental.pallas import tpu as pltpu
from jax.sharding import Mesh
from jax.sharding import PartitionSpec as P

ZL, X, CORE, ZH, YH, YL = 4, 4, 2, 2, 4, 2
GROUPS = ZH * YH
PLACES = GROUPS * YL
CHIPS = ZL * X
ROWS = 8
TILE = 64
PAIRS = 13
LANES = 2 * TILE
BLOCK = PAIRS * ROWS
SIDE = (PAIRS + 1) // 2
SKIP = PAIRS - SIDE
HALF = ROWS // YL
PIECE = PAIRS * HALF
EVERY = ("zl", "x", "core", "zh", "yh", "yl")
VMEM = pl.BlockSpec(memory_space=pltpu.VMEM)
SMEM = pl.BlockSpec(memory_space=pltpu.SMEM)
PARAMS = pltpu.CompilerParams(vmem_limit_bytes=32 * 1024 * 1024)


def split(value):
    high = value.astype(jnp.bfloat16)
    return high, (value - high.astype(jnp.float32)).astype(jnp.bfloat16)


def product(left, right):
    dot = functools.partial(jnp.dot, preferred_element_type=jnp.float32)
    return dot(left[0], right[1]) + dot(left[1], right[0]) + dot(left[0], right[0])


def low_half(shape):
    return lax.broadcasted_iota(jnp.int32, shape, 1) < TILE


def pair_up(first, second):
    low = low_half(first.shape)
    return (
        jnp.where(low, first, pltpu.roll(second, TILE, 1)),
        jnp.where(low, pltpu.roll(first, TILE, 1), second),
    )


def pack_kernel(amplitudes, out):
    for pair in range(PAIRS):
        tile = amplitudes[0, :, pair * LANES : (pair + 1) * LANES]
        for chip in range(YL * ZL):
            out[chip, pair * ROWS : (pair + 1) * ROWS, :] = tile


def window_kernel(tiles, gathered, out, window, columns, turned):
    core = lax.axis_index("core")
    for pair in range(TILE // 2):
        place = tiles[1] * (TILE // 2) + pair
        owner = place // PAIRS
        chip = owner // CORE
        for yl in range(YL):
            block = (chip % X * YL + yl) * ZL + chip // X
            row = (block * PAIRS + (place - owner * PAIRS)) * ROWS
            tile = gathered[pl.ds(pl.multiple_of(row, ROWS), ROWS), :]
            start = (yl * (TILE // 2) + pair) * ROWS
            window[start : start + ROWS, :] = jnp.where(owner % CORE == core, tile, 0.0)
    for yl in range(YL):
        for half in range(ROWS // 2):
            for inner in range(2):
                start = yl * (TILE // 2) * ROWS + half * 2 + inner
                both = window[pl.ds(start, TILE // 2, stride=ROWS), :]
                columns[pl.ds(inner * TILE, TILE // 2, stride=2), :] = both
                columns[pl.ds(inner * TILE + 1, TILE // 2, stride=2), :] = pltpu.roll(both, TILE, 1)
            turned[...] = jnp.transpose(columns[...])
            for part in range(2):
                even = turned[pl.ds(2 * part, PLACES, stride=4), :]
                odd = turned[pl.ds(2 * part + 1, PLACES, stride=4), :]
                for inner, value in enumerate(pair_up(even, odd)):
                    row = (yl * 2 + part) * ROWS + half * 2 + inner
                    out[pl.ds(row, PLACES, stride=4 * ROWS), :] = value


def cycle_kernel(gathered, own, first, second, out, ordered):
    core, yl = lax.axis_index("core"), lax.axis_index("yl")
    span = ZL * BLOCK
    for x in range(X):
        for half in range(YL):
            ordered[half, x * span : (x + 1) * span, :] = gathered[pl.ds((x * YL + half) * span, span), :]
    chunks = ([], [])
    for half in range(YL):
        for k in range(0, ROWS, 2):
            even = ordered[half, pl.ds(k, CHIPS * PAIRS, stride=ROWS), :]
            odd = ordered[half, pl.ds(k + 1, CHIPS * PAIRS, stride=ROWS), :]
            for chunk, value in zip(chunks, pair_up(even, odd)):
                chunk.append(value)
    left = split(jnp.concatenate([jnp.concatenate(chunk, 1) for chunk in chunks], 0))
    same = core == yl
    near = jnp.where(same, own[...], first[...])
    far = jnp.where(same, first[...], second[...])
    right = jnp.concatenate([jnp.where(yl == 0, near, far), jnp.where(yl == 0, far, near)], 0)
    result = product(left, split(right))
    for quarter in range(2):
        both = result[:, quarter * LANES : (quarter + 1) * LANES]
        rows = pair_up(both[: CHIPS * PAIRS], both[CHIPS * PAIRS :])
        for inner, value in enumerate(rows):
            out[pl.ds(quarter * 2 + inner, CHIPS * PAIRS, stride=HALF), :] = value


def join_kernel(cycle, own, other, out):
    for group in range(GROUPS):
        out[group, :BLOCK, :] = cycle[group, :, :]
        out[group, BLOCK:, :] = own[group, :, :] + other[group, :, :]


def sum_kernel(received, near, far):
    total = received[0, :BLOCK, :]
    for group in range(1, GROUPS):
        total = total + received[group, :BLOCK, :]
    first = lax.axis_index("yl") == 0
    near[...] = jnp.where(first, total[:PIECE], total[PIECE:])
    far[...] = jnp.where(first, total[PIECE:], total[:PIECE])


def ladder_kernel(received, own, other, out):
    slots = []
    for slot in range(YL):
        lefts = []
        for part in range(2):
            halves = []
            for yl in range(YL):
                start = BLOCK + ((slot * YL + yl) * 2 + part) * ROWS
                rows = received[:, start : start + ROWS, :]
                halves.append(rows.reshape(GROUPS * ROWS, LANES))
            lefts.append(jnp.concatenate(halves, 0))
        slots.append(jnp.concatenate(lefts, 1))
    yl = lax.axis_index("yl")
    mine = jnp.where(yl == 0, slots[0], slots[1])
    theirs = jnp.where(yl == 0, slots[1], slots[0])
    left = split(jnp.concatenate([mine, theirs], 1))
    first = yl * (SKIP * LANES)
    width = SIDE * LANES
    for start in range(0, width, 2 * LANES):
        stop = min(start + 2 * LANES, width)
        columns = pl.ds(pl.multiple_of(first + start, LANES), stop - start)
        right = jnp.concatenate([own[:, columns], other[:, start:stop]], 0)
        result = product(left, split(right))
        for column in range(start, stop, LANES):
            value = result[:, column - start : column - start + LANES]
            rows = pl.ds(column // LANES * ROWS, ROWS)
            for place in range(YL):
                part = value[place * GROUPS * ROWS : (place + 1) * GROUPS * ROWS]
                out[:, place, rows, :] = part.reshape(GROUPS, ROWS, LANES)


def last_kernel(tiles, occupied, virtual, ladder, near, far, out):
    column = lax.axis_index("zl") * (X * CORE) + lax.axis_index("x") * CORE + lax.axis_index("core")
    row = (lax.axis_index("zh") * YH + lax.axis_index("yh")) * YL + lax.axis_index("yl")
    shape = (ROWS, LANES)
    lane = lax.broadcasted_iota(jnp.int32, shape, 1)
    line = lax.broadcasted_iota(jnp.int32, shape, 0)
    spectator = jnp.zeros(shape, jnp.float32)
    for b in range(TILE):
        spectator = jnp.where(lane % TILE == b, virtual[tiles[0] * TILE + b], spectator)
    rows = jnp.zeros(shape, jnp.float32)
    for j in range(ROWS):
        rows = jnp.where(line == j, occupied[row * ROWS + j], rows)
    straight = lax.axis_index("zl") % 2 == 0
    for pair in range(PAIRS):
        piece = pl.ds(pair * HALF, HALF)
        one, two = near[piece, :], far[piece, :]
        low, high = jnp.where(straight, one, two), jnp.where(straight, two, one)
        total = jnp.concatenate([low, high], 0)
        side = int(pair >= SIDE)
        rows_of_side = pl.ds((pair - side * SKIP) * ROWS, ROWS)
        for place in range(side, PLACES, YL):
            total = total + ladder[place, rows_of_side, :]
        a = column * (2 * PAIRS) + 2 * pair
        energy = jnp.where(lane < TILE, virtual[a], virtual[a + 1]) + spectator
        out[0, :, pair * LANES : (pair + 1) * LANES] = total / (energy - occupied[0] - rows)


def call(kernel, shapes, specs, scratch=()):
    return pl.pallas_call(
        kernel,
        out_shape=[jax.ShapeDtypeStruct(shape, jnp.float32) for shape in shapes],
        in_specs=specs,
        out_specs=[VMEM] * len(shapes),
        scratch_shapes=[pltpu.VMEM(shape, jnp.float32) for shape in scratch],
        compiler_params=PARAMS,
    )


def places(rule):
    pairs = []
    for chip in range(CHIPS):
        for core in range(CORE):
            for place in range(PLACES):
                to = rule(chip, core, place)
                source = (chip * CORE + core) * PLACES + place
                pairs.append((source, (to[0] * CORE + to[1]) * PLACES + to[2]))
    return pairs


def chip_of(block):
    return block % ZL * X + block // ZL


def near_rule(chip, core, place):
    return chip_of(place), core, chip


def far_rule(chip, core, place):
    return chip_of(place ^ 1), core, chip


def per_device(amplitudes, cycle_block, ladder_block, occupied, virtual, tiles):
    first = lax.ppermute(cycle_block, ("core", "yl"), [(0, 2), (3, 1), (2, 3), (1, 0)])
    second = lax.ppermute(first, ("core", "yl"), [(0, 2), (3, 1)])
    integrals = ladder_block.reshape(-1, ladder_block.shape[2])
    start = (1 - lax.axis_index("yl")) * (SKIP * LANES)
    side = lax.dynamic_slice_in_dim(integrals, start, SIDE * LANES, 1)
    side = lax.ppermute(side, "yl", [(0, 1), (1, 0)])

    (copies,) = call(pack_kernel, [(YL * ZL, BLOCK, LANES)], [VMEM])(amplitudes)
    column = lax.all_to_all(copies, ("yl", "zl"), 0, 0, tiled=True)
    span = YL * ZL * BLOCK
    copies = jnp.broadcast_to(column.reshape(1, span, LANES), (X, span, LANES))
    gathered = lax.all_to_all(copies, "x", 0, 0, tiled=True)
    gathered = gathered.reshape(X * span, LANES)
    gathered, side = lax.optimization_barrier((gathered, side))

    (window,) = call(
        window_kernel,
        [(PLACES * 4 * ROWS, LANES)],
        [SMEM, VMEM],
        [(YL * TILE // 2 * ROWS, LANES), (LANES, LANES), (LANES, LANES)],
    )(tiles, gathered)
    window = window.reshape(GROUPS, 8 * ROWS, LANES)
    other_window = lax.ppermute(window, "core", [(0, 1), (1, 0)])
    (cycle,) = call(
        cycle_kernel, [(CHIPS * PIECE, LANES)], [VMEM] * 4, [(YL, CHIPS * BLOCK, LANES)]
    )(gathered, cycle_block, first, second)
    (joined,) = call(join_kernel, [(GROUPS, BLOCK + 8 * ROWS, LANES)], [VMEM] * 3)(
        cycle.reshape(GROUPS, BLOCK, LANES), window, other_window
    )
    received = lax.all_to_all(joined, ("zh", "yh"), 0, 0, tiled=True)
    (ladder,) = call(ladder_kernel, [(GROUPS, YL, SIDE * ROWS, LANES)], [VMEM] * 3)(
        received, integrals, side
    )
    ladder, received = lax.optimization_barrier((ladder, received))
    near, far = call(sum_kernel, [(PIECE, LANES)] * 2, [VMEM])(received)
    near = lax.ppermute(near, EVERY, places(near_rule))
    far = lax.ppermute(far, EVERY, places(far_rule))
    ladder = ladder.reshape(PLACES, SIDE * ROWS, LANES)
    ladder = lax.all_to_all(ladder, ("zh", "yh", "yl"), 0, 0, tiled=True)
    (result,) = call(last_kernel, [amplitudes.shape], [SMEM] * 3 + [VMEM] * 3)(
        tiles, occupied, virtual, ladder, near, far
    )
    return result


def solution(mesh):
    parts = Mesh(mesh.devices.reshape(ZL, X, CORE, ZH, YH, YL), EVERY)
    amp, intg = ("zl", "x", "core"), ("zh", "yh", "yl")
    return jax.shard_map(
        per_device,
        mesh=parts,
        in_specs=(P(None, intg, amp), P(intg, amp), P(intg, None, amp), P(), P(), P()),
        out_specs=P(None, intg, amp),
        check_vma=False,
    )
```

```python
import functools

import jax
import jax.numpy as jnp
from jax import lax
from jax.experimental import pallas as pl
from jax.experimental.pallas import tpu as pltpu
from jax.sharding import Mesh
from jax.sharding import PartitionSpec as P

ZL, X, CORE, ZH, Y = 4, 4, 2, 2, 8
CHIPS = ZL * X
ROWS = 8
TILE = 64
PAIRS = 13
LANES = 2 * TILE
BLOCK = PAIRS * ROWS
EVERY = ("zl", "x", "core", "zh", "y")
VMEM = pl.BlockSpec(memory_space=pltpu.VMEM)
SMEM = pl.BlockSpec(memory_space=pltpu.SMEM)
PARAMS = pltpu.CompilerParams(vmem_limit_bytes=32 * 1024 * 1024)


def split(value):
    high = value.astype(jnp.bfloat16)
    return high, (value - high.astype(jnp.float32)).astype(jnp.bfloat16)


def product(left, right):
    dot = functools.partial(jnp.dot, preferred_element_type=jnp.float32)
    return dot(left[0], right[1]) + dot(left[1], right[0]) + dot(left[0], right[0])


def low_half(shape):
    return lax.broadcasted_iota(jnp.int32, shape, 1) < TILE


def pair_up(first, second):
    low = low_half(first.shape)
    return (
        jnp.where(low, first, pltpu.roll(second, TILE, 1)),
        jnp.where(low, pltpu.roll(first, TILE, 1), second),
    )


def pack_kernel(amplitudes, out):
    for pair in range(PAIRS):
        tile = amplitudes[0, :, pair * LANES : (pair + 1) * LANES]
        for chip in range(ZL):
            out[chip, pair * ROWS : (pair + 1) * ROWS, :] = tile


def window_kernel(tiles, gathered, out, window, columns, turned):
    core = lax.axis_index("core")
    for pair in range(TILE // 2):
        place = tiles[1] * (TILE // 2) + pair
        owner = place // PAIRS
        chip = owner // CORE
        block = (chip % X) * ZL + chip // X
        row = (block * PAIRS + (place - owner * PAIRS)) * ROWS
        tile = gathered[pl.ds(pl.multiple_of(row, ROWS), ROWS), :]
        window[pair * ROWS : (pair + 1) * ROWS, :] = jnp.where(owner % 2 == core, tile, 0.0)
    for half in range(ROWS // 2):
        for inner in range(2):
            both = window[pl.ds(half * 2 + inner, TILE // 2, stride=ROWS), :]
            columns[pl.ds(inner * TILE, TILE // 2, stride=2), :] = both
            columns[pl.ds(inner * TILE + 1, TILE // 2, stride=2), :] = pltpu.roll(both, TILE, 1)
        turned[...] = jnp.transpose(columns[...])
        for part in range(2):
            even = turned[pl.ds(2 * part, CHIPS, stride=4), :]
            odd = turned[pl.ds(2 * part + 1, CHIPS, stride=4), :]
            for inner, value in enumerate(pair_up(even, odd)):
                row = part * ROWS + half * 2 + inner
                out[pl.ds(row, CHIPS, stride=2 * ROWS), :] = value


def cycle_kernel(gathered, own, other, out):
    core = lax.axis_index("core")
    chunks = ([], [])
    for k in range(0, ROWS, 2):
        first = gathered[pl.ds(k, CHIPS * PAIRS, stride=ROWS), :]
        second = gathered[pl.ds(k + 1, CHIPS * PAIRS, stride=ROWS), :]
        for chunk, value in zip(chunks, pair_up(first, second)):
            chunk.append(value)
    left = split(jnp.concatenate([jnp.concatenate(chunk, 1) for chunk in chunks], 0))
    for side in range(2):
        right = split(jnp.where(core == side, own[...], other[...]))
        result = product(left, right)
        for quarter in range(2):
            both = result[:, quarter * LANES : (quarter + 1) * LANES]
            rows = pair_up(both[: CHIPS * PAIRS], both[CHIPS * PAIRS :])
            for inner, value in enumerate(rows):
                j = side * 4 + quarter * 2 + inner
                out[pl.ds(j, CHIPS * PAIRS, stride=ROWS), :] = value


def sum_kernel(received, out):
    total = received[0, :, :]
    for place in range(1, CHIPS):
        total = total + received[place, :, :]
    out[...] = total


def ladder_kernel(window, integrals, out):
    lefts = []
    for part in range(2):
        rows = window[:, part * ROWS : (part + 1) * ROWS, :]
        lefts.append(rows.reshape(CHIPS * ROWS, LANES))
    left = split(jnp.concatenate(lefts, 1))
    width = PAIRS * LANES
    for start in range(0, width, 2 * LANES):
        stop = min(start + 2 * LANES, width)
        result = product(left, split(integrals[:, start:stop]))
        for column in range(start, stop, LANES):
            value = result[:, column - start : column - start + LANES]
            rows = pl.ds(column // LANES * ROWS, ROWS)
            out[:, rows, :] = value.reshape(CHIPS, ROWS, LANES)


def last_kernel(tiles, occupied, virtual, ladder, cycle, out):
    column = lax.axis_index("zl") * (X * CORE) + lax.axis_index("x") * CORE + lax.axis_index("core")
    row = lax.axis_index("zh") * Y + lax.axis_index("y")
    shape = (ROWS, LANES)
    lane = lax.broadcasted_iota(jnp.int32, shape, 1)
    line = lax.broadcasted_iota(jnp.int32, shape, 0)
    spectator = jnp.zeros(shape, jnp.float32)
    for b in range(TILE):
        spectator = jnp.where(lane % TILE == b, virtual[tiles[0] * TILE + b], spectator)
    rows = jnp.zeros(shape, jnp.float32)
    for j in range(ROWS):
        rows = jnp.where(line == j, occupied[row * ROWS + j], rows)
    for pair in range(PAIRS):
        piece = pl.ds(pair * ROWS, ROWS)
        total = cycle[piece, :]
        for chip in range(CHIPS):
            total = total + ladder[chip, piece, :]
        a = column * (2 * PAIRS) + 2 * pair
        energy = jnp.where(lane < TILE, virtual[a], virtual[a + 1]) + spectator
        out[0, :, pair * LANES : (pair + 1) * LANES] = total / (energy - occupied[0] - rows)


def call(kernel, shape, specs, scratch=()):
    return pl.pallas_call(
        kernel,
        out_shape=jax.ShapeDtypeStruct(shape, jnp.float32),
        in_specs=specs,
        out_specs=VMEM,
        scratch_shapes=[pltpu.VMEM(s, jnp.float32) for s in scratch],
        compiler_params=PARAMS,
    )


def places(rule):
    pairs = []
    for chip in range(CHIPS):
        for core in range(CORE):
            for place in range(ZH * Y):
                to = rule(chip, core, place)
                pairs.append(
                    (
                        (chip * CORE + core) * ZH * Y + place,
                        (to[0] * CORE + to[1]) * ZH * Y + to[2],
                    )
                )
    return pairs


def chip_of(block):
    return block % ZL * X + block // ZL


def owner_rule(chip, core, place):
    return chip_of(place), core, chip


def per_device(amplitudes, cycle_block, ladder_block, occupied, virtual, tiles):
    other = lax.ppermute(cycle_block, "core", [(0, 1), (1, 0)])
    copies = call(pack_kernel, (ZL, BLOCK, LANES), [VMEM])(amplitudes)
    column = lax.all_to_all(copies, "zl", 0, 0, tiled=True)
    copies = jnp.broadcast_to(column.reshape(1, ZL * BLOCK, LANES), (X, ZL * BLOCK, LANES))
    gathered = lax.all_to_all(copies, "x", 0, 0, tiled=True)
    gathered = gathered.reshape(CHIPS * BLOCK, LANES)
    cycle = call(cycle_kernel, (CHIPS * BLOCK, LANES), [VMEM] * 3)(gathered, cycle_block, other)
    cycle, gathered = lax.optimization_barrier((cycle, gathered))
    cycle = lax.all_to_all(cycle.reshape(CHIPS, BLOCK, LANES), ("zh", "y"), 0, 0, tiled=True)

    window = call(
        window_kernel,
        (CHIPS * 2 * ROWS, LANES),
        [SMEM, VMEM],
        [(TILE // 2 * ROWS, LANES), (LANES, LANES), (LANES, LANES)],
    )(tiles, gathered)
    window = window + lax.ppermute(window, "core", [(0, 1), (1, 0)])
    window, cycle = lax.optimization_barrier((window, cycle))
    window = lax.all_to_all(window.reshape(CHIPS, 2 * ROWS, LANES), ("zh", "y"), 0, 0, tiled=True)
    cycle = call(sum_kernel, (BLOCK, LANES), [VMEM])(cycle)
    cycle = lax.ppermute(cycle, EVERY, places(owner_rule))
    window, cycle = lax.optimization_barrier((window, cycle))

    integrals = ladder_block.reshape(-1, ladder_block.shape[2])
    ladder = call(ladder_kernel, (CHIPS, BLOCK, LANES), [VMEM] * 2)(window, integrals)
    ladder = lax.all_to_all(ladder, ("zh", "y"), 0, 0, tiled=True)
    return call(last_kernel, amplitudes.shape, [SMEM] * 3 + [VMEM] * 2)(
        tiles, occupied, virtual, ladder, cycle
    )


def solution(mesh):
    parts = Mesh(mesh.devices.reshape(ZL, X, CORE, ZH, Y), EVERY)
    amp, intg = ("zl", "x", "core"), ("zh", "y")
    return jax.shard_map(
        per_device,
        mesh=parts,
        in_specs=(P(None, intg, amp), P(intg, amp), P(intg, None, amp), P(), P(), P()),
        out_specs=P(None, intg, amp),
        check_vma=False,
    )
```

```python
import functools

import jax
import jax.numpy as jnp
from jax import lax
from jax.experimental import pallas as pl
from jax.experimental.pallas import tpu as pltpu
from jax.sharding import Mesh
from jax.sharding import PartitionSpec as P

ZL, X, CORE, ZH, Y = 4, 4, 2, 2, 8
CHIPS = ZL * X
ROWS = 8
TILE = 64
PAIRS = 13
LANES = 2 * TILE
BLOCK = PAIRS * ROWS
SIDE = (PAIRS + 1) // 2
SKIP = PAIRS - SIDE
HALF = ROWS // ZH
PIECE = PAIRS * HALF
EVERY = ("zl", "x", "core", "zh", "y")
VMEM = pl.BlockSpec(memory_space=pltpu.VMEM)
SMEM = pl.BlockSpec(memory_space=pltpu.SMEM)
PARAMS = pltpu.CompilerParams(vmem_limit_bytes=32 * 1024 * 1024)


def split(value):
    high = value.astype(jnp.bfloat16)
    return high, (value - high.astype(jnp.float32)).astype(jnp.bfloat16)


def product(left, right):
    dot = functools.partial(jnp.dot, preferred_element_type=jnp.float32)
    return dot(left[0], right[1]) + dot(left[1], right[0]) + dot(left[0], right[0])


def low_half(shape):
    return lax.broadcasted_iota(jnp.int32, shape, 1) < TILE


def pair_up(first, second):
    low = low_half(first.shape)
    return (
        jnp.where(low, first, pltpu.roll(second, TILE, 1)),
        jnp.where(low, pltpu.roll(first, TILE, 1), second),
    )


def pack_kernel(amplitudes, out):
    for pair in range(PAIRS):
        tile = amplitudes[0, :, pair * LANES : (pair + 1) * LANES]
        for chip in range(ZH * ZL):
            out[chip, pair * ROWS : (pair + 1) * ROWS, :] = tile


def window_kernel(tiles, gathered, out, window, columns, turned):
    core, first = lax.axis_index("core"), lax.axis_index("zh") == 0
    for pair in range(TILE // 2):
        place = tiles[1] * (TILE // 2) + pair
        owner = place // PAIRS
        chip = owner // CORE
        for zh in range(ZH):
            block = (chip % X * ZH + zh) * ZL + chip // X
            row = (block * PAIRS + (place - owner * PAIRS)) * ROWS
            tile = gathered[pl.ds(pl.multiple_of(row, ROWS), ROWS), :]
            start = (zh * (TILE // 2) + pair) * ROWS
            window[start : start + ROWS, :] = jnp.where(owner % CORE == core, tile, 0.0)
    for zh in range(ZH):
        for half in range(ROWS // 2):
            for inner in range(2):
                start = zh * (TILE // 2) * ROWS + half * 2 + inner
                both = window[pl.ds(start, TILE // 2, stride=ROWS), :]
                columns[pl.ds(inner * TILE, TILE // 2, stride=2), :] = both
                columns[pl.ds(inner * TILE + 1, TILE // 2, stride=2), :] = pltpu.roll(both, TILE, 1)
            turned[...] = jnp.transpose(columns[...])
            for part in range(2):
                even = turned[pl.ds(2 * part, CHIPS, stride=4), :]
                odd = turned[pl.ds(2 * part + 1, CHIPS, stride=4), :]
                for inner, value in enumerate(pair_up(even, odd)):
                    row = (zh * 2 + part) * ROWS + half * 2 + inner
                    mine = jnp.where(first, value[:Y], value[Y:])
                    out[pl.ds(row, Y, stride=4 * ROWS), :] = mine


def cycle_kernel(gathered, own, first, second, out, ordered):
    core, zh = lax.axis_index("core"), lax.axis_index("zh")
    span = ZL * BLOCK
    for x in range(X):
        for half in range(ZH):
            ordered[half, x * span : (x + 1) * span, :] = gathered[pl.ds((x * ZH + half) * span, span), :]
    chunks = ([], [])
    for half in range(ZH):
        for k in range(0, ROWS, 2):
            even = ordered[half, pl.ds(k, CHIPS * PAIRS, stride=ROWS), :]
            odd = ordered[half, pl.ds(k + 1, CHIPS * PAIRS, stride=ROWS), :]
            for chunk, value in zip(chunks, pair_up(even, odd)):
                chunk.append(value)
    left = split(jnp.concatenate([jnp.concatenate(chunk, 1) for chunk in chunks], 0))
    same = core == zh
    near = jnp.where(same, own[...], first[...])
    far = jnp.where(same, first[...], second[...])
    right = jnp.concatenate([jnp.where(zh == 0, near, far), jnp.where(zh == 0, far, near)], 0)
    result = product(left, split(right))
    for quarter in range(2):
        both = result[:, quarter * LANES : (quarter + 1) * LANES]
        rows = pair_up(both[: CHIPS * PAIRS], both[CHIPS * PAIRS :])
        for inner, value in enumerate(rows):
            out[pl.ds(quarter * 2 + inner, CHIPS * PAIRS, stride=HALF), :] = value


def join_kernel(cycle, own, other, out):
    for y in range(Y):
        out[y, :BLOCK, :] = cycle[y, :, :]
        for slot in range(2):
            start = BLOCK + slot * 4 * ROWS
            out[y, start : start + 4 * ROWS, :] = own[y ^ slot, :, :] + other[y ^ slot, :, :]


def sum_kernel(received, near, far):
    total = received[0, :BLOCK, :]
    for place in range(1, Y):
        total = total + received[place, :BLOCK, :]
    first = lax.axis_index("zh") == 0
    near[...] = jnp.where(first, total[:PIECE], total[PIECE:])
    far[...] = jnp.where(first, total[PIECE:], total[:PIECE])


def ladder_kernel(received, own, other, out):
    lefts = []
    for slot in range(2):
        for part in range(2):
            halves = []
            for zh in range(ZH):
                start = BLOCK + ((slot * ZH + zh) * 2 + part) * ROWS
                halves.append(received[:, start : start + ROWS, :].reshape(Y * ROWS, LANES))
            lefts.append(jnp.concatenate(halves, 0))
    left = split(jnp.concatenate(lefts, 1))
    first = lax.axis_index("y") % 2 * (SKIP * LANES)
    width = SIDE * LANES
    for start in range(0, width, 2 * LANES):
        stop = min(start + 2 * LANES, width)
        columns = pl.ds(pl.multiple_of(first + start, LANES), stop - start)
        right = jnp.concatenate([own[:, columns], other[:, start:stop]], 0)
        result = product(left, split(right))
        for column in range(start, stop, LANES):
            value = result[:, column - start : column - start + LANES]
            rows = pl.ds(column // LANES * ROWS, ROWS)
            out[:, rows, :] = value.reshape(CHIPS, ROWS, LANES)


def last_kernel(tiles, occupied, virtual, ladder, near, far, out):
    column = lax.axis_index("zl") * (X * CORE) + lax.axis_index("x") * CORE + lax.axis_index("core")
    row = lax.axis_index("zh") * Y + lax.axis_index("y")
    shape = (ROWS, LANES)
    lane = lax.broadcasted_iota(jnp.int32, shape, 1)
    line = lax.broadcasted_iota(jnp.int32, shape, 0)
    spectator = jnp.zeros(shape, jnp.float32)
    for b in range(TILE):
        spectator = jnp.where(lane % TILE == b, virtual[tiles[0] * TILE + b], spectator)
    rows = jnp.zeros(shape, jnp.float32)
    for j in range(ROWS):
        rows = jnp.where(line == j, occupied[row * ROWS + j], rows)
    straight = lax.axis_index("zl") % 2 == 0
    for pair in range(PAIRS):
        piece = pl.ds(pair * HALF, HALF)
        one, two = near[piece, :], far[piece, :]
        low, high = jnp.where(straight, one, two), jnp.where(straight, two, one)
        total = jnp.concatenate([low, high], 0)
        side = int(pair >= SIDE)
        rows_of_side = pl.ds((pair - side * SKIP) * ROWS, ROWS)
        for place in range(side, ZH * Y, 2):
            total = total + ladder[place, rows_of_side, :]
        a = column * (2 * PAIRS) + 2 * pair
        energy = jnp.where(lane < TILE, virtual[a], virtual[a + 1]) + spectator
        out[0, :, pair * LANES : (pair + 1) * LANES] = total / (energy - occupied[0] - rows)


def call(kernel, shapes, specs, scratch=()):
    return pl.pallas_call(
        kernel,
        out_shape=[jax.ShapeDtypeStruct(shape, jnp.float32) for shape in shapes],
        in_specs=specs,
        out_specs=[VMEM] * len(shapes),
        scratch_shapes=[pltpu.VMEM(shape, jnp.float32) for shape in scratch],
        compiler_params=PARAMS,
    )


def places(rule):
    pairs = []
    for chip in range(CHIPS):
        for core in range(CORE):
            for place in range(ZH * Y):
                to = rule(chip, core, place)
                pairs.append(
                    (
                        (chip * CORE + core) * ZH * Y + place,
                        (to[0] * CORE + to[1]) * ZH * Y + to[2],
                    )
                )
    return pairs


def chip_of(block):
    return block % ZL * X + block // ZL


def near_rule(chip, core, place):
    zh, y = divmod(place, Y)
    return chip_of(2 * y + zh), core, chip


def far_rule(chip, core, place):
    zh, y = divmod(place, Y)
    return chip_of(2 * y + 1 - zh), core, chip


def per_device(amplitudes, cycle_block, ladder_block, occupied, virtual, tiles):
    first = lax.ppermute(cycle_block, ("core", "zh"), [(0, 2), (3, 1), (2, 3), (1, 0)])
    integrals = ladder_block.reshape(-1, ladder_block.shape[2])
    start = (1 - lax.axis_index("y") % 2) * (SKIP * LANES)
    side = lax.dynamic_slice_in_dim(integrals, start, SIDE * LANES, 1)
    side = lax.ppermute(side, "y", [(y, y ^ 1) for y in range(Y)])

    (copies,) = call(pack_kernel, [(ZH * ZL, BLOCK, LANES)], [VMEM])(amplitudes)
    column = lax.all_to_all(copies, ("zh", "zl"), 0, 0, tiled=True)
    column, first = lax.optimization_barrier((column, first))
    span = ZH * ZL * BLOCK
    copies = jnp.broadcast_to(column.reshape(1, span, LANES), (X, span, LANES))
    gathered = lax.all_to_all(copies, "x", 0, 0, tiled=True)
    gathered = gathered.reshape(X * span, LANES)
    gathered, side = lax.optimization_barrier((gathered, side))

    second = lax.ppermute(first, ("core", "zh"), [(0, 2), (3, 1)])

    (window,) = call(
        window_kernel,
        [(Y * 4 * ROWS, LANES)],
        [SMEM, VMEM],
        [(ZH * TILE // 2 * ROWS, LANES), (LANES, LANES), (LANES, LANES)],
    )(tiles, gathered)
    window = window.reshape(Y, 4 * ROWS, LANES)
    other_window = lax.ppermute(window, "core", [(0, 1), (1, 0)])
    (cycle,) = call(
        cycle_kernel, [(CHIPS * PIECE, LANES)], [VMEM] * 4, [(ZH, CHIPS * BLOCK, LANES)]
    )(gathered, cycle_block, first, second)
    (joined,) = call(join_kernel, [(Y, BLOCK + 8 * ROWS, LANES)], [VMEM] * 3)(
        cycle.reshape(Y, BLOCK, LANES), window, other_window
    )
    received = lax.all_to_all(joined, "y", 0, 0, tiled=True)
    (ladder,) = call(ladder_kernel, [(CHIPS, SIDE * ROWS, LANES)], [VMEM] * 3)(
        received, integrals, side
    )
    ladder, received = lax.optimization_barrier((ladder, received))
    near, far = call(sum_kernel, [(PIECE, LANES)] * 2, [VMEM])(received)
    near = lax.ppermute(near, EVERY, places(near_rule))
    far = lax.ppermute(far, EVERY, places(far_rule))
    ladder = lax.all_to_all(ladder, ("zh", "y"), 0, 0, tiled=True)
    (result,) = call(last_kernel, [amplitudes.shape], [SMEM] * 3 + [VMEM] * 3)(
        tiles, occupied, virtual, ladder, near, far
    )
    return result


def solution(mesh):
    parts = Mesh(mesh.devices.reshape(ZL, X, CORE, ZH, Y), EVERY)
    amp, intg = ("zl", "x", "core"), ("zh", "y")
    return jax.shard_map(
        per_device,
        mesh=parts,
        in_specs=(P(None, intg, amp), P(intg, amp), P(intg, None, amp), P(), P(), P()),
        out_specs=P(None, intg, amp),
        check_vma=False,
    )
```

```python
import functools

import jax
import jax.numpy as jnp
from jax import lax
from jax.experimental import pallas as pl
from jax.experimental.pallas import tpu as pltpu
from jax.sharding import Mesh
from jax.sharding import PartitionSpec as P

ZL, X, CORE, ZH, Y = 4, 4, 2, 2, 8
CHIPS = ZL * X
ROWS = 8
TILE = 64
PAIRS = 13
LANES = 2 * TILE
BLOCK = PAIRS * ROWS
EVERY = ("zl", "x", "core", "zh", "y")
VMEM = pl.BlockSpec(memory_space=pltpu.VMEM)
SMEM = pl.BlockSpec(memory_space=pltpu.SMEM)
PARAMS = pltpu.CompilerParams(vmem_limit_bytes=32 * 1024 * 1024)


def split(value):
    high = value.astype(jnp.bfloat16)
    return high, (value - high.astype(jnp.float32)).astype(jnp.bfloat16)


def product(left, right):
    dot = functools.partial(jnp.dot, preferred_element_type=jnp.float32)
    return dot(left[0], right[1]) + dot(left[1], right[0]) + dot(left[0], right[0])


def low_half(shape):
    return lax.broadcasted_iota(jnp.int32, shape, 1) < TILE


def pair_up(first, second):
    low = low_half(first.shape)
    return (
        jnp.where(low, first, pltpu.roll(second, TILE, 1)),
        jnp.where(low, pltpu.roll(first, TILE, 1), second),
    )


def pack_kernel(amplitudes, out):
    for pair in range(PAIRS):
        tile = amplitudes[0, :, pair * LANES : (pair + 1) * LANES]
        for chip in range(ZL):
            out[chip, pair * ROWS : (pair + 1) * ROWS, :] = tile


def window_kernel(tiles, gathered, out, window, columns, turned):
    core = lax.axis_index("core")
    for pair in range(TILE // 2):
        place = tiles[1] * (TILE // 2) + pair
        owner = place // PAIRS
        chip = owner // CORE
        block = (chip % X) * ZL + chip // X
        row = (block * PAIRS + (place - owner * PAIRS)) * ROWS
        tile = gathered[pl.ds(pl.multiple_of(row, ROWS), ROWS), :]
        window[pair * ROWS : (pair + 1) * ROWS, :] = jnp.where(owner % 2 == core, tile, 0.0)
    for half in range(ROWS // 2):
        for inner in range(2):
            both = window[pl.ds(half * 2 + inner, TILE // 2, stride=ROWS), :]
            columns[pl.ds(inner * TILE, TILE // 2, stride=2), :] = both
            columns[pl.ds(inner * TILE + 1, TILE // 2, stride=2), :] = pltpu.roll(both, TILE, 1)
        turned[...] = jnp.transpose(columns[...])
        for part in range(2):
            even = turned[pl.ds(2 * part, CHIPS, stride=4), :]
            odd = turned[pl.ds(2 * part + 1, CHIPS, stride=4), :]
            for inner, value in enumerate(pair_up(even, odd)):
                row = part * ROWS + half * 2 + inner
                out[pl.ds(row, CHIPS, stride=2 * ROWS), :] = value


def cycle_kernel(gathered, own, other, out):
    core = lax.axis_index("core")
    chunks = ([], [])
    for k in range(0, ROWS, 2):
        first = gathered[pl.ds(k, CHIPS * PAIRS, stride=ROWS), :]
        second = gathered[pl.ds(k + 1, CHIPS * PAIRS, stride=ROWS), :]
        for chunk, value in zip(chunks, pair_up(first, second)):
            chunk.append(value)
    left = split(jnp.concatenate([jnp.concatenate(chunk, 1) for chunk in chunks], 0))
    for side in range(2):
        right = split(jnp.where(core == side, own[...], other[...]))
        result = product(left, right)
        for quarter in range(2):
            both = result[:, quarter * LANES : (quarter + 1) * LANES]
            rows = pair_up(both[: CHIPS * PAIRS], both[CHIPS * PAIRS :])
            for inner, value in enumerate(rows):
                j = side * 4 + quarter * 2 + inner
                out[pl.ds(j, CHIPS * PAIRS, stride=ROWS), :] = value


def join_kernel(cycle, own, other, out):
    for place in range(CHIPS):
        out[place, :BLOCK, :] = cycle[place, :, :]
        out[place, BLOCK:, :] = own[place, :, :] + other[place, :, :]


def sum_kernel(received, out):
    total = received[0, :BLOCK, :]
    for place in range(1, CHIPS):
        total = total + received[place, :BLOCK, :]
    out[...] = total


def ladder_kernel(received, integrals, out):
    lefts = []
    for part in range(2):
        rows = received[:, BLOCK + part * ROWS : BLOCK + (part + 1) * ROWS, :]
        lefts.append(rows.reshape(CHIPS * ROWS, LANES))
    left = split(jnp.concatenate(lefts, 1))
    width = PAIRS * LANES
    for start in range(0, width, 2 * LANES):
        stop = min(start + 2 * LANES, width)
        result = product(left, split(integrals[:, start:stop]))
        for column in range(start, stop, LANES):
            value = result[:, column - start : column - start + LANES]
            for zh in range(ZH):
                rows = pl.ds(zh * BLOCK + column // LANES * ROWS, ROWS)
                part = value[zh * Y * ROWS : (zh + 1) * Y * ROWS]
                out[:, rows, :] = part.reshape(Y, ROWS, LANES)


def halves_kernel(received, near, far):
    first = lax.axis_index("zh") == 0
    for row in range(0, BLOCK, ROWS):
        sums = []
        for start in (row, BLOCK + row):
            total = received[0, start : start + ROWS, :]
            for place in range(1, Y):
                total = total + received[place, start : start + ROWS, :]
            sums.append(total)
        near[row : row + ROWS, :] = jnp.where(first, sums[0], sums[1])
        far[row : row + ROWS, :] = jnp.where(first, sums[1], sums[0])


def last_kernel(tiles, occupied, virtual, near, far, cycle, out):
    column = lax.axis_index("zl") * (X * CORE) + lax.axis_index("x") * CORE + lax.axis_index("core")
    row = lax.axis_index("zh") * Y + lax.axis_index("y")
    shape = (ROWS, LANES)
    lane = lax.broadcasted_iota(jnp.int32, shape, 1)
    line = lax.broadcasted_iota(jnp.int32, shape, 0)
    spectator = jnp.zeros(shape, jnp.float32)
    for b in range(TILE):
        spectator = jnp.where(lane % TILE == b, virtual[tiles[0] * TILE + b], spectator)
    rows = jnp.zeros(shape, jnp.float32)
    for j in range(ROWS):
        rows = jnp.where(line == j, occupied[row * ROWS + j], rows)
    for pair in range(PAIRS):
        piece = pl.ds(pair * ROWS, ROWS)
        total = cycle[piece, :] + (near[piece, :] + far[piece, :])
        a = column * (2 * PAIRS) + 2 * pair
        energy = jnp.where(lane < TILE, virtual[a], virtual[a + 1]) + spectator
        out[0, :, pair * LANES : (pair + 1) * LANES] = total / (energy - occupied[0] - rows)


def call(kernel, shapes, specs, scratch=()):
    return pl.pallas_call(
        kernel,
        out_shape=[jax.ShapeDtypeStruct(shape, jnp.float32) for shape in shapes],
        in_specs=specs,
        out_specs=[VMEM] * len(shapes),
        scratch_shapes=[pltpu.VMEM(shape, jnp.float32) for shape in scratch],
        compiler_params=PARAMS,
    )


def places(rule):
    pairs = []
    for chip in range(CHIPS):
        for core in range(CORE):
            for place in range(ZH * Y):
                to = rule(chip, core, place)
                pairs.append(
                    (
                        (chip * CORE + core) * ZH * Y + place,
                        (to[0] * CORE + to[1]) * ZH * Y + to[2],
                    )
                )
    return pairs


def chip_of(block):
    return block % ZL * X + block // ZL


def owner_rule(chip, core, place):
    return chip_of(place), core, chip


def per_device(amplitudes, cycle_block, ladder_block, occupied, virtual, tiles):
    swap = [(0, 1), (1, 0)]
    other = lax.ppermute(cycle_block, "core", swap)
    (copies,) = call(pack_kernel, [(ZL, BLOCK, LANES)], [VMEM])(amplitudes)
    column = lax.all_to_all(copies, "zl", 0, 0, tiled=True)
    copies = jnp.broadcast_to(column.reshape(1, ZL * BLOCK, LANES), (X, ZL * BLOCK, LANES))
    gathered = lax.all_to_all(copies, "x", 0, 0, tiled=True)
    gathered = gathered.reshape(CHIPS * BLOCK, LANES)

    (window,) = call(
        window_kernel,
        [(CHIPS * 2 * ROWS, LANES)],
        [SMEM, VMEM],
        [(TILE // 2 * ROWS, LANES), (LANES, LANES), (LANES, LANES)],
    )(tiles, gathered)
    window = window.reshape(CHIPS, 2 * ROWS, LANES)
    other_window = lax.ppermute(window, "core", swap)
    (cycle,) = call(cycle_kernel, [(CHIPS * BLOCK, LANES)], [VMEM] * 3)(gathered, cycle_block, other)
    (joined,) = call(join_kernel, [(CHIPS, BLOCK + 2 * ROWS, LANES)], [VMEM] * 3)(
        cycle.reshape(CHIPS, BLOCK, LANES), window, other_window
    )
    received = lax.all_to_all(joined, ("zh", "y"), 0, 0, tiled=True)

    integrals = ladder_block.reshape(-1, ladder_block.shape[2])
    (ladder,) = call(ladder_kernel, [(Y, ZH * BLOCK, LANES)], [VMEM] * 2)(received, integrals)
    ladder, received = lax.optimization_barrier((ladder, received))
    (cycle,) = call(sum_kernel, [(BLOCK, LANES)], [VMEM])(received)
    cycle = lax.ppermute(cycle, EVERY, places(owner_rule))
    ladder = lax.all_to_all(ladder, "y", 0, 0, tiled=True)
    near, far = call(halves_kernel, [(BLOCK, LANES)] * 2, [VMEM])(ladder)
    far = lax.ppermute(far, "zh", swap)
    (result,) = call(last_kernel, [amplitudes.shape], [SMEM] * 3 + [VMEM] * 3)(
        tiles, occupied, virtual, near, far, cycle
    )
    return result


def solution(mesh):
    parts = Mesh(mesh.devices.reshape(ZL, X, CORE, ZH, Y), EVERY)
    amp, intg = ("zl", "x", "core"), ("zh", "y")
    return jax.shard_map(
        per_device,
        mesh=parts,
        in_specs=(P(None, intg, amp), P(intg, amp), P(intg, None, amp), P(), P(), P()),
        out_specs=P(None, intg, amp),
        check_vma=False,
    )
```

```python
import functools

import jax
import jax.numpy as jnp
from jax import lax
from jax.experimental import pallas as pl
from jax.experimental.pallas import tpu as pltpu
from jax.sharding import Mesh
from jax.sharding import PartitionSpec as P

ZL, X, CORE, ZH, Y = 4, 4, 2, 2, 8
CHIPS = ZL * X
ROWS = 8
TILE = 64
PAIRS = 13
LANES = 2 * TILE
BLOCK = PAIRS * ROWS
EVERY = ("zl", "x", "core", "zh", "y")
VMEM = pl.BlockSpec(memory_space=pltpu.VMEM)
SMEM = pl.BlockSpec(memory_space=pltpu.SMEM)
PARAMS = pltpu.CompilerParams(vmem_limit_bytes=32 * 1024 * 1024)


def split(value):
    high = value.astype(jnp.bfloat16)
    return high, (value - high.astype(jnp.float32)).astype(jnp.bfloat16)


def product(left, right):
    dot = functools.partial(jnp.dot, preferred_element_type=jnp.float32)
    return dot(left[0], right[1]) + dot(left[1], right[0]) + dot(left[0], right[0])


def low_half(shape):
    return lax.broadcasted_iota(jnp.int32, shape, 1) < TILE


def pair_up(first, second):
    low = low_half(first.shape)
    return (
        jnp.where(low, first, pltpu.roll(second, TILE, 1)),
        jnp.where(low, pltpu.roll(first, TILE, 1), second),
    )


def block_of(chip):
    return chip % X * ZL + chip // X


def pack_kernel(amplitudes, out):
    for pair in range(PAIRS):
        tile = amplitudes[0, :, pair * LANES : (pair + 1) * LANES]
        for chip in range(ZL):
            out[chip, pair * ROWS : (pair + 1) * ROWS, :] = tile


def window_kernel(tiles, gathered, out, window, columns, turned):
    core = lax.axis_index("core")
    for pair in range(TILE // 2):
        place = tiles[1] * (TILE // 2) + pair
        owner = place // PAIRS
        row = (block_of(owner // CORE) * PAIRS + (place - owner * PAIRS)) * ROWS
        tile = gathered[pl.ds(pl.multiple_of(row, ROWS), ROWS), :]
        window[pair * ROWS : (pair + 1) * ROWS, :] = jnp.where(owner % 2 == core, tile, 0.0)
    for half in range(ROWS // 2):
        for inner in range(2):
            both = window[pl.ds(half * 2 + inner, TILE // 2, stride=ROWS), :]
            columns[pl.ds(inner * TILE, TILE // 2, stride=2), :] = both
            columns[pl.ds(inner * TILE + 1, TILE // 2, stride=2), :] = pltpu.roll(both, TILE, 1)
        turned[...] = jnp.transpose(columns[...])
        for part in range(2):
            even = turned[pl.ds(2 * part, CHIPS, stride=4), :]
            odd = turned[pl.ds(2 * part + 1, CHIPS, stride=4), :]
            for inner, value in enumerate(pair_up(even, odd)):
                row = part * ROWS + half * 2 + inner
                out[pl.ds(row, CHIPS, stride=2 * ROWS), :] = value


def cycle_kernel(gathered, own, other, out):
    core = lax.axis_index("core")
    chunks = ([], [])
    for k in range(0, ROWS, 2):
        first = gathered[pl.ds(k, CHIPS * PAIRS, stride=ROWS), :]
        second = gathered[pl.ds(k + 1, CHIPS * PAIRS, stride=ROWS), :]
        for chunk, value in zip(chunks, pair_up(first, second)):
            chunk.append(value)
    left = split(jnp.concatenate([jnp.concatenate(chunk, 1) for chunk in chunks], 0))
    for side in range(2):
        right = split(jnp.where(core == side, own[...], other[...]))
        result = product(left, right)
        for quarter in range(2):
            both = result[:, quarter * LANES : (quarter + 1) * LANES]
            rows = pair_up(both[: CHIPS * PAIRS], both[CHIPS * PAIRS :])
            for inner, value in enumerate(rows):
                j = side * 4 + quarter * 2 + inner
                out[pl.ds(j, CHIPS * PAIRS, stride=ROWS), :] = value


def ladder_kernel(window, integrals, cycle, out):
    lefts = []
    for part in range(2):
        rows = window[:, part * ROWS : (part + 1) * ROWS, :]
        lefts.append(rows.reshape(CHIPS * ROWS, LANES))
    left = split(jnp.concatenate(lefts, 1))
    width = PAIRS * LANES
    for start in range(0, width, 2 * LANES):
        stop = min(start + 2 * LANES, width)
        result = product(left, split(integrals[:, start:stop]))
        for column in range(start, stop, LANES):
            value = result[:, column - start : column - start + LANES]
            rows = pl.ds(column // LANES * ROWS, ROWS)
            for chip in range(CHIPS):
                part = value[chip * ROWS : (chip + 1) * ROWS]
                out[chip, rows, :] = part + cycle[block_of(chip), rows, :]


def last_kernel(tiles, occupied, virtual, parts, out):
    column = lax.axis_index("zl") * (X * CORE) + lax.axis_index("x") * CORE + lax.axis_index("core")
    row = lax.axis_index("zh") * Y + lax.axis_index("y")
    shape = (ROWS, LANES)
    lane = lax.broadcasted_iota(jnp.int32, shape, 1)
    line = lax.broadcasted_iota(jnp.int32, shape, 0)
    spectator = jnp.zeros(shape, jnp.float32)
    for b in range(TILE):
        spectator = jnp.where(lane % TILE == b, virtual[tiles[0] * TILE + b], spectator)
    rows = jnp.zeros(shape, jnp.float32)
    for j in range(ROWS):
        rows = jnp.where(line == j, occupied[row * ROWS + j], rows)
    for pair in range(PAIRS):
        piece = pl.ds(pair * ROWS, ROWS)
        total = parts[0, piece, :]
        for place in range(1, ZH * Y):
            total = total + parts[place, piece, :]
        a = column * (2 * PAIRS) + 2 * pair
        energy = jnp.where(lane < TILE, virtual[a], virtual[a + 1]) + spectator
        out[0, :, pair * LANES : (pair + 1) * LANES] = total / (energy - occupied[0] - rows)


def call(kernel, shape, specs, scratch=()):
    return pl.pallas_call(
        kernel,
        out_shape=jax.ShapeDtypeStruct(shape, jnp.float32),
        in_specs=specs,
        out_specs=VMEM,
        scratch_shapes=[pltpu.VMEM(s, jnp.float32) for s in scratch],
        compiler_params=PARAMS,
    )


def per_device(amplitudes, cycle_block, ladder_block, occupied, virtual, tiles):
    other = lax.ppermute(cycle_block, "core", [(0, 1), (1, 0)])
    copies = call(pack_kernel, (ZL, BLOCK, LANES), [VMEM])(amplitudes)
    column = lax.all_to_all(copies, "zl", 0, 0, tiled=True)
    copies = jnp.broadcast_to(column.reshape(1, ZL * BLOCK, LANES), (X, ZL * BLOCK, LANES))
    gathered = lax.all_to_all(copies, "x", 0, 0, tiled=True)
    gathered = gathered.reshape(CHIPS * BLOCK, LANES)
    cycle = call(cycle_kernel, (CHIPS * BLOCK, LANES), [VMEM] * 3)(gathered, cycle_block, other)
    cycle, gathered = lax.optimization_barrier((cycle, gathered))
    cycle = lax.all_to_all(cycle.reshape(CHIPS, BLOCK, LANES), ("x", "zl"), 0, 0, tiled=True)

    window = call(
        window_kernel,
        (CHIPS * 2 * ROWS, LANES),
        [SMEM, VMEM],
        [(TILE // 2 * ROWS, LANES), (LANES, LANES), (LANES, LANES)],
    )(tiles, gathered)
    window = window + lax.ppermute(window, "core", [(0, 1), (1, 0)])
    window, cycle = lax.optimization_barrier((window, cycle))
    window = lax.all_to_all(window.reshape(CHIPS, 2 * ROWS, LANES), ("zh", "y"), 0, 0, tiled=True)

    integrals = ladder_block.reshape(-1, ladder_block.shape[2])
    parts = call(ladder_kernel, (CHIPS, BLOCK, LANES), [VMEM] * 3)(window, integrals, cycle)
    parts = lax.all_to_all(parts, ("zh", "y"), 0, 0, tiled=True)
    return call(last_kernel, amplitudes.shape, [SMEM] * 3 + [VMEM])(
        tiles, occupied, virtual, parts
    )


def solution(mesh):
    parts = Mesh(mesh.devices.reshape(ZL, X, CORE, ZH, Y), EVERY)
    amp, intg = ("zl", "x", "core"), ("zh", "y")
    return jax.shard_map(
        per_device,
        mesh=parts,
        in_specs=(P(None, intg, amp), P(intg, amp), P(intg, None, amp), P(), P(), P()),
        out_specs=P(None, intg, amp),
        check_vma=False,
    )
```

```python
import functools

import jax
import jax.numpy as jnp
from jax import lax
from jax.experimental import pallas as pl
from jax.experimental.pallas import tpu as pltpu
from jax.sharding import Mesh
from jax.sharding import PartitionSpec as P

ZL, X, CORE, ZH, Y = 4, 4, 2, 2, 8
CHIPS = ZL * X
ROWS = 8
TILE = 64
PAIRS = 13
LANES = 2 * TILE
BLOCK = PAIRS * ROWS
EVERY = ("zl", "x", "core", "zh", "y")
VMEM = pl.BlockSpec(memory_space=pltpu.VMEM)
SMEM = pl.BlockSpec(memory_space=pltpu.SMEM)
PARAMS = pltpu.CompilerParams(vmem_limit_bytes=32 * 1024 * 1024)


def split(value):
    high = value.astype(jnp.bfloat16)
    return high, (value - high.astype(jnp.float32)).astype(jnp.bfloat16)


def product(left, right):
    dot = functools.partial(jnp.dot, preferred_element_type=jnp.float32)
    return dot(left[0], right[1]) + dot(left[1], right[0]) + dot(left[0], right[0])


def low_half(shape):
    return lax.broadcasted_iota(jnp.int32, shape, 1) < TILE


def pair_up(first, second):
    low = low_half(first.shape)
    return (
        jnp.where(low, first, pltpu.roll(second, TILE, 1)),
        jnp.where(low, pltpu.roll(first, TILE, 1), second),
    )


def block_of(chip):
    return chip % X * ZL + chip // X


def pack_kernel(amplitudes, out):
    for pair in range(PAIRS):
        tile = amplitudes[0, :, pair * LANES : (pair + 1) * LANES]
        for chip in range(ZL):
            out[chip, pair * ROWS : (pair + 1) * ROWS, :] = tile


def window_kernel(tiles, gathered, near, far, window, columns, turned):
    core, first = lax.axis_index("core"), lax.axis_index("zh") == 0
    for pair in range(TILE // 2):
        place = tiles[1] * (TILE // 2) + pair
        owner = place // PAIRS
        row = (block_of(owner // CORE) * PAIRS + (place - owner * PAIRS)) * ROWS
        tile = gathered[pl.ds(pl.multiple_of(row, ROWS), ROWS), :]
        window[pair * ROWS : (pair + 1) * ROWS, :] = jnp.where(owner % 2 == core, tile, 0.0)
    for half in range(ROWS // 2):
        for inner in range(2):
            both = window[pl.ds(half * 2 + inner, TILE // 2, stride=ROWS), :]
            columns[pl.ds(inner * TILE, TILE // 2, stride=2), :] = both
            columns[pl.ds(inner * TILE + 1, TILE // 2, stride=2), :] = pltpu.roll(both, TILE, 1)
        turned[...] = jnp.transpose(columns[...])
        for part in range(2):
            even = turned[pl.ds(2 * part, CHIPS, stride=4), :]
            odd = turned[pl.ds(2 * part + 1, CHIPS, stride=4), :]
            for inner, value in enumerate(pair_up(even, odd)):
                row = part * ROWS + half * 2 + inner
                rows = pl.ds(row, Y, stride=2 * ROWS)
                near[rows, :] = jnp.where(first, value[:Y], value[Y:])
                far[rows, :] = jnp.where(first, value[Y:], value[:Y])


def join_kernel(near_own, near_other, far_one, far_two, out):
    out[:, : 2 * ROWS, :] = near_own[...] + near_other[...]
    out[:, 2 * ROWS :, :] = far_one[...] + far_two[...]


def cycle_kernel(gathered, own, other, out):
    core = lax.axis_index("core")
    chunks = ([], [])
    for k in range(0, ROWS, 2):
        first = gathered[pl.ds(k, CHIPS * PAIRS, stride=ROWS), :]
        second = gathered[pl.ds(k + 1, CHIPS * PAIRS, stride=ROWS), :]
        for chunk, value in zip(chunks, pair_up(first, second)):
            chunk.append(value)
    left = split(jnp.concatenate([jnp.concatenate(chunk, 1) for chunk in chunks], 0))
    for side in range(2):
        right = split(jnp.where(core == side, own[...], other[...]))
        result = product(left, right)
        for quarter in range(2):
            both = result[:, quarter * LANES : (quarter + 1) * LANES]
            rows = pair_up(both[: CHIPS * PAIRS], both[CHIPS * PAIRS :])
            for inner, value in enumerate(rows):
                j = side * 4 + quarter * 2 + inner
                out[pl.ds(j, CHIPS * PAIRS, stride=ROWS), :] = value


def ladder_kernel(window, integrals, cycle, out):
    first = lax.axis_index("zh") == 0
    lefts = []
    for part in range(2):
        near, far = [
            window[:, start : start + ROWS, :].reshape(Y * ROWS, LANES)
            for start in (part * ROWS, (2 + part) * ROWS)
        ]
        halves = [jnp.where(first, near, far), jnp.where(first, far, near)]
        lefts.append(jnp.concatenate(halves, 0))
    left = split(jnp.concatenate(lefts, 1))
    width = PAIRS * LANES
    for start in range(0, width, 2 * LANES):
        stop = min(start + 2 * LANES, width)
        result = product(left, split(integrals[:, start:stop]))
        for column in range(start, stop, LANES):
            value = result[:, column - start : column - start + LANES]
            rows = pl.ds(column // LANES * ROWS, ROWS)
            for chip in range(CHIPS):
                part = value[chip * ROWS : (chip + 1) * ROWS]
                out[chip, rows, :] = part + cycle[block_of(chip), rows, :]


def denominator_kernel(tiles, occupied, virtual, out):
    column = lax.axis_index("zl") * (X * CORE) + lax.axis_index("x") * CORE + lax.axis_index("core")
    row = lax.axis_index("zh") * Y + lax.axis_index("y")
    shape = (ROWS, LANES)
    lane = lax.broadcasted_iota(jnp.int32, shape, 1)
    line = lax.broadcasted_iota(jnp.int32, shape, 0)
    spectator = jnp.zeros(shape, jnp.float32)
    for b in range(TILE):
        spectator = jnp.where(lane % TILE == b, virtual[tiles[0] * TILE + b], spectator)
    rows = jnp.zeros(shape, jnp.float32)
    for j in range(ROWS):
        rows = jnp.where(line == j, occupied[row * ROWS + j], rows)
    for pair in range(PAIRS):
        a = column * (2 * PAIRS) + 2 * pair
        energy = jnp.where(lane < TILE, virtual[a], virtual[a + 1]) + spectator
        out[pair * ROWS : (pair + 1) * ROWS, :] = energy - occupied[0] - rows


def last_kernel(denominator, parts, out):
    for pair in range(PAIRS):
        piece = pl.ds(pair * ROWS, ROWS)
        total = parts[0, piece, :]
        for place in range(1, ZH * Y):
            total = total + parts[place, piece, :]
        out[0, :, pair * LANES : (pair + 1) * LANES] = total / denominator[piece, :]


def call(kernel, shapes, specs, scratch=()):
    return pl.pallas_call(
        kernel,
        out_shape=[jax.ShapeDtypeStruct(shape, jnp.float32) for shape in shapes],
        in_specs=specs,
        out_specs=[VMEM] * len(shapes),
        scratch_shapes=[pltpu.VMEM(shape, jnp.float32) for shape in scratch],
        compiler_params=PARAMS,
    )


def per_device(amplitudes, cycle_block, ladder_block, occupied, virtual, tiles):
    swap = [(0, 1), (1, 0)]
    other = lax.ppermute(cycle_block, "core", swap)
    (copies,) = call(pack_kernel, [(ZL, BLOCK, LANES)], [VMEM])(amplitudes)
    column = lax.all_to_all(copies, "zl", 0, 0, tiled=True)
    copies = jnp.broadcast_to(column.reshape(1, ZL * BLOCK, LANES), (X, ZL * BLOCK, LANES))
    gathered = lax.all_to_all(copies, "x", 0, 0, tiled=True)
    gathered = gathered.reshape(CHIPS * BLOCK, LANES)
    (cycle,) = call(cycle_kernel, [(CHIPS * BLOCK, LANES)], [VMEM] * 3)(gathered, cycle_block, other)
    cycle, gathered = lax.optimization_barrier((cycle, gathered))
    cycle = lax.all_to_all(cycle.reshape(CHIPS, BLOCK, LANES), ("x", "zl"), 0, 0, tiled=True)

    near, far = call(
        window_kernel,
        [(Y * 2 * ROWS, LANES)] * 2,
        [SMEM, VMEM],
        [(TILE // 2 * ROWS, LANES), (LANES, LANES), (LANES, LANES)],
    )(tiles, gathered)
    near, far = near.reshape(Y, 2 * ROWS, LANES), far.reshape(Y, 2 * ROWS, LANES)
    near_other = lax.ppermute(near, "core", swap)
    far_one = lax.ppermute(far, "zh", swap)
    far_two = lax.ppermute(far, ("core", "zh"), [(0, 3), (1, 2), (2, 1), (3, 0)])
    (window,) = call(join_kernel, [(Y, 4 * ROWS, LANES)], [VMEM] * 4)(
        near, near_other, far_one, far_two
    )
    (denominator,) = call(denominator_kernel, [(BLOCK, LANES)], [SMEM] * 3)(
        tiles, occupied, virtual
    )
    window, denominator, cycle = lax.optimization_barrier((window, denominator, cycle))
    window = lax.all_to_all(window, "y", 0, 0, tiled=True)

    integrals = ladder_block.reshape(-1, ladder_block.shape[2])
    (parts,) = call(ladder_kernel, [(CHIPS, BLOCK, LANES)], [VMEM] * 3)(window, integrals, cycle)
    parts = lax.all_to_all(parts, ("zh", "y"), 0, 0, tiled=True)
    (result,) = call(last_kernel, [amplitudes.shape], [VMEM] * 2)(denominator, parts)
    return result


def solution(mesh):
    parts = Mesh(mesh.devices.reshape(ZL, X, CORE, ZH, Y), EVERY)
    amp, intg = ("zl", "x", "core"), ("zh", "y")
    return jax.shard_map(
        per_device,
        mesh=parts,
        in_specs=(P(None, intg, amp), P(intg, amp), P(intg, None, amp), P(), P(), P()),
        out_specs=P(None, intg, amp),
        check_vma=False,
    )
```

```python
import functools

import jax
import jax.numpy as jnp
from jax import lax
from jax.experimental import pallas as pl
from jax.experimental.pallas import tpu as pltpu
from jax.sharding import Mesh
from jax.sharding import PartitionSpec as P

ZL, X, CORE, ZH, Y = 4, 4, 2, 2, 8
CHIPS = ZL * X
ROWS = 8
TILE = 64
PAIRS = 13
LANES = 2 * TILE
BLOCK = PAIRS * ROWS
EVERY = ("zl", "x", "core", "zh", "y")
VMEM = pl.BlockSpec(memory_space=pltpu.VMEM)
SMEM = pl.BlockSpec(memory_space=pltpu.SMEM)
PARAMS = pltpu.CompilerParams(vmem_limit_bytes=32 * 1024 * 1024)


def split(value):
    high = value.astype(jnp.bfloat16)
    return high, (value - high.astype(jnp.float32)).astype(jnp.bfloat16)


def product(left, right):
    dot = functools.partial(jnp.dot, preferred_element_type=jnp.float32)
    return dot(left[0], right[1]) + dot(left[1], right[0]) + dot(left[0], right[0])


def low_half(shape):
    return lax.broadcasted_iota(jnp.int32, shape, 1) < TILE


def pair_up(first, second):
    low = low_half(first.shape)
    return (
        jnp.where(low, first, pltpu.roll(second, TILE, 1)),
        jnp.where(low, pltpu.roll(first, TILE, 1), second),
    )


def block_of(chip):
    return chip % X * ZL + chip // X


def pack_kernel(amplitudes, out):
    for pair in range(PAIRS):
        tile = amplitudes[0, :, pair * LANES : (pair + 1) * LANES]
        for chip in range(ZL):
            out[chip, pair * ROWS : (pair + 1) * ROWS, :] = tile


def window_kernel(tiles, gathered, out, window, columns, turned):
    core, first = lax.axis_index("core"), lax.axis_index("zh") == 0
    for pair in range(TILE // 2):
        place = tiles[1] * (TILE // 2) + pair
        owner = place // PAIRS
        row = (block_of(owner // CORE) * PAIRS + (place - owner * PAIRS)) * ROWS
        tile = gathered[pl.ds(pl.multiple_of(row, ROWS), ROWS), :]
        window[pair * ROWS : (pair + 1) * ROWS, :] = jnp.where(owner % 2 == core, tile, 0.0)
    for half in range(ROWS // 2):
        for inner in range(2):
            both = window[pl.ds(half * 2 + inner, TILE // 2, stride=ROWS), :]
            columns[pl.ds(inner * TILE, TILE // 2, stride=2), :] = both
            columns[pl.ds(inner * TILE + 1, TILE // 2, stride=2), :] = pltpu.roll(both, TILE, 1)
        turned[...] = jnp.transpose(columns[...])
        for part in range(2):
            even = turned[pl.ds(2 * part, CHIPS, stride=4), :]
            odd = turned[pl.ds(2 * part + 1, CHIPS, stride=4), :]
            for inner, value in enumerate(pair_up(even, odd)):
                row = part * ROWS + half * 2 + inner
                rows = pl.ds(row, Y, stride=2 * ROWS)
                out[0, rows, :] = jnp.where(first, value[:Y], value[Y:])
                out[1, rows, :] = jnp.where(first, value[Y:], value[:Y])


def add_kernel(own, other, near, far):
    near[...] = own[0] + other[0]
    far[...] = own[1] + other[1]


def join_kernel(near, far, out):
    out[:, : 2 * ROWS, :] = near[...]
    out[:, 2 * ROWS :, :] = far[...]


def cycle_kernel(gathered, own, other, out):
    core = lax.axis_index("core")
    chunks = ([], [])
    for k in range(0, ROWS, 2):
        first = gathered[pl.ds(k, CHIPS * PAIRS, stride=ROWS), :]
        second = gathered[pl.ds(k + 1, CHIPS * PAIRS, stride=ROWS), :]
        for chunk, value in zip(chunks, pair_up(first, second)):
            chunk.append(value)
    left = split(jnp.concatenate([jnp.concatenate(chunk, 1) for chunk in chunks], 0))
    for side in range(2):
        right = split(jnp.where(core == side, own[...], other[...]))
        result = product(left, right)
        for quarter in range(2):
            both = result[:, quarter * LANES : (quarter + 1) * LANES]
            rows = pair_up(both[: CHIPS * PAIRS], both[CHIPS * PAIRS :])
            for inner, value in enumerate(rows):
                j = side * 4 + quarter * 2 + inner
                out[pl.ds(j, CHIPS * PAIRS, stride=ROWS), :] = value


def ladder_kernel(window, integrals, cycle, out):
    first = lax.axis_index("zh") == 0
    lefts = []
    for part in range(2):
        near, far = [
            window[:, start : start + ROWS, :].reshape(Y * ROWS, LANES)
            for start in (part * ROWS, (2 + part) * ROWS)
        ]
        halves = [jnp.where(first, near, far), jnp.where(first, far, near)]
        lefts.append(jnp.concatenate(halves, 0))
    left = split(jnp.concatenate(lefts, 1))
    width = PAIRS * LANES
    for start in range(0, width, 2 * LANES):
        stop = min(start + 2 * LANES, width)
        result = product(left, split(integrals[:, start:stop]))
        for column in range(start, stop, LANES):
            value = result[:, column - start : column - start + LANES]
            rows = pl.ds(column // LANES * ROWS, ROWS)
            for chip in range(CHIPS):
                part = value[chip * ROWS : (chip + 1) * ROWS]
                out[chip, rows, :] = part + cycle[block_of(chip), rows, :]


def denominator_kernel(tiles, occupied, virtual, out):
    column = lax.axis_index("zl") * (X * CORE) + lax.axis_index("x") * CORE + lax.axis_index("core")
    row = lax.axis_index("zh") * Y + lax.axis_index("y")
    shape = (ROWS, LANES)
    lane = lax.broadcasted_iota(jnp.int32, shape, 1)
    line = lax.broadcasted_iota(jnp.int32, shape, 0)
    spectator = jnp.zeros(shape, jnp.float32)
    for b in range(TILE):
        spectator = jnp.where(lane % TILE == b, virtual[tiles[0] * TILE + b], spectator)
    rows = jnp.zeros(shape, jnp.float32)
    for j in range(ROWS):
        rows = jnp.where(line == j, occupied[row * ROWS + j], rows)
    for pair in range(PAIRS):
        a = column * (2 * PAIRS) + 2 * pair
        energy = jnp.where(lane < TILE, virtual[a], virtual[a + 1]) + spectator
        out[pair * ROWS : (pair + 1) * ROWS, :] = energy - occupied[0] - rows


def last_kernel(denominator, parts, out):
    for pair in range(PAIRS):
        piece = pl.ds(pair * ROWS, ROWS)
        total = parts[0, piece, :]
        for place in range(1, ZH * Y):
            total = total + parts[place, piece, :]
        out[0, :, pair * LANES : (pair + 1) * LANES] = total / denominator[piece, :]


def call(kernel, shapes, specs, scratch=()):
    return pl.pallas_call(
        kernel,
        out_shape=[jax.ShapeDtypeStruct(shape, jnp.float32) for shape in shapes],
        in_specs=specs,
        out_specs=[VMEM] * len(shapes),
        scratch_shapes=[pltpu.VMEM(shape, jnp.float32) for shape in scratch],
        compiler_params=PARAMS,
    )


def per_device(amplitudes, cycle_block, ladder_block, occupied, virtual, tiles):
    swap = [(0, 1), (1, 0)]
    other = lax.ppermute(cycle_block, "core", swap)
    (copies,) = call(pack_kernel, [(ZL, BLOCK, LANES)], [VMEM])(amplitudes)
    column = lax.all_to_all(copies, "zl", 0, 0, tiled=True)
    copies = jnp.broadcast_to(column.reshape(1, ZL * BLOCK, LANES), (X, ZL * BLOCK, LANES))
    gathered = lax.all_to_all(copies, "x", 0, 0, tiled=True)
    gathered = gathered.reshape(CHIPS * BLOCK, LANES)
    (cycle,) = call(cycle_kernel, [(CHIPS * BLOCK, LANES)], [VMEM] * 3)(gathered, cycle_block, other)
    cycle, gathered = lax.optimization_barrier((cycle, gathered))
    cycle = lax.all_to_all(cycle.reshape(CHIPS, BLOCK, LANES), ("x", "zl"), 0, 0, tiled=True)

    (window,) = call(
        window_kernel,
        [(2, Y * 2 * ROWS, LANES)],
        [SMEM, VMEM],
        [(TILE // 2 * ROWS, LANES), (LANES, LANES), (LANES, LANES)],
    )(tiles, gathered)
    window = window.reshape(2, Y, 2 * ROWS, LANES)
    other_window = lax.ppermute(window, "core", swap)
    near, far = call(add_kernel, [(Y, 2 * ROWS, LANES)] * 2, [VMEM] * 2)(window, other_window)
    far = lax.ppermute(far, "zh", swap)
    (window,) = call(join_kernel, [(Y, 4 * ROWS, LANES)], [VMEM] * 2)(near, far)
    (denominator,) = call(denominator_kernel, [(BLOCK, LANES)], [SMEM] * 3)(
        tiles, occupied, virtual
    )
    window, denominator, cycle = lax.optimization_barrier((window, denominator, cycle))
    window = lax.all_to_all(window, "y", 0, 0, tiled=True)

    integrals = ladder_block.reshape(-1, ladder_block.shape[2])
    (parts,) = call(ladder_kernel, [(CHIPS, BLOCK, LANES)], [VMEM] * 3)(window, integrals, cycle)
    parts = lax.all_to_all(parts, ("zh", "y"), 0, 0, tiled=True)
    (result,) = call(last_kernel, [amplitudes.shape], [VMEM] * 2)(denominator, parts)
    return result


def solution(mesh):
    parts = Mesh(mesh.devices.reshape(ZL, X, CORE, ZH, Y), EVERY)
    amp, intg = ("zl", "x", "core"), ("zh", "y")
    return jax.shard_map(
        per_device,
        mesh=parts,
        in_specs=(P(None, intg, amp), P(intg, amp), P(intg, None, amp), P(), P(), P()),
        out_specs=P(None, intg, amp),
        check_vma=False,
    )
```

```python
import functools

import jax
import jax.numpy as jnp
from jax import lax
from jax.experimental import pallas as pl
from jax.experimental.pallas import tpu as pltpu
from jax.sharding import Mesh
from jax.sharding import PartitionSpec as P

ZL, X, CORE, ZH, YH, YL = 4, 4, 2, 2, 4, 2
Y = YH * YL
CHIPS = ZL * X
ROWS = 8
TILE = 64
PAIRS = 13
LANES = 2 * TILE
BLOCK = PAIRS * ROWS
EVERY = ("zl", "x", "core", "zh", "yh", "yl")
VMEM = pl.BlockSpec(memory_space=pltpu.VMEM)
SMEM = pl.BlockSpec(memory_space=pltpu.SMEM)
PARAMS = pltpu.CompilerParams(vmem_limit_bytes=32 * 1024 * 1024)


def split(value):
    high = value.astype(jnp.bfloat16)
    return high, (value - high.astype(jnp.float32)).astype(jnp.bfloat16)


def product(left, right):
    dot = functools.partial(jnp.dot, preferred_element_type=jnp.float32)
    return dot(left[0], right[1]) + dot(left[1], right[0]) + dot(left[0], right[0])


def low_half(shape):
    return lax.broadcasted_iota(jnp.int32, shape, 1) < TILE


def pair_up(first, second):
    low = low_half(first.shape)
    return (
        jnp.where(low, first, pltpu.roll(second, TILE, 1)),
        jnp.where(low, pltpu.roll(first, TILE, 1), second),
    )


def block_of(chip):
    return chip % X * ZL + chip // X


def peer_of(place):
    return place // Y * Y + place % YL * YH + place % Y // YL


def pack_kernel(amplitudes, out):
    for pair in range(PAIRS):
        tile = amplitudes[0, :, pair * LANES : (pair + 1) * LANES]
        for chip in range(ZL):
            out[chip, pair * ROWS : (pair + 1) * ROWS, :] = tile


def window_kernel(tiles, gathered, out, window, columns, turned):
    core, first = lax.axis_index("core"), lax.axis_index("zh") == 0
    for pair in range(TILE // 2):
        place = tiles[1] * (TILE // 2) + pair
        owner = place // PAIRS
        row = (block_of(owner // CORE) * PAIRS + (place - owner * PAIRS)) * ROWS
        tile = gathered[pl.ds(pl.multiple_of(row, ROWS), ROWS), :]
        window[pair * ROWS : (pair + 1) * ROWS, :] = jnp.where(owner % 2 == core, tile, 0.0)
    for half in range(ROWS // 2):
        for inner in range(2):
            both = window[pl.ds(half * 2 + inner, TILE // 2, stride=ROWS), :]
            columns[pl.ds(inner * TILE, TILE // 2, stride=2), :] = both
            columns[pl.ds(inner * TILE + 1, TILE // 2, stride=2), :] = pltpu.roll(both, TILE, 1)
        turned[...] = jnp.transpose(columns[...])
        for part in range(2):
            even = turned[pl.ds(2 * part, CHIPS, stride=4), :]
            odd = turned[pl.ds(2 * part + 1, CHIPS, stride=4), :]
            for inner, value in enumerate(pair_up(even, odd)):
                row = part * ROWS + half * 2 + inner
                rows = pl.ds(row, Y, stride=2 * ROWS)
                out[0, rows, :] = jnp.where(first, value[:Y], value[Y:])
                out[1, rows, :] = jnp.where(first, value[Y:], value[:Y])


def add_kernel(own, other, near, far):
    near[...] = own[0] + other[0]
    far[...] = own[1] + other[1]


def join_kernel(near, far, out):
    out[:, : 2 * ROWS, :] = near[...]
    out[:, 2 * ROWS :, :] = far[...]


def cycle_kernel(gathered, own, other, out):
    core = lax.axis_index("core")
    chunks = ([], [])
    for k in range(0, ROWS, 2):
        first = gathered[pl.ds(k, CHIPS * PAIRS, stride=ROWS), :]
        second = gathered[pl.ds(k + 1, CHIPS * PAIRS, stride=ROWS), :]
        for chunk, value in zip(chunks, pair_up(first, second)):
            chunk.append(value)
    left = split(jnp.concatenate([jnp.concatenate(chunk, 1) for chunk in chunks], 0))
    for side in range(2):
        right = split(jnp.where(core == side, own[...], other[...]))
        result = product(left, right)
        for quarter in range(2):
            both = result[:, quarter * LANES : (quarter + 1) * LANES]
            rows = pair_up(both[: CHIPS * PAIRS], both[CHIPS * PAIRS :])
            for inner, value in enumerate(rows):
                j = side * 4 + quarter * 2 + inner
                out[pl.ds(j, CHIPS * PAIRS, stride=ROWS), :] = value


def ladder_kernel(window, integrals, cycle, out):
    first = lax.axis_index("zh") == 0
    lefts = []
    for part in range(2):
        near, far = [
            window[:, start : start + ROWS, :].reshape(Y * ROWS, LANES)
            for start in (part * ROWS, (2 + part) * ROWS)
        ]
        halves = [jnp.where(first, near, far), jnp.where(first, far, near)]
        lefts.append(jnp.concatenate(halves, 0))
    left = split(jnp.concatenate(lefts, 1))
    width = PAIRS * LANES
    for start in range(0, width, 2 * LANES):
        stop = min(start + 2 * LANES, width)
        result = product(left, split(integrals[:, start:stop]))
        for column in range(start, stop, LANES):
            value = result[:, column - start : column - start + LANES]
            rows = pl.ds(column // LANES * ROWS, ROWS)
            for chip in range(CHIPS):
                part = value[chip * ROWS : (chip + 1) * ROWS]
                out[peer_of(chip), rows, :] = part + cycle[block_of(chip), rows, :]


def denominator_kernel(tiles, occupied, virtual, out):
    column = lax.axis_index("zl") * (X * CORE) + lax.axis_index("x") * CORE + lax.axis_index("core")
    row = lax.axis_index("zh") * Y + lax.axis_index("yh") * YL + lax.axis_index("yl")
    shape = (ROWS, LANES)
    lane = lax.broadcasted_iota(jnp.int32, shape, 1)
    line = lax.broadcasted_iota(jnp.int32, shape, 0)
    spectator = jnp.zeros(shape, jnp.float32)
    for b in range(TILE):
        spectator = jnp.where(lane % TILE == b, virtual[tiles[0] * TILE + b], spectator)
    rows = jnp.zeros(shape, jnp.float32)
    for j in range(ROWS):
        rows = jnp.where(line == j, occupied[row * ROWS + j], rows)
    for pair in range(PAIRS):
        a = column * (2 * PAIRS) + 2 * pair
        energy = jnp.where(lane < TILE, virtual[a], virtual[a + 1]) + spectator
        out[pair * ROWS : (pair + 1) * ROWS, :] = energy - occupied[0] - rows


def last_kernel(denominator, parts, out):
    for pair in range(PAIRS):
        piece = pl.ds(pair * ROWS, ROWS)
        total = parts[0, piece, :]
        for place in range(1, ZH * Y):
            total = total + parts[place, piece, :]
        out[0, :, pair * LANES : (pair + 1) * LANES] = total / denominator[piece, :]


def call(kernel, shapes, specs, scratch=()):
    return pl.pallas_call(
        kernel,
        out_shape=[jax.ShapeDtypeStruct(shape, jnp.float32) for shape in shapes],
        in_specs=specs,
        out_specs=[VMEM] * len(shapes),
        scratch_shapes=[pltpu.VMEM(shape, jnp.float32) for shape in scratch],
        compiler_params=PARAMS,
    )


def per_device(amplitudes, cycle_block, ladder_block, occupied, virtual, tiles):
    swap = [(0, 1), (1, 0)]
    other = lax.ppermute(cycle_block, "core", swap)
    (copies,) = call(pack_kernel, [(ZL, BLOCK, LANES)], [VMEM])(amplitudes)
    column = lax.all_to_all(copies, "zl", 0, 0, tiled=True)
    column, other = lax.optimization_barrier((column, other))
    copies = jnp.broadcast_to(column.reshape(1, ZL * BLOCK, LANES), (X, ZL * BLOCK, LANES))
    gathered = lax.all_to_all(copies, "x", 0, 0, tiled=True)
    gathered = gathered.reshape(CHIPS * BLOCK, LANES)
    (cycle,) = call(cycle_kernel, [(CHIPS * BLOCK, LANES)], [VMEM] * 3)(gathered, cycle_block, other)
    cycle, gathered = lax.optimization_barrier((cycle, gathered))
    cycle = lax.all_to_all(cycle.reshape(CHIPS, BLOCK, LANES), ("x", "zl"), 0, 0, tiled=True)

    (window,) = call(
        window_kernel,
        [(2, Y * 2 * ROWS, LANES)],
        [SMEM, VMEM],
        [(TILE // 2 * ROWS, LANES), (LANES, LANES), (LANES, LANES)],
    )(tiles, gathered)
    window = window.reshape(2, Y, 2 * ROWS, LANES)
    other_window = lax.ppermute(window, "core", swap)
    near, far = call(add_kernel, [(Y, 2 * ROWS, LANES)] * 2, [VMEM] * 2)(window, other_window)
    far = lax.ppermute(far, "zh", swap)
    (window,) = call(join_kernel, [(Y, 4 * ROWS, LANES)], [VMEM] * 2)(near, far)
    (denominator,) = call(denominator_kernel, [(BLOCK, LANES)], [SMEM] * 3)(
        tiles, occupied, virtual
    )
    window, denominator, cycle = lax.optimization_barrier((window, denominator, cycle))
    window = lax.all_to_all(window, ("yh", "yl"), 0, 0, tiled=True)

    integrals = ladder_block.reshape(-1, ladder_block.shape[2])
    (parts,) = call(ladder_kernel, [(CHIPS, BLOCK, LANES)], [VMEM] * 3)(window, integrals, cycle)
    parts = lax.all_to_all(parts, ("zh", "yl", "yh"), 0, 0, tiled=True)
    (result,) = call(last_kernel, [amplitudes.shape], [VMEM] * 2)(denominator, parts)
    return result


def solution(mesh):
    parts = Mesh(mesh.devices.reshape(ZL, X, CORE, ZH, YH, YL), EVERY)
    amp, intg = ("zl", "x", "core"), ("zh", "yh", "yl")
    return jax.shard_map(
        per_device,
        mesh=parts,
        in_specs=(P(None, intg, amp), P(intg, amp), P(intg, None, amp), P(), P(), P()),
        out_specs=P(None, intg, amp),
        check_vma=False,
    )
```

```python
import functools

import jax
import jax.numpy as jnp
from jax import lax
from jax.experimental import pallas as pl
from jax.experimental.pallas import tpu as pltpu
from jax.sharding import Mesh
from jax.sharding import PartitionSpec as P

ZL, X, CORE, ZH, Y = 4, 4, 2, 2, 8
CHIPS = ZL * X
ROWS = 8
TILE = 64
PAIRS = 13
LANES = 2 * TILE
BLOCK = PAIRS * ROWS
EVERY = ("zl", "x", "core", "zh", "y")
VMEM = pl.BlockSpec(memory_space=pltpu.VMEM)
SMEM = pl.BlockSpec(memory_space=pltpu.SMEM)
PARAMS = pltpu.CompilerParams(vmem_limit_bytes=32 * 1024 * 1024)


def split(value):
    high = value.astype(jnp.bfloat16)
    return high, (value - high.astype(jnp.float32)).astype(jnp.bfloat16)


def product(left, right):
    dot = functools.partial(jnp.dot, preferred_element_type=jnp.float32)
    return dot(left[0], right[1]) + dot(left[1], right[0]) + dot(left[0], right[0])


def low_half(shape):
    return lax.broadcasted_iota(jnp.int32, shape, 1) < TILE


def pair_up(first, second):
    low = low_half(first.shape)
    return (
        jnp.where(low, first, pltpu.roll(second, TILE, 1)),
        jnp.where(low, pltpu.roll(first, TILE, 1), second),
    )


def block_of(chip):
    return chip % X * ZL + chip // X


def pack_kernel(amplitudes, out):
    for pair in range(PAIRS):
        out[pair * ROWS : (pair + 1) * ROWS, :] = amplitudes[0, :, pair * LANES : (pair + 1) * LANES]


def spread_kernel(*blocks):
    out = blocks[-1]
    zl = lax.axis_index("zl")
    for back, block in enumerate(blocks[:-1]):
        start = pl.multiple_of((zl + ZL - back) % ZL * BLOCK, ROWS)
        value = block[...]
        for x in range(X):
            out[x, pl.ds(start, BLOCK), :] = value


def window_kernel(tiles, gathered, out, window, columns, turned):
    core, first = lax.axis_index("core"), lax.axis_index("zh") == 0
    for pair in range(TILE // 2):
        place = tiles[1] * (TILE // 2) + pair
        owner = place // PAIRS
        row = (block_of(owner // CORE) * PAIRS + (place - owner * PAIRS)) * ROWS
        tile = gathered[pl.ds(pl.multiple_of(row, ROWS), ROWS), :]
        window[pair * ROWS : (pair + 1) * ROWS, :] = jnp.where(owner % 2 == core, tile, 0.0)
    for half in range(ROWS // 2):
        for inner in range(2):
            both = window[pl.ds(half * 2 + inner, TILE // 2, stride=ROWS), :]
            columns[pl.ds(inner * TILE, TILE // 2, stride=2), :] = both
            columns[pl.ds(inner * TILE + 1, TILE // 2, stride=2), :] = pltpu.roll(both, TILE, 1)
        turned[...] = jnp.transpose(columns[...])
        for part in range(2):
            even = turned[pl.ds(2 * part, CHIPS, stride=4), :]
            odd = turned[pl.ds(2 * part + 1, CHIPS, stride=4), :]
            for inner, value in enumerate(pair_up(even, odd)):
                row = part * ROWS + half * 2 + inner
                rows = pl.ds(row, Y, stride=2 * ROWS)
                out[0, rows, :] = jnp.where(first, value[:Y], value[Y:])
                out[1, rows, :] = jnp.where(first, value[Y:], value[:Y])


def add_kernel(own, other, near, far):
    near[...] = own[0] + other[0]
    far[...] = own[1] + other[1]


def join_kernel(near, far, out):
    out[:, : 2 * ROWS, :] = near[...]
    out[:, 2 * ROWS :, :] = far[...]


def cycle_kernel(gathered, own, other, out):
    core = lax.axis_index("core")
    chunks = ([], [])
    for k in range(0, ROWS, 2):
        first = gathered[pl.ds(k, CHIPS * PAIRS, stride=ROWS), :]
        second = gathered[pl.ds(k + 1, CHIPS * PAIRS, stride=ROWS), :]
        for chunk, value in zip(chunks, pair_up(first, second)):
            chunk.append(value)
    left = split(jnp.concatenate([jnp.concatenate(chunk, 1) for chunk in chunks], 0))
    for side in range(2):
        right = split(jnp.where(core == side, own[...], other[...]))
        result = product(left, right)
        for quarter in range(2):
            both = result[:, quarter * LANES : (quarter + 1) * LANES]
            rows = pair_up(both[: CHIPS * PAIRS], both[CHIPS * PAIRS :])
            for inner, value in enumerate(rows):
                j = side * 4 + quarter * 2 + inner
                out[pl.ds(j, CHIPS * PAIRS, stride=ROWS), :] = value


def ladder_kernel(window, integrals, cycle, out):
    first = lax.axis_index("zh") == 0
    lefts = []
    for part in range(2):
        near, far = [
            window[:, start : start + ROWS, :].reshape(Y * ROWS, LANES)
            for start in (part * ROWS, (2 + part) * ROWS)
        ]
        halves = [jnp.where(first, near, far), jnp.where(first, far, near)]
        lefts.append(jnp.concatenate(halves, 0))
    left = split(jnp.concatenate(lefts, 1))
    width = PAIRS * LANES
    for start in range(0, width, 2 * LANES):
        stop = min(start + 2 * LANES, width)
        result = product(left, split(integrals[:, start:stop]))
        for column in range(start, stop, LANES):
            value = result[:, column - start : column - start + LANES]
            rows = pl.ds(column // LANES * ROWS, ROWS)
            for chip in range(CHIPS):
                part = value[chip * ROWS : (chip + 1) * ROWS]
                out[chip, rows, :] = part + cycle[block_of(chip), rows, :]


def denominator_kernel(tiles, occupied, virtual, out):
    column = lax.axis_index("zl") * (X * CORE) + lax.axis_index("x") * CORE + lax.axis_index("core")
    row = lax.axis_index("zh") * Y + lax.axis_index("y")
    shape = (ROWS, LANES)
    lane = lax.broadcasted_iota(jnp.int32, shape, 1)
    line = lax.broadcasted_iota(jnp.int32, shape, 0)
    spectator = jnp.zeros(shape, jnp.float32)
    for b in range(TILE):
        spectator = jnp.where(lane % TILE == b, virtual[tiles[0] * TILE + b], spectator)
    rows = jnp.zeros(shape, jnp.float32)
    for j in range(ROWS):
        rows = jnp.where(line == j, occupied[row * ROWS + j], rows)
    for pair in range(PAIRS):
        a = column * (2 * PAIRS) + 2 * pair
        energy = jnp.where(lane < TILE, virtual[a], virtual[a + 1]) + spectator
        out[pair * ROWS : (pair + 1) * ROWS, :] = energy - occupied[0] - rows


def last_kernel(denominator, parts, out):
    for pair in range(PAIRS):
        piece = pl.ds(pair * ROWS, ROWS)
        total = parts[0, piece, :]
        for place in range(1, ZH * Y):
            total = total + parts[place, piece, :]
        out[0, :, pair * LANES : (pair + 1) * LANES] = total / denominator[piece, :]


def call(kernel, shapes, specs, scratch=()):
    return pl.pallas_call(
        kernel,
        out_shape=[jax.ShapeDtypeStruct(shape, jnp.float32) for shape in shapes],
        in_specs=specs,
        out_specs=[VMEM] * len(shapes),
        scratch_shapes=[pltpu.VMEM(shape, jnp.float32) for shape in scratch],
        compiler_params=PARAMS,
    )


def per_device(amplitudes, cycle_block, ladder_block, occupied, virtual, tiles):
    swap = [(0, 1), (1, 0)]
    other = lax.ppermute(cycle_block, "core", swap)
    (packed,) = call(pack_kernel, [(BLOCK, LANES)], [VMEM])(amplitudes)
    blocks = [packed]
    for step in range(1, ZL):
        blocks.append(lax.ppermute(packed, "zl", [(i, (i + step) % ZL) for i in range(ZL)]))
    (copies,) = call(spread_kernel, [(X, ZL * BLOCK, LANES)], [VMEM] * ZL)(*blocks)
    gathered = lax.all_to_all(copies, "x", 0, 0, tiled=True)
    gathered = gathered.reshape(CHIPS * BLOCK, LANES)
    (cycle,) = call(cycle_kernel, [(CHIPS * BLOCK, LANES)], [VMEM] * 3)(gathered, cycle_block, other)
    cycle, gathered = lax.optimization_barrier((cycle, gathered))
    cycle = lax.all_to_all(cycle.reshape(CHIPS, BLOCK, LANES), ("x", "zl"), 0, 0, tiled=True)

    (window,) = call(
        window_kernel,
        [(2, Y * 2 * ROWS, LANES)],
        [SMEM, VMEM],
        [(TILE // 2 * ROWS, LANES), (LANES, LANES), (LANES, LANES)],
    )(tiles, gathered)
    window = window.reshape(2, Y, 2 * ROWS, LANES)
    other_window = lax.ppermute(window, "core", swap)
    near, far = call(add_kernel, [(Y, 2 * ROWS, LANES)] * 2, [VMEM] * 2)(window, other_window)
    far = lax.ppermute(far, "zh", swap)
    (window,) = call(join_kernel, [(Y, 4 * ROWS, LANES)], [VMEM] * 2)(near, far)
    (denominator,) = call(denominator_kernel, [(BLOCK, LANES)], [SMEM] * 3)(
        tiles, occupied, virtual
    )
    window, denominator, cycle = lax.optimization_barrier((window, denominator, cycle))
    window = lax.all_to_all(window, "y", 0, 0, tiled=True)

    integrals = ladder_block.reshape(-1, ladder_block.shape[2])
    (parts,) = call(ladder_kernel, [(CHIPS, BLOCK, LANES)], [VMEM] * 3)(window, integrals, cycle)
    parts = lax.all_to_all(parts, ("zh", "y"), 0, 0, tiled=True)
    (result,) = call(last_kernel, [amplitudes.shape], [VMEM] * 2)(denominator, parts)
    return result


def solution(mesh):
    parts = Mesh(mesh.devices.reshape(ZL, X, CORE, ZH, Y), EVERY)
    amp, intg = ("zl", "x", "core"), ("zh", "y")
    return jax.shard_map(
        per_device,
        mesh=parts,
        in_specs=(P(None, intg, amp), P(intg, amp), P(intg, None, amp), P(), P(), P()),
        out_specs=P(None, intg, amp),
        check_vma=False,
    )
```

```python
import functools

import jax
import jax.numpy as jnp
from jax import lax
from jax.experimental import pallas as pl
from jax.experimental.pallas import tpu as pltpu
from jax.sharding import Mesh
from jax.sharding import PartitionSpec as P

ZL, X, CORE, ZH, Y = 4, 4, 2, 2, 8
CHIPS = ZL * X
ROWS = 8
TILE = 64
PAIRS = 13
LANES = 2 * TILE
BLOCK = PAIRS * ROWS
EVERY = ("zl", "x", "core", "zh", "y")
VMEM = pl.BlockSpec(memory_space=pltpu.VMEM)
SMEM = pl.BlockSpec(memory_space=pltpu.SMEM)
PARAMS = pltpu.CompilerParams(vmem_limit_bytes=32 * 1024 * 1024)


def split(value):
    high = value.astype(jnp.bfloat16)
    return high, (value - high.astype(jnp.float32)).astype(jnp.bfloat16)


def product(left, right):
    dot = functools.partial(jnp.dot, preferred_element_type=jnp.float32)
    return dot(left[0], right[1]) + dot(left[1], right[0]) + dot(left[0], right[0])


def low_half(shape):
    return lax.broadcasted_iota(jnp.int32, shape, 1) < TILE


def pair_up(first, second):
    low = low_half(first.shape)
    return (
        jnp.where(low, first, pltpu.roll(second, TILE, 1)),
        jnp.where(low, pltpu.roll(first, TILE, 1), second),
    )


def block_of(chip):
    return chip % X * ZL + chip // X


def pack_kernel(amplitudes, out):
    for pair in range(PAIRS):
        tile = amplitudes[0, :, pair * LANES : (pair + 1) * LANES]
        for chip in range(ZL):
            out[chip, pair * ROWS : (pair + 1) * ROWS, :] = tile


def window_kernel(tiles, gathered, out, window, columns, turned):
    core, first = lax.axis_index("core"), lax.axis_index("zh") == 0
    for pair in range(TILE // 2):
        place = tiles[1] * (TILE // 2) + pair
        owner = place // PAIRS
        row = (block_of(owner // CORE) * PAIRS + (place - owner * PAIRS)) * ROWS
        tile = gathered[pl.ds(pl.multiple_of(row, ROWS), ROWS), :]
        window[pair * ROWS : (pair + 1) * ROWS, :] = jnp.where(owner % 2 == core, tile, 0.0)
    for half in range(ROWS // 2):
        for inner in range(2):
            both = window[pl.ds(half * 2 + inner, TILE // 2, stride=ROWS), :]
            columns[pl.ds(inner * TILE, TILE // 2, stride=2), :] = both
            columns[pl.ds(inner * TILE + 1, TILE // 2, stride=2), :] = pltpu.roll(both, TILE, 1)
        turned[...] = jnp.transpose(columns[...])
        for part in range(2):
            even = turned[pl.ds(2 * part, CHIPS, stride=4), :]
            odd = turned[pl.ds(2 * part + 1, CHIPS, stride=4), :]
            for inner, value in enumerate(pair_up(even, odd)):
                row = part * ROWS + half * 2 + inner
                rows = pl.ds(row, Y, stride=2 * ROWS)
                out[0, rows, :] = jnp.where(first, value[:Y], value[Y:])
                out[1, rows, :] = jnp.where(first, value[Y:], value[:Y])


def add_kernel(own, other, near, far):
    core = lax.axis_index("core")
    near[...] = own[0] + other[0]
    total = own[1] + other[1]
    far[...] = jnp.where(core == 0, total[:, :ROWS], total[:, ROWS:])


def join_kernel(near, mine, theirs, out):
    core = lax.axis_index("core")
    out[:, : 2 * ROWS, :] = near[...]
    out[:, 2 * ROWS : 3 * ROWS, :] = jnp.where(core == 0, mine[...], theirs[...])
    out[:, 3 * ROWS :, :] = jnp.where(core == 0, theirs[...], mine[...])


def cycle_kernel(gathered, own, other, out):
    core = lax.axis_index("core")
    chunks = ([], [])
    for k in range(0, ROWS, 2):
        first = gathered[pl.ds(k, CHIPS * PAIRS, stride=ROWS), :]
        second = gathered[pl.ds(k + 1, CHIPS * PAIRS, stride=ROWS), :]
        for chunk, value in zip(chunks, pair_up(first, second)):
            chunk.append(value)
    left = split(jnp.concatenate([jnp.concatenate(chunk, 1) for chunk in chunks], 0))
    for side in range(2):
        right = split(jnp.where(core == side, own[...], other[...]))
        result = product(left, right)
        for quarter in range(2):
            both = result[:, quarter * LANES : (quarter + 1) * LANES]
            rows = pair_up(both[: CHIPS * PAIRS], both[CHIPS * PAIRS :])
            for inner, value in enumerate(rows):
                j = side * 4 + quarter * 2 + inner
                out[pl.ds(j, CHIPS * PAIRS, stride=ROWS), :] = value


def ladder_kernel(window, integrals, cycle, out):
    first = lax.axis_index("zh") == 0
    lefts = []
    for part in range(2):
        near, far = [
            window[:, start : start + ROWS, :].reshape(Y * ROWS, LANES)
            for start in (part * ROWS, (2 + part) * ROWS)
        ]
        halves = [jnp.where(first, near, far), jnp.where(first, far, near)]
        lefts.append(jnp.concatenate(halves, 0))
    left = split(jnp.concatenate(lefts, 1))
    width = PAIRS * LANES
    for start in range(0, width, 2 * LANES):
        stop = min(start + 2 * LANES, width)
        result = product(left, split(integrals[:, start:stop]))
        for column in range(start, stop, LANES):
            value = result[:, column - start : column - start + LANES]
            rows = pl.ds(column // LANES * ROWS, ROWS)
            for chip in range(CHIPS):
                part = value[chip * ROWS : (chip + 1) * ROWS]
                out[chip, rows, :] = part + cycle[block_of(chip), rows, :]


def denominator_kernel(tiles, occupied, virtual, out):
    column = lax.axis_index("zl") * (X * CORE) + lax.axis_index("x") * CORE + lax.axis_index("core")
    row = lax.axis_index("zh") * Y + lax.axis_index("y")
    shape = (ROWS, LANES)
    lane = lax.broadcasted_iota(jnp.int32, shape, 1)
    line = lax.broadcasted_iota(jnp.int32, shape, 0)
    spectator = jnp.zeros(shape, jnp.float32)
    for b in range(TILE):
        spectator = jnp.where(lane % TILE == b, virtual[tiles[0] * TILE + b], spectator)
    rows = jnp.zeros(shape, jnp.float32)
    for j in range(ROWS):
        rows = jnp.where(line == j, occupied[row * ROWS + j], rows)
    for pair in range(PAIRS):
        a = column * (2 * PAIRS) + 2 * pair
        energy = jnp.where(lane < TILE, virtual[a], virtual[a + 1]) + spectator
        out[pair * ROWS : (pair + 1) * ROWS, :] = energy - occupied[0] - rows


def last_kernel(denominator, parts, out):
    for pair in range(PAIRS):
        piece = pl.ds(pair * ROWS, ROWS)
        total = parts[0, piece, :]
        for place in range(1, ZH * Y):
            total = total + parts[place, piece, :]
        out[0, :, pair * LANES : (pair + 1) * LANES] = total / denominator[piece, :]


def call(kernel, shapes, specs, scratch=()):
    return pl.pallas_call(
        kernel,
        out_shape=[jax.ShapeDtypeStruct(shape, jnp.float32) for shape in shapes],
        in_specs=specs,
        out_specs=[VMEM] * len(shapes),
        scratch_shapes=[pltpu.VMEM(shape, jnp.float32) for shape in scratch],
        compiler_params=PARAMS,
    )


def per_device(amplitudes, cycle_block, ladder_block, occupied, virtual, tiles):
    swap = [(0, 1), (1, 0)]
    other = lax.ppermute(cycle_block, "core", swap)
    (copies,) = call(pack_kernel, [(ZL, BLOCK, LANES)], [VMEM])(amplitudes)
    column = lax.all_to_all(copies, "zl", 0, 0, tiled=True)
    copies = jnp.broadcast_to(column.reshape(1, ZL * BLOCK, LANES), (X, ZL * BLOCK, LANES))
    gathered = lax.all_to_all(copies, "x", 0, 0, tiled=True)
    gathered = gathered.reshape(CHIPS * BLOCK, LANES)
    (cycle,) = call(cycle_kernel, [(CHIPS * BLOCK, LANES)], [VMEM] * 3)(gathered, cycle_block, other)
    cycle, gathered = lax.optimization_barrier((cycle, gathered))
    cycle = lax.all_to_all(cycle.reshape(CHIPS, BLOCK, LANES), ("x", "zl"), 0, 0, tiled=True)

    (window,) = call(
        window_kernel,
        [(2, Y * 2 * ROWS, LANES)],
        [SMEM, VMEM],
        [(TILE // 2 * ROWS, LANES), (LANES, LANES), (LANES, LANES)],
    )(tiles, gathered)
    window = window.reshape(2, Y, 2 * ROWS, LANES)
    other_window = lax.ppermute(window, "core", swap)
    near, far = call(
        add_kernel, [(Y, 2 * ROWS, LANES), (Y, ROWS, LANES)], [VMEM] * 2
    )(window, other_window)
    mine = lax.ppermute(far, "zh", swap)
    theirs = lax.ppermute(mine, "core", swap)
    (window,) = call(join_kernel, [(Y, 4 * ROWS, LANES)], [VMEM] * 3)(near, mine, theirs)
    (denominator,) = call(denominator_kernel, [(BLOCK, LANES)], [SMEM] * 3)(
        tiles, occupied, virtual
    )
    window, denominator, cycle = lax.optimization_barrier((window, denominator, cycle))
    window = lax.all_to_all(window, "y", 0, 0, tiled=True)

    integrals = ladder_block.reshape(-1, ladder_block.shape[2])
    (parts,) = call(ladder_kernel, [(CHIPS, BLOCK, LANES)], [VMEM] * 3)(window, integrals, cycle)
    parts = lax.all_to_all(parts, ("zh", "y"), 0, 0, tiled=True)
    (result,) = call(last_kernel, [amplitudes.shape], [VMEM] * 2)(denominator, parts)
    return result


def solution(mesh):
    parts = Mesh(mesh.devices.reshape(ZL, X, CORE, ZH, Y), EVERY)
    amp, intg = ("zl", "x", "core"), ("zh", "y")
    return jax.shard_map(
        per_device,
        mesh=parts,
        in_specs=(P(None, intg, amp), P(intg, amp), P(intg, None, amp), P(), P(), P()),
        out_specs=P(None, intg, amp),
        check_vma=False,
    )
```

```python
import functools

import jax
import jax.numpy as jnp
from jax import lax
from jax.experimental import pallas as pl
from jax.experimental.pallas import tpu as pltpu
from jax.sharding import Mesh
from jax.sharding import PartitionSpec as P

ZL, X, CORE, ZH, Y = 4, 4, 2, 2, 8
CHIPS = ZL * X
ROWS = 8
TILE = 64
PAIRS = 13
LANES = 2 * TILE
BLOCK = PAIRS * ROWS
EVERY = ("zl", "x", "core", "zh", "y")
VMEM = pl.BlockSpec(memory_space=pltpu.VMEM)
SMEM = pl.BlockSpec(memory_space=pltpu.SMEM)
PARAMS = pltpu.CompilerParams(vmem_limit_bytes=32 * 1024 * 1024)


def split(value):
    high = value.astype(jnp.bfloat16)
    return high, (value - high.astype(jnp.float32)).astype(jnp.bfloat16)


def product(left, right):
    dot = functools.partial(jnp.dot, preferred_element_type=jnp.float32)
    return dot(left[0], right[1]) + dot(left[1], right[0]) + dot(left[0], right[0])


def low_half(shape):
    return lax.broadcasted_iota(jnp.int32, shape, 1) < TILE


def pair_up(first, second):
    low = low_half(first.shape)
    return (
        jnp.where(low, first, pltpu.roll(second, TILE, 1)),
        jnp.where(low, pltpu.roll(first, TILE, 1), second),
    )


def block_of(chip):
    return chip % X * ZL + chip // X


def pack_kernel(amplitudes, out):
    for pair in range(PAIRS):
        tile = amplitudes[0, :, pair * LANES : (pair + 1) * LANES]
        for chip in range(ZL):
            out[chip, pair * ROWS : (pair + 1) * ROWS, :] = tile


def window_kernel(tiles, gathered, out, window, columns, turned):
    core, first = lax.axis_index("core"), lax.axis_index("zh") == 0
    for pair in range(TILE // 2):
        place = tiles[1] * (TILE // 2) + pair
        owner = place // PAIRS
        row = (block_of(owner // CORE) * PAIRS + (place - owner * PAIRS)) * ROWS
        tile = gathered[pl.ds(pl.multiple_of(row, ROWS), ROWS), :]
        window[pair * ROWS : (pair + 1) * ROWS, :] = jnp.where(owner % 2 == core, tile, 0.0)
    for half in range(ROWS // 2):
        for inner in range(2):
            both = window[pl.ds(half * 2 + inner, TILE // 2, stride=ROWS), :]
            columns[pl.ds(inner * TILE, TILE // 2, stride=2), :] = both
            columns[pl.ds(inner * TILE + 1, TILE // 2, stride=2), :] = pltpu.roll(both, TILE, 1)
        turned[...] = jnp.transpose(columns[...])
        for part in range(2):
            even = turned[pl.ds(2 * part, CHIPS, stride=4), :]
            odd = turned[pl.ds(2 * part + 1, CHIPS, stride=4), :]
            for inner, value in enumerate(pair_up(even, odd)):
                row = part * ROWS + half * 2 + inner
                rows = pl.ds(row, Y, stride=2 * ROWS)
                out[0, rows, :] = jnp.where(first, value[:Y], value[Y:])
                out[1, rows, :] = jnp.where(first, value[Y:], value[:Y])


def add_kernel(own, other, near, far):
    core = lax.axis_index("core")
    near[...] = own[0] + other[0]
    total = own[1] + other[1]
    far[...] = jnp.where(core == 0, total[:, :ROWS], total[:, ROWS:])


def join_kernel(near, mine, theirs, out):
    core = lax.axis_index("core")
    out[:, : 2 * ROWS, :] = near[...]
    out[:, 2 * ROWS : 3 * ROWS, :] = jnp.where(core == 0, mine[...], theirs[...])
    out[:, 3 * ROWS :, :] = jnp.where(core == 0, theirs[...], mine[...])


def prepare_kernel(own, other, high, low):
    core = lax.axis_index("core")
    for side in range(2):
        columns = slice(side * own.shape[1], (side + 1) * own.shape[1])
        high[:, columns], low[:, columns] = split(jnp.where(core == side, own[...], other[...]))


def cycle_kernel(gathered, high, low, out, staged, done):
    span = CHIPS // 2 * BLOCK
    rows = CHIPS // 2 * PAIRS
    copies = []
    for half in range(2):
        chunks = ([], [])
        for k in range(0, ROWS, 2):
            first = gathered[pl.ds(half * span + k, rows, stride=ROWS), :]
            second = gathered[pl.ds(half * span + k + 1, rows, stride=ROWS), :]
            for chunk, value in zip(chunks, pair_up(first, second)):
                chunk.append(value)
        left = split(jnp.concatenate([jnp.concatenate(chunk, 1) for chunk in chunks], 0))
        for pair in range(0, ROWS // 2, 2):
            columns = slice(pair * LANES, (pair + 2) * LANES)
            result = product(left, (high[:, columns], low[:, columns]))
            for quarter in range(2):
                both = result[:, quarter * LANES : (quarter + 1) * LANES]
                for inner, value in enumerate(pair_up(both[:rows], both[rows:])):
                    j = (pair + quarter) * 2 + inner
                    staged[pl.ds(half * span + j, rows, stride=ROWS), :] = value
        piece = pl.ds(half * span, span)
        copies.append(pltpu.make_async_copy(staged.at[piece], out.at[piece], done.at[half]))
        copies[-1].start()
    for copy in copies:
        copy.wait()


def ladder_kernel(window, integrals, cycle, out):
    first = lax.axis_index("zh") == 0
    lefts = []
    for part in range(2):
        near, far = [
            window[:, start : start + ROWS, :].reshape(Y * ROWS, LANES)
            for start in (part * ROWS, (2 + part) * ROWS)
        ]
        halves = [jnp.where(first, near, far), jnp.where(first, far, near)]
        lefts.append(jnp.concatenate(halves, 0))
    left = split(jnp.concatenate(lefts, 1))
    width = PAIRS * LANES
    for start in range(0, width, 2 * LANES):
        stop = min(start + 2 * LANES, width)
        result = product(left, split(integrals[:, start:stop]))
        for column in range(start, stop, LANES):
            value = result[:, column - start : column - start + LANES]
            rows = pl.ds(column // LANES * ROWS, ROWS)
            for chip in range(CHIPS):
                part = value[chip * ROWS : (chip + 1) * ROWS]
                out[chip, rows, :] = part + cycle[block_of(chip), rows, :]


def denominator_kernel(tiles, occupied, virtual, out):
    column = lax.axis_index("zl") * (X * CORE) + lax.axis_index("x") * CORE + lax.axis_index("core")
    row = lax.axis_index("zh") * Y + lax.axis_index("y")
    shape = (ROWS, LANES)
    lane = lax.broadcasted_iota(jnp.int32, shape, 1)
    line = lax.broadcasted_iota(jnp.int32, shape, 0)
    spectator = jnp.zeros(shape, jnp.float32)
    for b in range(TILE):
        spectator = jnp.where(lane % TILE == b, virtual[tiles[0] * TILE + b], spectator)
    rows = jnp.zeros(shape, jnp.float32)
    for j in range(ROWS):
        rows = jnp.where(line == j, occupied[row * ROWS + j], rows)
    for pair in range(PAIRS):
        a = column * (2 * PAIRS) + 2 * pair
        energy = jnp.where(lane < TILE, virtual[a], virtual[a + 1]) + spectator
        out[pair * ROWS : (pair + 1) * ROWS, :] = energy - occupied[0] - rows


def last_kernel(denominator, parts, out):
    for pair in range(PAIRS):
        piece = pl.ds(pair * ROWS, ROWS)
        total = parts[0, piece, :]
        for place in range(1, ZH * Y):
            total = total + parts[place, piece, :]
        out[0, :, pair * LANES : (pair + 1) * LANES] = total / denominator[piece, :]


def call(kernel, shapes, specs, scratch=()):
    return pl.pallas_call(
        kernel,
        out_shape=[jax.ShapeDtypeStruct(shape, jnp.float32) for shape in shapes],
        in_specs=specs,
        out_specs=[VMEM] * len(shapes),
        scratch_shapes=[pltpu.VMEM(shape, jnp.float32) for shape in scratch],
        compiler_params=PARAMS,
    )


def per_device(amplitudes, cycle_block, ladder_block, occupied, virtual, tiles):
    swap = [(0, 1), (1, 0)]
    other = lax.ppermute(cycle_block, "core", swap)
    (copies,) = call(pack_kernel, [(ZL, BLOCK, LANES)], [VMEM])(amplitudes)
    column = lax.all_to_all(copies, "zl", 0, 0, tiled=True)
    copies = jnp.broadcast_to(column.reshape(1, ZL * BLOCK, LANES), (X, ZL * BLOCK, LANES))
    gathered = lax.all_to_all(copies, "x", 0, 0, tiled=True)
    gathered = gathered.reshape(CHIPS * BLOCK, LANES)
    halves = jax.ShapeDtypeStruct((cycle_block.shape[0], 2 * cycle_block.shape[1]), jnp.bfloat16)
    high, low = pl.pallas_call(
        prepare_kernel,
        out_shape=[halves] * 2,
        in_specs=[VMEM] * 2,
        out_specs=[VMEM] * 2,
        compiler_params=PARAMS,
    )(cycle_block, other)
    cycle = pl.pallas_call(
        cycle_kernel,
        out_shape=jax.ShapeDtypeStruct((CHIPS * BLOCK, LANES), jnp.float32),
        in_specs=[VMEM] * 3,
        out_specs=pl.BlockSpec(memory_space=pl.ANY),
        scratch_shapes=[
            pltpu.VMEM((CHIPS * BLOCK, LANES), jnp.float32),
            pltpu.SemaphoreType.DMA((2,)),
        ],
        compiler_params=PARAMS,
    )(gathered, high, low)
    cycle, gathered = lax.optimization_barrier((cycle, gathered))
    cycle = lax.all_to_all(cycle.reshape(CHIPS, BLOCK, LANES), ("x", "zl"), 0, 0, tiled=True)

    (window,) = call(
        window_kernel,
        [(2, Y * 2 * ROWS, LANES)],
        [SMEM, VMEM],
        [(TILE // 2 * ROWS, LANES), (LANES, LANES), (LANES, LANES)],
    )(tiles, gathered)
    window = window.reshape(2, Y, 2 * ROWS, LANES)
    other_window = lax.ppermute(window, "core", swap)
    near, far = call(
        add_kernel, [(Y, 2 * ROWS, LANES), (Y, ROWS, LANES)], [VMEM] * 2
    )(window, other_window)
    mine = lax.ppermute(far, "zh", swap)
    theirs = lax.ppermute(mine, "core", swap)
    (window,) = call(join_kernel, [(Y, 4 * ROWS, LANES)], [VMEM] * 3)(near, mine, theirs)
    (denominator,) = call(denominator_kernel, [(BLOCK, LANES)], [SMEM] * 3)(
        tiles, occupied, virtual
    )
    window, denominator, cycle = lax.optimization_barrier((window, denominator, cycle))
    window = lax.all_to_all(window, "y", 0, 0, tiled=True)

    integrals = ladder_block.reshape(-1, ladder_block.shape[2])
    (parts,) = call(ladder_kernel, [(CHIPS, BLOCK, LANES)], [VMEM] * 3)(window, integrals, cycle)
    parts = lax.all_to_all(parts, ("zh", "y"), 0, 0, tiled=True)
    (result,) = call(last_kernel, [amplitudes.shape], [VMEM] * 2)(denominator, parts)
    return result


def solution(mesh):
    parts = Mesh(mesh.devices.reshape(ZL, X, CORE, ZH, Y), EVERY)
    amp, intg = ("zl", "x", "core"), ("zh", "y")
    return jax.shard_map(
        per_device,
        mesh=parts,
        in_specs=(P(None, intg, amp), P(intg, amp), P(intg, None, amp), P(), P(), P()),
        out_specs=P(None, intg, amp),
        check_vma=False,
    )
```

```python
import functools

import jax
import jax.numpy as jnp
from jax import lax
from jax.experimental import pallas as pl
from jax.experimental.pallas import tpu as pltpu
from jax.sharding import Mesh
from jax.sharding import PartitionSpec as P

ZL, X, CORE, ZH, Y = 4, 4, 2, 2, 8
CHIPS = ZL * X
ROWS = 8
TILE = 64
PAIRS = 13
LANES = 2 * TILE
BLOCK = PAIRS * ROWS
EVERY = ("zl", "x", "core", "zh", "y")
VMEM = pl.BlockSpec(memory_space=pltpu.VMEM)
SMEM = pl.BlockSpec(memory_space=pltpu.SMEM)
PARAMS = pltpu.CompilerParams(vmem_limit_bytes=32 * 1024 * 1024)


def split(value):
    high = value.astype(jnp.bfloat16)
    return high, (value - high.astype(jnp.float32)).astype(jnp.bfloat16)


def product(left, right):
    dot = functools.partial(jnp.dot, preferred_element_type=jnp.float32)
    return dot(left[0], right[1]) + dot(left[1], right[0]) + dot(left[0], right[0])


def low_half(shape):
    return lax.broadcasted_iota(jnp.int32, shape, 1) < TILE


def pair_up(first, second):
    low = low_half(first.shape)
    return (
        jnp.where(low, first, pltpu.roll(second, TILE, 1)),
        jnp.where(low, pltpu.roll(first, TILE, 1), second),
    )


def block_of(chip):
    return chip % X * ZL + chip // X


def spread_kernel(column, out):
    for zl in range(ZL):
        for pair in range(PAIRS):
            tile = column[zl, :, pair * LANES : (pair + 1) * LANES]
            start = zl * BLOCK + pair * ROWS
            for x in range(X):
                out[x, start : start + ROWS, :] = tile


def window_kernel(tiles, gathered, out, window, columns, turned):
    core, first = lax.axis_index("core"), lax.axis_index("zh") == 0
    for pair in range(TILE // 2):
        place = tiles[1] * (TILE // 2) + pair
        owner = place // PAIRS
        row = (block_of(owner // CORE) * PAIRS + (place - owner * PAIRS)) * ROWS
        tile = gathered[pl.ds(pl.multiple_of(row, ROWS), ROWS), :]
        window[pair * ROWS : (pair + 1) * ROWS, :] = jnp.where(owner % 2 == core, tile, 0.0)
    for half in range(ROWS // 2):
        for inner in range(2):
            both = window[pl.ds(half * 2 + inner, TILE // 2, stride=ROWS), :]
            columns[pl.ds(inner * TILE, TILE // 2, stride=2), :] = both
            columns[pl.ds(inner * TILE + 1, TILE // 2, stride=2), :] = pltpu.roll(both, TILE, 1)
        turned[...] = jnp.transpose(columns[...])
        for part in range(2):
            even = turned[pl.ds(2 * part, CHIPS, stride=4), :]
            odd = turned[pl.ds(2 * part + 1, CHIPS, stride=4), :]
            for inner, value in enumerate(pair_up(even, odd)):
                row = part * ROWS + half * 2 + inner
                rows = pl.ds(row, Y, stride=2 * ROWS)
                out[0, rows, :] = jnp.where(first, value[:Y], value[Y:])
                out[1, rows, :] = jnp.where(first, value[Y:], value[:Y])


def add_kernel(own, other, near, far):
    core = lax.axis_index("core")
    near[...] = own[0] + other[0]
    total = own[1] + other[1]
    far[...] = jnp.where(core == 0, total[:, :ROWS], total[:, ROWS:])


def join_kernel(near, mine, theirs, out):
    core = lax.axis_index("core")
    out[:, : 2 * ROWS, :] = near[...]
    out[:, 2 * ROWS : 3 * ROWS, :] = jnp.where(core == 0, mine[...], theirs[...])
    out[:, 3 * ROWS :, :] = jnp.where(core == 0, theirs[...], mine[...])


def prepare_kernel(own, other, high, low):
    core = lax.axis_index("core")
    for side in range(2):
        columns = slice(side * own.shape[1], (side + 1) * own.shape[1])
        high[:, columns], low[:, columns] = split(jnp.where(core == side, own[...], other[...]))


def cycle_kernel(gathered, high, low, out, staged, done):
    span = CHIPS // 2 * BLOCK
    rows = CHIPS // 2 * PAIRS
    copies = []
    for half in range(2):
        chunks = ([], [])
        for k in range(0, ROWS, 2):
            first = gathered[pl.ds(half * span + k, rows, stride=ROWS), :]
            second = gathered[pl.ds(half * span + k + 1, rows, stride=ROWS), :]
            for chunk, value in zip(chunks, pair_up(first, second)):
                chunk.append(value)
        left = split(jnp.concatenate([jnp.concatenate(chunk, 1) for chunk in chunks], 0))
        for pair in range(0, ROWS // 2, 2):
            columns = slice(pair * LANES, (pair + 2) * LANES)
            result = product(left, (high[:, columns], low[:, columns]))
            for quarter in range(2):
                both = result[:, quarter * LANES : (quarter + 1) * LANES]
                for inner, value in enumerate(pair_up(both[:rows], both[rows:])):
                    j = (pair + quarter) * 2 + inner
                    staged[pl.ds(half * span + j, rows, stride=ROWS), :] = value
        piece = pl.ds(half * span, span)
        copies.append(pltpu.make_async_copy(staged.at[piece], out.at[piece], done.at[half]))
        copies[-1].start()
    for copy in copies:
        copy.wait()


def ladder_kernel(window, integrals, cycle, out):
    first = lax.axis_index("zh") == 0
    lefts = []
    for part in range(2):
        near, far = [
            window[:, start : start + ROWS, :].reshape(Y * ROWS, LANES)
            for start in (part * ROWS, (2 + part) * ROWS)
        ]
        halves = [jnp.where(first, near, far), jnp.where(first, far, near)]
        lefts.append(jnp.concatenate(halves, 0))
    left = split(jnp.concatenate(lefts, 1))
    width = PAIRS * LANES
    for start in range(0, width, 2 * LANES):
        stop = min(start + 2 * LANES, width)
        result = product(left, split(integrals[:, start:stop]))
        for column in range(start, stop, LANES):
            value = result[:, column - start : column - start + LANES]
            rows = pl.ds(column // LANES * ROWS, ROWS)
            for chip in range(CHIPS):
                part = value[chip * ROWS : (chip + 1) * ROWS]
                out[chip, rows, :] = part + cycle[block_of(chip), rows, :]


def denominator_kernel(tiles, occupied, virtual, out):
    column = lax.axis_index("zl") * (X * CORE) + lax.axis_index("x") * CORE + lax.axis_index("core")
    row = lax.axis_index("zh") * Y + lax.axis_index("y")
    shape = (ROWS, LANES)
    lane = lax.broadcasted_iota(jnp.int32, shape, 1)
    line = lax.broadcasted_iota(jnp.int32, shape, 0)
    spectator = jnp.zeros(shape, jnp.float32)
    for b in range(TILE):
        spectator = jnp.where(lane % TILE == b, virtual[tiles[0] * TILE + b], spectator)
    rows = jnp.zeros(shape, jnp.float32)
    for j in range(ROWS):
        rows = jnp.where(line == j, occupied[row * ROWS + j], rows)
    for pair in range(PAIRS):
        a = column * (2 * PAIRS) + 2 * pair
        energy = jnp.where(lane < TILE, virtual[a], virtual[a + 1]) + spectator
        out[pair * ROWS : (pair + 1) * ROWS, :] = energy - occupied[0] - rows


def last_kernel(denominator, parts, out):
    for pair in range(PAIRS):
        piece = pl.ds(pair * ROWS, ROWS)
        total = parts[0, piece, :]
        for place in range(1, ZH * Y):
            total = total + parts[place, piece, :]
        out[0, :, pair * LANES : (pair + 1) * LANES] = total / denominator[piece, :]


def call(kernel, shapes, specs, scratch=()):
    return pl.pallas_call(
        kernel,
        out_shape=[jax.ShapeDtypeStruct(shape, jnp.float32) for shape in shapes],
        in_specs=specs,
        out_specs=[VMEM] * len(shapes),
        scratch_shapes=[pltpu.VMEM(shape, jnp.float32) for shape in scratch],
        compiler_params=PARAMS,
    )


def per_device(amplitudes, cycle_block, ladder_block, occupied, virtual, tiles):
    swap = [(0, 1), (1, 0)]
    other = lax.ppermute(cycle_block, "core", swap)
    copies = jnp.broadcast_to(amplitudes, (ZL,) + amplitudes.shape[1:])
    column = lax.all_to_all(copies, "zl", 0, 0, tiled=True)
    (copies,) = call(spread_kernel, [(X, ZL * BLOCK, LANES)], [VMEM])(column)
    gathered = lax.all_to_all(copies, "x", 0, 0, tiled=True)
    gathered = gathered.reshape(CHIPS * BLOCK, LANES)
    halves = jax.ShapeDtypeStruct((cycle_block.shape[0], 2 * cycle_block.shape[1]), jnp.bfloat16)
    high, low = pl.pallas_call(
        prepare_kernel,
        out_shape=[halves] * 2,
        in_specs=[VMEM] * 2,
        out_specs=[VMEM] * 2,
        compiler_params=PARAMS,
    )(cycle_block, other)
    cycle = pl.pallas_call(
        cycle_kernel,
        out_shape=jax.ShapeDtypeStruct((CHIPS * BLOCK, LANES), jnp.float32),
        in_specs=[VMEM] * 3,
        out_specs=pl.BlockSpec(memory_space=pl.ANY),
        scratch_shapes=[
            pltpu.VMEM((CHIPS * BLOCK, LANES), jnp.float32),
            pltpu.SemaphoreType.DMA((2,)),
        ],
        compiler_params=PARAMS,
    )(gathered, high, low)
    cycle, gathered = lax.optimization_barrier((cycle, gathered))
    cycle = lax.all_to_all(cycle.reshape(CHIPS, BLOCK, LANES), ("x", "zl"), 0, 0, tiled=True)

    (window,) = call(
        window_kernel,
        [(2, Y * 2 * ROWS, LANES)],
        [SMEM, VMEM],
        [(TILE // 2 * ROWS, LANES), (LANES, LANES), (LANES, LANES)],
    )(tiles, gathered)
    window = window.reshape(2, Y, 2 * ROWS, LANES)
    other_window = lax.ppermute(window, "core", swap)
    near, far = call(
        add_kernel, [(Y, 2 * ROWS, LANES), (Y, ROWS, LANES)], [VMEM] * 2
    )(window, other_window)
    mine = lax.ppermute(far, "zh", swap)
    theirs = lax.ppermute(mine, "core", swap)
    (window,) = call(join_kernel, [(Y, 4 * ROWS, LANES)], [VMEM] * 3)(near, mine, theirs)
    (denominator,) = call(denominator_kernel, [(BLOCK, LANES)], [SMEM] * 3)(
        tiles, occupied, virtual
    )
    window, denominator, cycle = lax.optimization_barrier((window, denominator, cycle))
    window = lax.all_to_all(window, "y", 0, 0, tiled=True)

    integrals = ladder_block.reshape(-1, ladder_block.shape[2])
    (parts,) = call(ladder_kernel, [(CHIPS, BLOCK, LANES)], [VMEM] * 3)(window, integrals, cycle)
    parts = lax.all_to_all(parts, ("zh", "y"), 0, 0, tiled=True)
    (result,) = call(last_kernel, [amplitudes.shape], [VMEM] * 2)(denominator, parts)
    return result


def solution(mesh):
    parts = Mesh(mesh.devices.reshape(ZL, X, CORE, ZH, Y), EVERY)
    amp, intg = ("zl", "x", "core"), ("zh", "y")
    return jax.shard_map(
        per_device,
        mesh=parts,
        in_specs=(P(None, intg, amp), P(intg, amp), P(intg, None, amp), P(), P(), P()),
        out_specs=P(None, intg, amp),
        check_vma=False,
    )
```

```python
import functools

import jax
import jax.numpy as jnp
from jax import lax
from jax.experimental import pallas as pl
from jax.experimental.pallas import tpu as pltpu
from jax.sharding import Mesh
from jax.sharding import PartitionSpec as P

ZL, X, CORE, ZH, YH, YL = 4, 4, 2, 2, 4, 2
Y = YH * YL
CHIPS = ZL * X
ROWS = 8
TILE = 64
PAIRS = 13
LANES = 2 * TILE
BLOCK = PAIRS * ROWS
EVERY = ("zl", "x", "core", "zh", "yh", "yl")
VMEM = pl.BlockSpec(memory_space=pltpu.VMEM)
SMEM = pl.BlockSpec(memory_space=pltpu.SMEM)
PARAMS = pltpu.CompilerParams(vmem_limit_bytes=32 * 1024 * 1024)


def split(value):
    high = value.astype(jnp.bfloat16)
    return high, (value - high.astype(jnp.float32)).astype(jnp.bfloat16)


def product(left, right):
    dot = functools.partial(jnp.dot, preferred_element_type=jnp.float32)
    return dot(left[0], right[1]) + dot(left[1], right[0]) + dot(left[0], right[0])


def low_half(shape):
    return lax.broadcasted_iota(jnp.int32, shape, 1) < TILE


def pair_up(first, second):
    low = low_half(first.shape)
    return (
        jnp.where(low, first, pltpu.roll(second, TILE, 1)),
        jnp.where(low, pltpu.roll(first, TILE, 1), second),
    )


def block_of(chip):
    return chip % X * ZL + chip // X


def peer_of(place):
    return place // Y * Y + place % YL * YH + place % Y // YL


def pack_kernel(amplitudes, out):
    for pair in range(PAIRS):
        tile = amplitudes[0, :, pair * LANES : (pair + 1) * LANES]
        for chip in range(ZL):
            out[chip, pair * ROWS : (pair + 1) * ROWS, :] = tile


def window_kernel(tiles, gathered, out, window, columns, turned):
    core, first = lax.axis_index("core"), lax.axis_index("zh") == 0
    for pair in range(TILE // 2):
        place = tiles[1] * (TILE // 2) + pair
        owner = place // PAIRS
        row = (block_of(owner // CORE) * PAIRS + (place - owner * PAIRS)) * ROWS
        tile = gathered[pl.ds(pl.multiple_of(row, ROWS), ROWS), :]
        window[pair * ROWS : (pair + 1) * ROWS, :] = jnp.where(owner % 2 == core, tile, 0.0)
    for half in range(ROWS // 2):
        for inner in range(2):
            both = window[pl.ds(half * 2 + inner, TILE // 2, stride=ROWS), :]
            columns[pl.ds(inner * TILE, TILE // 2, stride=2), :] = both
            columns[pl.ds(inner * TILE + 1, TILE // 2, stride=2), :] = pltpu.roll(both, TILE, 1)
        turned[...] = jnp.transpose(columns[...])
        for part in range(2):
            even = turned[pl.ds(2 * part, CHIPS, stride=4), :]
            odd = turned[pl.ds(2 * part + 1, CHIPS, stride=4), :]
            for inner, value in enumerate(pair_up(even, odd)):
                row = part * ROWS + half * 2 + inner
                rows = pl.ds(row, Y, stride=2 * ROWS)
                out[0, rows, :] = jnp.where(first, value[:Y], value[Y:])
                out[1, rows, :] = jnp.where(first, value[Y:], value[:Y])


def add_kernel(own, other, near, far):
    core = lax.axis_index("core")
    near[...] = own[0] + other[0]
    total = own[1] + other[1]
    far[...] = jnp.where(core == 0, total[:, :ROWS], total[:, ROWS:])


def join_kernel(near, mine, theirs, out):
    core = lax.axis_index("core")
    out[:, : 2 * ROWS, :] = near[...]
    out[:, 2 * ROWS : 3 * ROWS, :] = jnp.where(core == 0, mine[...], theirs[...])
    out[:, 3 * ROWS :, :] = jnp.where(core == 0, theirs[...], mine[...])


def prepare_kernel(own, other, high, low):
    core = lax.axis_index("core")
    for side in range(2):
        columns = slice(side * own.shape[1], (side + 1) * own.shape[1])
        high[:, columns], low[:, columns] = split(jnp.where(core == side, own[...], other[...]))


def cycle_kernel(gathered, high, low, out, staged, done):
    span = CHIPS // 2 * BLOCK
    rows = CHIPS // 2 * PAIRS
    copies = []
    for half in range(2):
        chunks = ([], [])
        for k in range(0, ROWS, 2):
            first = gathered[pl.ds(half * span + k, rows, stride=ROWS), :]
            second = gathered[pl.ds(half * span + k + 1, rows, stride=ROWS), :]
            for chunk, value in zip(chunks, pair_up(first, second)):
                chunk.append(value)
        left = split(jnp.concatenate([jnp.concatenate(chunk, 1) for chunk in chunks], 0))
        for pair in range(0, ROWS // 2, 2):
            columns = slice(pair * LANES, (pair + 2) * LANES)
            result = product(left, (high[:, columns], low[:, columns]))
            for quarter in range(2):
                both = result[:, quarter * LANES : (quarter + 1) * LANES]
                for inner, value in enumerate(pair_up(both[:rows], both[rows:])):
                    j = (pair + quarter) * 2 + inner
                    staged[pl.ds(half * span + j, rows, stride=ROWS), :] = value
        piece = pl.ds(half * span, span)
        copies.append(pltpu.make_async_copy(staged.at[piece], out.at[piece], done.at[half]))
        copies[-1].start()
    for copy in copies:
        copy.wait()


def ladder_kernel(window, integrals, cycle, out):
    first = lax.axis_index("zh") == 0
    lefts = []
    for part in range(2):
        near, far = [
            window[:, start : start + ROWS, :].reshape(Y * ROWS, LANES)
            for start in (part * ROWS, (2 + part) * ROWS)
        ]
        halves = [jnp.where(first, near, far), jnp.where(first, far, near)]
        lefts.append(jnp.concatenate(halves, 0))
    left = split(jnp.concatenate(lefts, 1))
    width = PAIRS * LANES
    for start in range(0, width, 2 * LANES):
        stop = min(start + 2 * LANES, width)
        result = product(left, split(integrals[:, start:stop]))
        for column in range(start, stop, LANES):
            value = result[:, column - start : column - start + LANES]
            rows = pl.ds(column // LANES * ROWS, ROWS)
            for chip in range(CHIPS):
                part = value[chip * ROWS : (chip + 1) * ROWS]
                out[peer_of(chip), rows, :] = part + cycle[block_of(chip), rows, :]


def denominator_kernel(tiles, occupied, virtual, out):
    column = lax.axis_index("zl") * (X * CORE) + lax.axis_index("x") * CORE + lax.axis_index("core")
    row = lax.axis_index("zh") * Y + lax.axis_index("yh") * YL + lax.axis_index("yl")
    shape = (ROWS, LANES)
    lane = lax.broadcasted_iota(jnp.int32, shape, 1)
    line = lax.broadcasted_iota(jnp.int32, shape, 0)
    spectator = jnp.zeros(shape, jnp.float32)
    for b in range(TILE):
        spectator = jnp.where(lane % TILE == b, virtual[tiles[0] * TILE + b], spectator)
    rows = jnp.zeros(shape, jnp.float32)
    for j in range(ROWS):
        rows = jnp.where(line == j, occupied[row * ROWS + j], rows)
    for pair in range(PAIRS):
        a = column * (2 * PAIRS) + 2 * pair
        energy = jnp.where(lane < TILE, virtual[a], virtual[a + 1]) + spectator
        out[pair * ROWS : (pair + 1) * ROWS, :] = energy - occupied[0] - rows


def last_kernel(denominator, parts, out):
    for pair in range(PAIRS):
        piece = pl.ds(pair * ROWS, ROWS)
        total = parts[0, piece, :]
        for place in range(1, ZH * Y):
            total = total + parts[place, piece, :]
        out[0, :, pair * LANES : (pair + 1) * LANES] = total / denominator[piece, :]


def call(kernel, shapes, specs, scratch=()):
    return pl.pallas_call(
        kernel,
        out_shape=[jax.ShapeDtypeStruct(shape, jnp.float32) for shape in shapes],
        in_specs=specs,
        out_specs=[VMEM] * len(shapes),
        scratch_shapes=[pltpu.VMEM(shape, jnp.float32) for shape in scratch],
        compiler_params=PARAMS,
    )


def per_device(amplitudes, cycle_block, ladder_block, occupied, virtual, tiles):
    swap = [(0, 1), (1, 0)]
    other = lax.ppermute(cycle_block, "core", swap)
    (copies,) = call(pack_kernel, [(ZL, BLOCK, LANES)], [VMEM])(amplitudes)
    column = lax.all_to_all(copies, "zl", 0, 0, tiled=True)
    copies = jnp.broadcast_to(column.reshape(1, ZL * BLOCK, LANES), (X, ZL * BLOCK, LANES))
    gathered = lax.all_to_all(copies, "x", 0, 0, tiled=True)
    gathered = gathered.reshape(CHIPS * BLOCK, LANES)
    halves = jax.ShapeDtypeStruct((cycle_block.shape[0], 2 * cycle_block.shape[1]), jnp.bfloat16)
    high, low = pl.pallas_call(
        prepare_kernel,
        out_shape=[halves] * 2,
        in_specs=[VMEM] * 2,
        out_specs=[VMEM] * 2,
        compiler_params=PARAMS,
    )(cycle_block, other)
    cycle = pl.pallas_call(
        cycle_kernel,
        out_shape=jax.ShapeDtypeStruct((CHIPS * BLOCK, LANES), jnp.float32),
        in_specs=[VMEM] * 3,
        out_specs=pl.BlockSpec(memory_space=pl.ANY),
        scratch_shapes=[
            pltpu.VMEM((CHIPS * BLOCK, LANES), jnp.float32),
            pltpu.SemaphoreType.DMA((2,)),
        ],
        compiler_params=PARAMS,
    )(gathered, high, low)
    cycle, gathered = lax.optimization_barrier((cycle, gathered))
    cycle = lax.all_to_all(cycle.reshape(CHIPS, BLOCK, LANES), ("x", "zl"), 0, 0, tiled=True)

    (window,) = call(
        window_kernel,
        [(2, Y * 2 * ROWS, LANES)],
        [SMEM, VMEM],
        [(TILE // 2 * ROWS, LANES), (LANES, LANES), (LANES, LANES)],
    )(tiles, gathered)
    window = window.reshape(2, Y, 2 * ROWS, LANES)
    other_window = lax.ppermute(window, "core", swap)
    near, far = call(
        add_kernel, [(Y, 2 * ROWS, LANES), (Y, ROWS, LANES)], [VMEM] * 2
    )(window, other_window)
    mine = lax.ppermute(far, "zh", swap)
    theirs = lax.ppermute(mine, "core", swap)
    (window,) = call(join_kernel, [(Y, 4 * ROWS, LANES)], [VMEM] * 3)(near, mine, theirs)
    (denominator,) = call(denominator_kernel, [(BLOCK, LANES)], [SMEM] * 3)(
        tiles, occupied, virtual
    )
    window, denominator, cycle = lax.optimization_barrier((window, denominator, cycle))
    window = lax.all_to_all(window, ("yh", "yl"), 0, 0, tiled=True)

    integrals = ladder_block.reshape(-1, ladder_block.shape[2])
    (parts,) = call(ladder_kernel, [(CHIPS, BLOCK, LANES)], [VMEM] * 3)(window, integrals, cycle)
    parts = lax.all_to_all(parts, ("zh", "yl", "yh"), 0, 0, tiled=True)
    (result,) = call(last_kernel, [amplitudes.shape], [VMEM] * 2)(denominator, parts)
    return result


def solution(mesh):
    parts = Mesh(mesh.devices.reshape(ZL, X, CORE, ZH, YH, YL), EVERY)
    amp, intg = ("zl", "x", "core"), ("zh", "yh", "yl")
    return jax.shard_map(
        per_device,
        mesh=parts,
        in_specs=(P(None, intg, amp), P(intg, amp), P(intg, None, amp), P(), P(), P()),
        out_specs=P(None, intg, amp),
        check_vma=False,
    )
```

```python
import functools

import jax
import jax.numpy as jnp
from jax import lax
from jax.experimental import pallas as pl
from jax.experimental.pallas import tpu as pltpu
from jax.sharding import Mesh
from jax.sharding import PartitionSpec as P

ZL, X, CORE, ZH, YH, YL = 4, 4, 2, 2, 4, 2
Y = YH * YL
CHIPS = ZL * X
ROWS = 8
TILE = 64
PAIRS = 13
LANES = 2 * TILE
BLOCK = PAIRS * ROWS
EVERY = ("zl", "x", "core", "zh", "yh", "yl")
VMEM = pl.BlockSpec(memory_space=pltpu.VMEM)
SMEM = pl.BlockSpec(memory_space=pltpu.SMEM)
PARAMS = pltpu.CompilerParams(vmem_limit_bytes=32 * 1024 * 1024)


def split(value):
    high = value.astype(jnp.bfloat16)
    return high, (value - high.astype(jnp.float32)).astype(jnp.bfloat16)


def product(left, right):
    dot = functools.partial(jnp.dot, preferred_element_type=jnp.float32)
    return dot(left[0], right[1]) + dot(left[1], right[0]) + dot(left[0], right[0])


def low_half(shape):
    return lax.broadcasted_iota(jnp.int32, shape, 1) < TILE


def pair_up(first, second):
    low = low_half(first.shape)
    return (
        jnp.where(low, first, pltpu.roll(second, TILE, 1)),
        jnp.where(low, pltpu.roll(first, TILE, 1), second),
    )


def block_of(chip):
    return chip % X * ZL + chip // X


def peer_of(place):
    return (place % YL * YH + place % Y // YL) * ZH + place // Y


def pack_kernel(amplitudes, out):
    for pair in range(PAIRS):
        tile = amplitudes[0, :, pair * LANES : (pair + 1) * LANES]
        for chip in range(ZL):
            out[chip, pair * ROWS : (pair + 1) * ROWS, :] = tile


def window_kernel(tiles, gathered, out, window, columns, turned):
    core, first = lax.axis_index("core"), lax.axis_index("zh") == 0
    for pair in range(TILE // 2):
        place = tiles[1] * (TILE // 2) + pair
        owner = place // PAIRS
        row = (block_of(owner // CORE) * PAIRS + (place - owner * PAIRS)) * ROWS
        tile = gathered[pl.ds(pl.multiple_of(row, ROWS), ROWS), :]
        window[pair * ROWS : (pair + 1) * ROWS, :] = jnp.where(owner % 2 == core, tile, 0.0)
    for half in range(ROWS // 2):
        for inner in range(2):
            both = window[pl.ds(half * 2 + inner, TILE // 2, stride=ROWS), :]
            columns[pl.ds(inner * TILE, TILE // 2, stride=2), :] = both
            columns[pl.ds(inner * TILE + 1, TILE // 2, stride=2), :] = pltpu.roll(both, TILE, 1)
        turned[...] = jnp.transpose(columns[...])
        for part in range(2):
            even = turned[pl.ds(2 * part, CHIPS, stride=4), :]
            odd = turned[pl.ds(2 * part + 1, CHIPS, stride=4), :]
            for inner, value in enumerate(pair_up(even, odd)):
                row = part * ROWS + half * 2 + inner
                rows = pl.ds(row, Y, stride=2 * ROWS)
                out[0, rows, :] = jnp.where(first, value[:Y], value[Y:])
                out[1, rows, :] = jnp.where(first, value[Y:], value[:Y])


def add_kernel(own, other, near, far):
    core = lax.axis_index("core")
    near[...] = own[0] + other[0]
    total = own[1] + other[1]
    far[...] = jnp.where(core == 0, total[:, :ROWS], total[:, ROWS:])


def join_kernel(near, mine, theirs, out):
    core = lax.axis_index("core")
    out[:, : 2 * ROWS, :] = near[...]
    out[:, 2 * ROWS : 3 * ROWS, :] = jnp.where(core == 0, mine[...], theirs[...])
    out[:, 3 * ROWS :, :] = jnp.where(core == 0, theirs[...], mine[...])


def prepare_kernel(own, other, high, low):
    core = lax.axis_index("core")
    for side in range(2):
        columns = slice(side * own.shape[1], (side + 1) * own.shape[1])
        high[:, columns], low[:, columns] = split(jnp.where(core == side, own[...], other[...]))


def cycle_kernel(gathered, high, low, out, staged, done):
    span = CHIPS // 2 * BLOCK
    rows = CHIPS // 2 * PAIRS
    copies = []
    for half in range(2):
        chunks = ([], [])
        for k in range(0, ROWS, 2):
            first = gathered[pl.ds(half * span + k, rows, stride=ROWS), :]
            second = gathered[pl.ds(half * span + k + 1, rows, stride=ROWS), :]
            for chunk, value in zip(chunks, pair_up(first, second)):
                chunk.append(value)
        left = split(jnp.concatenate([jnp.concatenate(chunk, 1) for chunk in chunks], 0))
        for pair in range(0, ROWS // 2, 2):
            columns = slice(pair * LANES, (pair + 2) * LANES)
            result = product(left, (high[:, columns], low[:, columns]))
            for quarter in range(2):
                both = result[:, quarter * LANES : (quarter + 1) * LANES]
                for inner, value in enumerate(pair_up(both[:rows], both[rows:])):
                    j = (pair + quarter) * 2 + inner
                    staged[pl.ds(half * span + j, rows, stride=ROWS), :] = value
        piece = pl.ds(half * span, span)
        copies.append(pltpu.make_async_copy(staged.at[piece], out.at[piece], done.at[half]))
        copies[-1].start()
    for copy in copies:
        copy.wait()


def ladder_kernel(window, integrals, cycle, out):
    first = lax.axis_index("zh") == 0
    lefts = []
    for part in range(2):
        near, far = [
            window[:, start : start + ROWS, :].reshape(Y * ROWS, LANES)
            for start in (part * ROWS, (2 + part) * ROWS)
        ]
        halves = [jnp.where(first, near, far), jnp.where(first, far, near)]
        lefts.append(jnp.concatenate(halves, 0))
    left = split(jnp.concatenate(lefts, 1))
    width = PAIRS * LANES
    for start in range(0, width, 2 * LANES):
        stop = min(start + 2 * LANES, width)
        result = product(left, split(integrals[:, start:stop]))
        for column in range(start, stop, LANES):
            value = result[:, column - start : column - start + LANES]
            rows = pl.ds(column // LANES * ROWS, ROWS)
            for chip in range(CHIPS):
                part = value[chip * ROWS : (chip + 1) * ROWS]
                out[peer_of(chip), rows, :] = part + cycle[block_of(chip), rows, :]


def denominator_kernel(tiles, occupied, virtual, out):
    column = lax.axis_index("zl") * (X * CORE) + lax.axis_index("x") * CORE + lax.axis_index("core")
    row = lax.axis_index("zh") * Y + lax.axis_index("yh") * YL + lax.axis_index("yl")
    shape = (ROWS, LANES)
    lane = lax.broadcasted_iota(jnp.int32, shape, 1)
    line = lax.broadcasted_iota(jnp.int32, shape, 0)
    spectator = jnp.zeros(shape, jnp.float32)
    for b in range(TILE):
        spectator = jnp.where(lane % TILE == b, virtual[tiles[0] * TILE + b], spectator)
    rows = jnp.zeros(shape, jnp.float32)
    for j in range(ROWS):
        rows = jnp.where(line == j, occupied[row * ROWS + j], rows)
    for pair in range(PAIRS):
        a = column * (2 * PAIRS) + 2 * pair
        energy = jnp.where(lane < TILE, virtual[a], virtual[a + 1]) + spectator
        out[pair * ROWS : (pair + 1) * ROWS, :] = energy - occupied[0] - rows


def last_kernel(denominator, parts, out):
    for pair in range(PAIRS):
        piece = pl.ds(pair * ROWS, ROWS)
        total = parts[0, piece, :]
        for place in range(1, ZH * Y):
            total = total + parts[place, piece, :]
        out[0, :, pair * LANES : (pair + 1) * LANES] = total / denominator[piece, :]


def call(kernel, shapes, specs, scratch=()):
    return pl.pallas_call(
        kernel,
        out_shape=[jax.ShapeDtypeStruct(shape, jnp.float32) for shape in shapes],
        in_specs=specs,
        out_specs=[VMEM] * len(shapes),
        scratch_shapes=[pltpu.VMEM(shape, jnp.float32) for shape in scratch],
        compiler_params=PARAMS,
    )


def per_device(amplitudes, cycle_block, ladder_block, occupied, virtual, tiles):
    swap = [(0, 1), (1, 0)]
    other = lax.ppermute(cycle_block, "core", swap)
    (copies,) = call(pack_kernel, [(ZL, BLOCK, LANES)], [VMEM])(amplitudes)
    column = lax.all_to_all(copies, "zl", 0, 0, tiled=True)
    copies = jnp.broadcast_to(column.reshape(1, ZL * BLOCK, LANES), (X, ZL * BLOCK, LANES))
    gathered = lax.all_to_all(copies, "x", 0, 0, tiled=True)
    gathered = gathered.reshape(CHIPS * BLOCK, LANES)
    halves = jax.ShapeDtypeStruct((cycle_block.shape[0], 2 * cycle_block.shape[1]), jnp.bfloat16)
    high, low = pl.pallas_call(
        prepare_kernel,
        out_shape=[halves] * 2,
        in_specs=[VMEM] * 2,
        out_specs=[VMEM] * 2,
        compiler_params=PARAMS,
    )(cycle_block, other)
    cycle = pl.pallas_call(
        cycle_kernel,
        out_shape=jax.ShapeDtypeStruct((CHIPS * BLOCK, LANES), jnp.float32),
        in_specs=[VMEM] * 3,
        out_specs=pl.BlockSpec(memory_space=pl.ANY),
        scratch_shapes=[
            pltpu.VMEM((CHIPS * BLOCK, LANES), jnp.float32),
            pltpu.SemaphoreType.DMA((2,)),
        ],
        compiler_params=PARAMS,
    )(gathered, high, low)
    cycle, gathered = lax.optimization_barrier((cycle, gathered))
    cycle = lax.all_to_all(cycle.reshape(CHIPS, BLOCK, LANES), ("x", "zl"), 0, 0, tiled=True)

    (window,) = call(
        window_kernel,
        [(2, Y * 2 * ROWS, LANES)],
        [SMEM, VMEM],
        [(TILE // 2 * ROWS, LANES), (LANES, LANES), (LANES, LANES)],
    )(tiles, gathered)
    window = window.reshape(2, Y, 2 * ROWS, LANES)
    other_window = lax.ppermute(window, "core", swap)
    near, far = call(
        add_kernel, [(Y, 2 * ROWS, LANES), (Y, ROWS, LANES)], [VMEM] * 2
    )(window, other_window)
    mine = lax.ppermute(far, "zh", swap)
    theirs = lax.ppermute(mine, "core", swap)
    (window,) = call(join_kernel, [(Y, 4 * ROWS, LANES)], [VMEM] * 3)(near, mine, theirs)
    (denominator,) = call(denominator_kernel, [(BLOCK, LANES)], [SMEM] * 3)(
        tiles, occupied, virtual
    )
    window, denominator, cycle = lax.optimization_barrier((window, denominator, cycle))
    window = lax.all_to_all(window, ("yh", "yl"), 0, 0, tiled=True)

    integrals = ladder_block.reshape(-1, ladder_block.shape[2])
    (parts,) = call(ladder_kernel, [(CHIPS, BLOCK, LANES)], [VMEM] * 3)(window, integrals, cycle)
    parts = lax.all_to_all(parts, ("yl", "yh", "zh"), 0, 0, tiled=True)
    (result,) = call(last_kernel, [amplitudes.shape], [VMEM] * 2)(denominator, parts)
    return result


def solution(mesh):
    parts = Mesh(mesh.devices.reshape(ZL, X, CORE, ZH, YH, YL), EVERY)
    amp, intg = ("zl", "x", "core"), ("zh", "yh", "yl")
    return jax.shard_map(
        per_device,
        mesh=parts,
        in_specs=(P(None, intg, amp), P(intg, amp), P(intg, None, amp), P(), P(), P()),
        out_specs=P(None, intg, amp),
        check_vma=False,
    )
```

```python
import functools

import jax
import jax.numpy as jnp
from jax import lax
from jax.experimental import pallas as pl
from jax.experimental.pallas import tpu as pltpu
from jax.sharding import Mesh
from jax.sharding import PartitionSpec as P

ZL, X, CORE, ZH, YH, YL = 4, 4, 2, 2, 4, 2
Y = YH * YL
CHIPS = ZL * X
ROWS = 8
TILE = 64
PAIRS = 13
LANES = 2 * TILE
BLOCK = PAIRS * ROWS
EVERY = ("zl", "x", "core", "zh", "yh", "yl")
VMEM = pl.BlockSpec(memory_space=pltpu.VMEM)
SMEM = pl.BlockSpec(memory_space=pltpu.SMEM)
PARAMS = pltpu.CompilerParams(vmem_limit_bytes=32 * 1024 * 1024)


def split(value):
    high = value.astype(jnp.bfloat16)
    return high, (value - high.astype(jnp.float32)).astype(jnp.bfloat16)


def product(left, right):
    dot = functools.partial(jnp.dot, preferred_element_type=jnp.float32)
    return dot(left[0], right[1]) + dot(left[1], right[0]) + dot(left[0], right[0])


def low_half(shape):
    return lax.broadcasted_iota(jnp.int32, shape, 1) < TILE


def pair_up(first, second):
    low = low_half(first.shape)
    return (
        jnp.where(low, first, pltpu.roll(second, TILE, 1)),
        jnp.where(low, pltpu.roll(first, TILE, 1), second),
    )


def block_of(chip):
    return chip % X * ZL + chip // X


def peer_of(place):
    return place // Y * Y + place % YL * YH + place % Y // YL


def pack_kernel(amplitudes, out):
    for pair in range(PAIRS):
        tile = amplitudes[0, :, pair * LANES : (pair + 1) * LANES]
        for chip in range(ZL):
            out[chip, pair * ROWS : (pair + 1) * ROWS, :] = tile


def window_kernel(tiles, gathered, out, window, columns, turned):
    core, first = lax.axis_index("core"), lax.axis_index("zh") == 0
    for pair in range(TILE // 2):
        place = tiles[1] * (TILE // 2) + pair
        owner = place // PAIRS
        row = (block_of(owner // CORE) * PAIRS + (place - owner * PAIRS)) * ROWS
        tile = gathered[pl.ds(pl.multiple_of(row, ROWS), ROWS), :]
        window[pair * ROWS : (pair + 1) * ROWS, :] = jnp.where(owner % 2 == core, tile, 0.0)
    for half in range(ROWS // 2):
        for inner in range(2):
            both = window[pl.ds(half * 2 + inner, TILE // 2, stride=ROWS), :]
            columns[pl.ds(inner * TILE, TILE // 2, stride=2), :] = both
            columns[pl.ds(inner * TILE + 1, TILE // 2, stride=2), :] = pltpu.roll(both, TILE, 1)
        turned[...] = jnp.transpose(columns[...])
        for part in range(2):
            even = turned[pl.ds(2 * part, CHIPS, stride=4), :]
            odd = turned[pl.ds(2 * part + 1, CHIPS, stride=4), :]
            for inner, value in enumerate(pair_up(even, odd)):
                row = part * ROWS + half * 2 + inner
                rows = pl.ds(row, Y, stride=2 * ROWS)
                out[0, rows, :] = jnp.where(first, value[:Y], value[Y:])
                out[1, rows, :] = jnp.where(first, value[Y:], value[:Y])


def add_kernel(own, other, near, far):
    core = lax.axis_index("core")
    near[...] = own[0] + other[0]
    total = own[1] + other[1]
    far[...] = jnp.where(core == 0, total[:, :ROWS], total[:, ROWS:])


def join_kernel(near, mine, theirs, out):
    core = lax.axis_index("core")
    for y in range(Y):
        out[peer_of(y), : 2 * ROWS, :] = near[y]
        out[peer_of(y), 2 * ROWS : 3 * ROWS, :] = jnp.where(core == 0, mine[y], theirs[y])
        out[peer_of(y), 3 * ROWS :, :] = jnp.where(core == 0, theirs[y], mine[y])


def prepare_kernel(own, other, high, low):
    core = lax.axis_index("core")
    for side in range(2):
        columns = slice(side * own.shape[1], (side + 1) * own.shape[1])
        high[:, columns], low[:, columns] = split(jnp.where(core == side, own[...], other[...]))


def cycle_kernel(gathered, high, low, out, staged, done):
    span = CHIPS // 2 * BLOCK
    rows = CHIPS // 2 * PAIRS
    copies = []
    for half in range(2):
        chunks = ([], [])
        for k in range(0, ROWS, 2):
            first = gathered[pl.ds(half * span + k, rows, stride=ROWS), :]
            second = gathered[pl.ds(half * span + k + 1, rows, stride=ROWS), :]
            for chunk, value in zip(chunks, pair_up(first, second)):
                chunk.append(value)
        left = split(jnp.concatenate([jnp.concatenate(chunk, 1) for chunk in chunks], 0))
        for pair in range(0, ROWS // 2, 2):
            columns = slice(pair * LANES, (pair + 2) * LANES)
            result = product(left, (high[:, columns], low[:, columns]))
            for quarter in range(2):
                both = result[:, quarter * LANES : (quarter + 1) * LANES]
                for inner, value in enumerate(pair_up(both[:rows], both[rows:])):
                    j = (pair + quarter) * 2 + inner
                    staged[pl.ds(half * span + j, rows, stride=ROWS), :] = value
        piece = pl.ds(half * span, span)
        copies.append(pltpu.make_async_copy(staged.at[piece], out.at[piece], done.at[half]))
        copies[-1].start()
    for copy in copies:
        copy.wait()


def ladder_kernel(window, integrals, cycle, out):
    first = lax.axis_index("zh") == 0
    lefts = []
    for part in range(2):
        near, far = [
            jnp.concatenate([window[peer_of(y), start : start + ROWS, :] for y in range(Y)], 0)
            for start in (part * ROWS, (2 + part) * ROWS)
        ]
        halves = [jnp.where(first, near, far), jnp.where(first, far, near)]
        lefts.append(jnp.concatenate(halves, 0))
    left = split(jnp.concatenate(lefts, 1))
    width = PAIRS * LANES
    for start in range(0, width, 2 * LANES):
        stop = min(start + 2 * LANES, width)
        result = product(left, split(integrals[:, start:stop]))
        for column in range(start, stop, LANES):
            value = result[:, column - start : column - start + LANES]
            rows = pl.ds(column // LANES * ROWS, ROWS)
            for chip in range(CHIPS):
                part = value[chip * ROWS : (chip + 1) * ROWS]
                out[peer_of(chip), rows, :] = part + cycle[block_of(chip), rows, :]


def denominator_kernel(tiles, occupied, virtual, out):
    column = lax.axis_index("zl") * (X * CORE) + lax.axis_index("x") * CORE + lax.axis_index("core")
    row = lax.axis_index("zh") * Y + lax.axis_index("yh") * YL + lax.axis_index("yl")
    shape = (ROWS, LANES)
    lane = lax.broadcasted_iota(jnp.int32, shape, 1)
    line = lax.broadcasted_iota(jnp.int32, shape, 0)
    spectator = jnp.zeros(shape, jnp.float32)
    for b in range(TILE):
        spectator = jnp.where(lane % TILE == b, virtual[tiles[0] * TILE + b], spectator)
    rows = jnp.zeros(shape, jnp.float32)
    for j in range(ROWS):
        rows = jnp.where(line == j, occupied[row * ROWS + j], rows)
    for pair in range(PAIRS):
        a = column * (2 * PAIRS) + 2 * pair
        energy = jnp.where(lane < TILE, virtual[a], virtual[a + 1]) + spectator
        out[pair * ROWS : (pair + 1) * ROWS, :] = energy - occupied[0] - rows


def last_kernel(denominator, parts, out):
    for pair in range(PAIRS):
        piece = pl.ds(pair * ROWS, ROWS)
        total = parts[0, piece, :]
        for place in range(1, ZH * Y):
            total = total + parts[place, piece, :]
        out[0, :, pair * LANES : (pair + 1) * LANES] = total / denominator[piece, :]


def call(kernel, shapes, specs, scratch=()):
    return pl.pallas_call(
        kernel,
        out_shape=[jax.ShapeDtypeStruct(shape, jnp.float32) for shape in shapes],
        in_specs=specs,
        out_specs=[VMEM] * len(shapes),
        scratch_shapes=[pltpu.VMEM(shape, jnp.float32) for shape in scratch],
        compiler_params=PARAMS,
    )


def per_device(amplitudes, cycle_block, ladder_block, occupied, virtual, tiles):
    swap = [(0, 1), (1, 0)]
    other = lax.ppermute(cycle_block, "core", swap)
    (copies,) = call(pack_kernel, [(ZL, BLOCK, LANES)], [VMEM])(amplitudes)
    column = lax.all_to_all(copies, "zl", 0, 0, tiled=True)
    copies = jnp.broadcast_to(column.reshape(1, ZL * BLOCK, LANES), (X, ZL * BLOCK, LANES))
    gathered = lax.all_to_all(copies, "x", 0, 0, tiled=True)
    gathered = gathered.reshape(CHIPS * BLOCK, LANES)
    halves = jax.ShapeDtypeStruct((cycle_block.shape[0], 2 * cycle_block.shape[1]), jnp.bfloat16)
    high, low = pl.pallas_call(
        prepare_kernel,
        out_shape=[halves] * 2,
        in_specs=[VMEM] * 2,
        out_specs=[VMEM] * 2,
        compiler_params=PARAMS,
    )(cycle_block, other)
    cycle = pl.pallas_call(
        cycle_kernel,
        out_shape=jax.ShapeDtypeStruct((CHIPS * BLOCK, LANES), jnp.float32),
        in_specs=[VMEM] * 3,
        out_specs=pl.BlockSpec(memory_space=pl.ANY),
        scratch_shapes=[
            pltpu.VMEM((CHIPS * BLOCK, LANES), jnp.float32),
            pltpu.SemaphoreType.DMA((2,)),
        ],
        compiler_params=PARAMS,
    )(gathered, high, low)
    cycle, gathered = lax.optimization_barrier((cycle, gathered))
    cycle = lax.all_to_all(cycle.reshape(CHIPS, BLOCK, LANES), ("x", "zl"), 0, 0, tiled=True)

    (window,) = call(
        window_kernel,
        [(2, Y * 2 * ROWS, LANES)],
        [SMEM, VMEM],
        [(TILE // 2 * ROWS, LANES), (LANES, LANES), (LANES, LANES)],
    )(tiles, gathered)
    window = window.reshape(2, Y, 2 * ROWS, LANES)
    other_window = lax.ppermute(window, "core", swap)
    near, far = call(
        add_kernel, [(Y, 2 * ROWS, LANES), (Y, ROWS, LANES)], [VMEM] * 2
    )(window, other_window)
    mine = lax.ppermute(far, "zh", swap)
    theirs = lax.ppermute(mine, "core", swap)
    (window,) = call(join_kernel, [(Y, 4 * ROWS, LANES)], [VMEM] * 3)(near, mine, theirs)
    (denominator,) = call(denominator_kernel, [(BLOCK, LANES)], [SMEM] * 3)(
        tiles, occupied, virtual
    )
    window, denominator, cycle = lax.optimization_barrier((window, denominator, cycle))
    window = lax.all_to_all(window, ("yl", "yh"), 0, 0, tiled=True)

    integrals = ladder_block.reshape(-1, ladder_block.shape[2])
    (parts,) = call(ladder_kernel, [(CHIPS, BLOCK, LANES)], [VMEM] * 3)(window, integrals, cycle)
    parts = lax.all_to_all(parts, ("zh", "yl", "yh"), 0, 0, tiled=True)
    (result,) = call(last_kernel, [amplitudes.shape], [VMEM] * 2)(denominator, parts)
    return result


def solution(mesh):
    parts = Mesh(mesh.devices.reshape(ZL, X, CORE, ZH, YH, YL), EVERY)
    amp, intg = ("zl", "x", "core"), ("zh", "yh", "yl")
    return jax.shard_map(
        per_device,
        mesh=parts,
        in_specs=(P(None, intg, amp), P(intg, amp), P(intg, None, amp), P(), P(), P()),
        out_specs=P(None, intg, amp),
        check_vma=False,
    )
```

```python
import functools

import jax
import jax.numpy as jnp
from jax import lax
from jax.experimental import pallas as pl
from jax.experimental.pallas import tpu as pltpu
from jax.sharding import Mesh
from jax.sharding import PartitionSpec as P

ZL, X, CORE, ZH, YH, YL = 4, 4, 2, 2, 4, 2
Y = YH * YL
CHIPS = ZL * X
ROWS = 8
TILE = 64
PAIRS = 13
LANES = 2 * TILE
BLOCK = PAIRS * ROWS
EVERY = ("zl", "x", "core", "zh", "yh", "yl")
VMEM = pl.BlockSpec(memory_space=pltpu.VMEM)
SMEM = pl.BlockSpec(memory_space=pltpu.SMEM)
PARAMS = pltpu.CompilerParams(vmem_limit_bytes=16 * 1024 * 1024)


def split(value):
    high = value.astype(jnp.bfloat16)
    return high, (value - high.astype(jnp.float32)).astype(jnp.bfloat16)


def product(left, right):
    dot = functools.partial(jnp.dot, preferred_element_type=jnp.float32)
    return dot(left[0], right[1]) + dot(left[1], right[0]) + dot(left[0], right[0])


def low_half(shape):
    return lax.broadcasted_iota(jnp.int32, shape, 1) < TILE


def pair_up(first, second):
    low = low_half(first.shape)
    return (
        jnp.where(low, first, pltpu.roll(second, TILE, 1)),
        jnp.where(low, pltpu.roll(first, TILE, 1), second),
    )


def block_of(chip):
    return chip % X * ZL + chip // X


def peer_of(place):
    return place // Y * Y + place % YL * YH + place % Y // YL


def pack_kernel(amplitudes, out):
    for pair in range(PAIRS):
        tile = amplitudes[0, :, pair * LANES : (pair + 1) * LANES]
        for chip in range(ZL):
            out[chip, pair * ROWS : (pair + 1) * ROWS, :] = tile


def window_kernel(tiles, gathered, out, window, columns, turned):
    core, first = lax.axis_index("core"), lax.axis_index("zh") == 0
    for pair in range(TILE // 2):
        place = tiles[1] * (TILE // 2) + pair
        owner = place // PAIRS
        row = (block_of(owner // CORE) * PAIRS + (place - owner * PAIRS)) * ROWS
        tile = gathered[pl.ds(pl.multiple_of(row, ROWS), ROWS), :]
        window[pair * ROWS : (pair + 1) * ROWS, :] = jnp.where(owner % 2 == core, tile, 0.0)
    for half in range(ROWS // 2):
        for inner in range(2):
            both = window[pl.ds(half * 2 + inner, TILE // 2, stride=ROWS), :]
            columns[pl.ds(inner * TILE, TILE // 2, stride=2), :] = both
            columns[pl.ds(inner * TILE + 1, TILE // 2, stride=2), :] = pltpu.roll(both, TILE, 1)
        turned[...] = jnp.transpose(columns[...])
        for part in range(2):
            even = turned[pl.ds(2 * part, CHIPS, stride=4), :]
            odd = turned[pl.ds(2 * part + 1, CHIPS, stride=4), :]
            for inner, value in enumerate(pair_up(even, odd)):
                row = part * ROWS + half * 2 + inner
                rows = pl.ds(row, Y, stride=2 * ROWS)
                out[0, rows, :] = jnp.where(first, value[:Y], value[Y:])
                out[1, rows, :] = jnp.where(first, value[Y:], value[:Y])


def add_kernel(own, other, near, far):
    core = lax.axis_index("core")
    near[...] = own[0] + other[0]
    total = own[1] + other[1]
    far[...] = jnp.where(core == 0, total[:, :ROWS], total[:, ROWS:])


def join_kernel(near, mine, theirs, out):
    core = lax.axis_index("core")
    out[:, : 2 * ROWS, :] = near[...]
    out[:, 2 * ROWS : 3 * ROWS, :] = jnp.where(core == 0, mine[...], theirs[...])
    out[:, 3 * ROWS :, :] = jnp.where(core == 0, theirs[...], mine[...])


def prepare_kernel(own, other, high, low):
    core = lax.axis_index("core")
    for side in range(2):
        columns = slice(side * own.shape[1], (side + 1) * own.shape[1])
        high[:, columns], low[:, columns] = split(jnp.where(core == side, own[...], other[...]))


def cycle_kernel(gathered, high, low, out, staged, done):
    span = CHIPS // 2 * BLOCK
    rows = CHIPS // 2 * PAIRS
    copies = []
    for half in range(2):
        chunks = ([], [])
        for k in range(0, ROWS, 2):
            first = gathered[pl.ds(half * span + k, rows, stride=ROWS), :]
            second = gathered[pl.ds(half * span + k + 1, rows, stride=ROWS), :]
            for chunk, value in zip(chunks, pair_up(first, second)):
                chunk.append(value)
        left = split(jnp.concatenate([jnp.concatenate(chunk, 1) for chunk in chunks], 0))
        for pair in range(0, ROWS // 2, 2):
            columns = slice(pair * LANES, (pair + 2) * LANES)
            result = product(left, (high[:, columns], low[:, columns]))
            for quarter in range(2):
                both = result[:, quarter * LANES : (quarter + 1) * LANES]
                for inner, value in enumerate(pair_up(both[:rows], both[rows:])):
                    j = (pair + quarter) * 2 + inner
                    staged[pl.ds(half * span + j, rows, stride=ROWS), :] = value
        piece = pl.ds(half * span, span)
        copies.append(pltpu.make_async_copy(staged.at[piece], out.at[piece], done.at[half]))
        copies[-1].start()
    for copy in copies:
        copy.wait()


def ladder_kernel(window, integrals, cycle, out):
    first = lax.axis_index("zh") == 0
    lefts = []
    for part in range(2):
        near, far = [
            window[:, start : start + ROWS, :].reshape(Y * ROWS, LANES)
            for start in (part * ROWS, (2 + part) * ROWS)
        ]
        halves = [jnp.where(first, near, far), jnp.where(first, far, near)]
        lefts.append(jnp.concatenate(halves, 0))
    left = split(jnp.concatenate(lefts, 1))
    width = PAIRS * LANES
    for start in range(0, width, 2 * LANES):
        stop = min(start + 2 * LANES, width)
        result = product(left, split(integrals[:, start:stop]))
        for column in range(start, stop, LANES):
            value = result[:, column - start : column - start + LANES]
            rows = pl.ds(column // LANES * ROWS, ROWS)
            for chip in range(CHIPS):
                part = value[chip * ROWS : (chip + 1) * ROWS]
                out[peer_of(chip), rows, :] = part + cycle[block_of(chip), rows, :]


def denominator_kernel(tiles, occupied, virtual, out):
    column = lax.axis_index("zl") * (X * CORE) + lax.axis_index("x") * CORE + lax.axis_index("core")
    row = lax.axis_index("zh") * Y + lax.axis_index("yh") * YL + lax.axis_index("yl")
    shape = (ROWS, LANES)
    lane = lax.broadcasted_iota(jnp.int32, shape, 1)
    line = lax.broadcasted_iota(jnp.int32, shape, 0)
    spectator = jnp.zeros(shape, jnp.float32)
    for b in range(TILE):
        spectator = jnp.where(lane % TILE == b, virtual[tiles[0] * TILE + b], spectator)
    rows = jnp.zeros(shape, jnp.float32)
    for j in range(ROWS):
        rows = jnp.where(line == j, occupied[row * ROWS + j], rows)
    for pair in range(PAIRS):
        a = column * (2 * PAIRS) + 2 * pair
        energy = jnp.where(lane < TILE, virtual[a], virtual[a + 1]) + spectator
        out[pair * ROWS : (pair + 1) * ROWS, :] = energy - occupied[0] - rows


def last_kernel(denominator, parts, out):
    for pair in range(PAIRS):
        piece = pl.ds(pair * ROWS, ROWS)
        total = parts[0, piece, :]
        for place in range(1, ZH * Y):
            total = total + parts[place, piece, :]
        out[0, :, pair * LANES : (pair + 1) * LANES] = total / denominator[piece, :]


def call(kernel, shapes, specs, scratch=()):
    return pl.pallas_call(
        kernel,
        out_shape=[jax.ShapeDtypeStruct(shape, jnp.float32) for shape in shapes],
        in_specs=specs,
        out_specs=[VMEM] * len(shapes),
        scratch_shapes=[pltpu.VMEM(shape, jnp.float32) for shape in scratch],
        compiler_params=PARAMS,
    )


def per_device(amplitudes, cycle_block, ladder_block, occupied, virtual, tiles):
    swap = [(0, 1), (1, 0)]
    other = lax.ppermute(cycle_block, "core", swap)
    (copies,) = call(pack_kernel, [(ZL, BLOCK, LANES)], [VMEM])(amplitudes)
    column = lax.all_to_all(copies, "zl", 0, 0, tiled=True)
    copies = jnp.broadcast_to(column.reshape(1, ZL * BLOCK, LANES), (X, ZL * BLOCK, LANES))
    gathered = lax.all_to_all(copies, "x", 0, 0, tiled=True)
    gathered = gathered.reshape(CHIPS * BLOCK, LANES)
    halves = jax.ShapeDtypeStruct((cycle_block.shape[0], 2 * cycle_block.shape[1]), jnp.bfloat16)
    high, low = pl.pallas_call(
        prepare_kernel,
        out_shape=[halves] * 2,
        in_specs=[VMEM] * 2,
        out_specs=[VMEM] * 2,
        compiler_params=PARAMS,
    )(cycle_block, other)
    cycle = pl.pallas_call(
        cycle_kernel,
        out_shape=jax.ShapeDtypeStruct((CHIPS * BLOCK, LANES), jnp.float32),
        in_specs=[VMEM] * 3,
        out_specs=pl.BlockSpec(memory_space=pl.ANY),
        scratch_shapes=[
            pltpu.VMEM((CHIPS * BLOCK, LANES), jnp.float32),
            pltpu.SemaphoreType.DMA((2,)),
        ],
        compiler_params=PARAMS,
    )(gathered, high, low)
    cycle, gathered = lax.optimization_barrier((cycle, gathered))
    cycle = lax.all_to_all(cycle.reshape(CHIPS, BLOCK, LANES), ("x", "zl"), 0, 0, tiled=True)

    (window,) = call(
        window_kernel,
        [(2, Y * 2 * ROWS, LANES)],
        [SMEM, VMEM],
        [(TILE // 2 * ROWS, LANES), (LANES, LANES), (LANES, LANES)],
    )(tiles, gathered)
    window = window.reshape(2, Y, 2 * ROWS, LANES)
    other_window = lax.ppermute(window, "core", swap)
    near, far = call(
        add_kernel, [(Y, 2 * ROWS, LANES), (Y, ROWS, LANES)], [VMEM] * 2
    )(window, other_window)
    mine = lax.ppermute(far, "zh", swap)
    theirs = lax.ppermute(mine, "core", swap)
    (window,) = call(join_kernel, [(Y, 4 * ROWS, LANES)], [VMEM] * 3)(near, mine, theirs)
    (denominator,) = call(denominator_kernel, [(BLOCK, LANES)], [SMEM] * 3)(
        tiles, occupied, virtual
    )
    window, denominator, cycle = lax.optimization_barrier((window, denominator, cycle))
    window = lax.all_to_all(window, ("yh", "yl"), 0, 0, tiled=True)

    integrals = ladder_block.reshape(-1, ladder_block.shape[2])
    (parts,) = call(ladder_kernel, [(CHIPS, BLOCK, LANES)], [VMEM] * 3)(window, integrals, cycle)
    parts = lax.all_to_all(parts, ("zh", "yl", "yh"), 0, 0, tiled=True)
    (result,) = call(last_kernel, [amplitudes.shape], [VMEM] * 2)(denominator, parts)
    return result


def solution(mesh):
    parts = Mesh(mesh.devices.reshape(ZL, X, CORE, ZH, YH, YL), EVERY)
    amp, intg = ("zl", "x", "core"), ("zh", "yh", "yl")
    return jax.shard_map(
        per_device,
        mesh=parts,
        in_specs=(P(None, intg, amp), P(intg, amp), P(intg, None, amp), P(), P(), P()),
        out_specs=P(None, intg, amp),
        check_vma=False,
    )
```
